32 devices in a mesh: fsdp: 4 (over y, x), ep: 8 (over z, core).
Axes of the slice: x: 2, y: 2, z: 4, core: 2. Of those that a mesh axis runs over, the one named last changes fastest.
Arguments:
- tokens: bfloat16 [4096, 7168], P('ep', 'fsdp'), may hold values from -6 to 6
- cotangent: bfloat16 [4096, 7168], P('ep', 'fsdp'), may hold values from -3 to 3
- gate_weight: bfloat16 [8, 7168, 2048], P('ep', None, 'fsdp'), may hold values from -0.0625 to 0.0625
- up_weight: bfloat16 [8, 7168, 2048], P('ep', None, 'fsdp'), may hold values from -0.0625 to 0.0625
- down_weight: bfloat16 [8, 2048, 7168], P('ep', 'fsdp'), may hold values from -0.125 to 0.125
- chosen: int32 [8, 8, 16], P(None, 'ep'), may hold values from 0 to 511, as said below
- counts: int32 [8, 8], P(None, 'ep'), may hold values from 1 to 16, as said below
- gate_prob: float32 [8, 8, 16], P(None, 'ep'), may hold values from 0.2 to 1
Outputs:
- mixture: bfloat16 [4096, 7168], P('ep', 'fsdp')
- grad_tokens: bfloat16 [4096, 7168], P('ep', 'fsdp')
- grad_gate: bfloat16 [8, 7168, 2048], P('ep', None, 'fsdp')
- grad_up: bfloat16 [8, 7168, 2048], P('ep', None, 'fsdp')
- grad_down: bfloat16 [8, 2048, 7168], P('ep', 'fsdp')
The draws below stay inside these ranges and needn't reach their ends.
Inputs may be any that keep to these rules, and one draw needn't show every extreme that they name: For each expert e and group s the entries chosen[e, s, j] with j < counts[e, s] are distinct; the remaining entries are padding. `counts`: in every draw one expert takes 16 rows from every group.
All inputs are finite; a program needn't handle non-finite values.
Results may differ from the reference program's by a relative error of at most 0.017.
Values may be sent and summed in bfloat16 or wider, within the bound.
No kernel may reach another device: no remote copies, remote signals or barrier semaphores. Data moves between devices by JAX's collectives and lax.ppermute only.
A program may use at most 192 MiB of HBM per device.

```python
import jax
import jax.numpy as jnp
from jax import lax

D = 7168
H = 2048
TOK = 512
SLOT = 16
GROUPS = 8
EXPERTS = 8
TOKENS = 4096
N_FSDP = 4


def first_slots(subkey):
    return jax.random.permutation(subkey, TOK)[:SLOT]


def draw_chosen(key, part):
    subkeys = jax.random.split(jax.random.fold_in(key, 11), EXPERTS * GROUPS)
    picked = jax.vmap(first_slots)(subkeys)
    return picked.reshape(EXPERTS, GROUPS, SLOT).astype(jnp.int32)


def draw_counts(key, part):
    level_key, count_key, busy_key = jax.random.split(jax.random.fold_in(key, 23), 3)
    levels = jax.random.randint(level_key, (EXPERTS, 1), 1, SLOT + 1)
    lowest = jnp.maximum(levels // 2, 1)
    spread = jax.random.randint(count_key, (EXPERTS, GROUPS), 0, 1048576)
    drawn = lowest + spread % (levels - lowest + 1)
    busiest = jax.random.randint(busy_key, (1, 1), 0, EXPERTS)
    expert_ids = jnp.arange(EXPERTS)[:, None]
    return jnp.where(expert_ids == busiest, SLOT, drawn).astype(jnp.int32)


def shard_levels(stream_key, extent, shards, smallest, high):
    loudness, own = 1.0, jax.random.fold_in(stream_key, 6)
    for dim, blocks in shards:
        draws = jnp.exp(jax.random.uniform(jax.random.fold_in(own, dim), (blocks,), jnp.float32, smallest / len(shards), high / len(shards)))
        loudness = loudness * jnp.repeat(draws, extent[dim] // blocks).reshape([-1 if axis == dim else 1 for axis in range(len(extent))])
    return loudness


def bell_draw(stream_key, dims, deviation, limit, cuts=(), kind=jnp.bfloat16):
    factor_of = shard_levels(stream_key, dims, cuts, -0.22, 0.18) if cuts else 1.0
    entries = jax.random.normal(stream_key, dims, jnp.float32) * deviation * factor_of
    return jnp.minimum(jnp.maximum(entries, -limit), limit).astype(kind)


def setup_inputs(seed: int = 0) -> dict:
    streams_of = jax.random.split(jax.random.key(seed), 9)
    tokens = bell_draw(streams_of[0], (TOKENS, D), 1.0, 6.0, ((0, 8), (1, 4)))
    cotangent = bell_draw(streams_of[1], (TOKENS, D), 0.5, 3.0, ((0, 8), (1, 4)))
    gate_weight = bell_draw(streams_of[2], (EXPERTS, D, H), D ** -0.5, 0.0625, ((0, 8), (2, 4)))
    up_weight = bell_draw(streams_of[3], (EXPERTS, D, H), D ** -0.5, 0.0625, ((0, 8), (2, 4)))
    down_weight = bell_draw(streams_of[4], (EXPERTS, H, D), H ** -0.5, 0.125, ((0, 8), (1, 4)))
    chosen = draw_chosen(jax.random.fold_in(streams_of[8], 71), 0)
    counts = draw_counts(jax.random.fold_in(streams_of[8], 71), 0)
    gate_prob = jnp.clip(0.2 + 0.8 * jax.random.uniform(streams_of[7], (EXPERTS, GROUPS, SLOT), jnp.float32) ** shard_levels(streams_of[7], (EXPERTS, GROUPS, SLOT), ((1, 8),), -0.2, 0.2), 0.2, 1.0)
    return dict(tokens=tokens, cotangent=cotangent, gate_weight=gate_weight, up_weight=up_weight, down_weight=down_weight, chosen=chosen, counts=counts, gate_prob=gate_prob)


def split_hidden(matrix):
    return matrix.astype(jnp.float32).reshape(matrix.shape[0], N_FSDP, matrix.shape[1] // N_FSDP)


def rounded_total(partials):
    kept = lax.optimization_barrier(partials.astype(jnp.bfloat16))
    return jnp.sum(kept.astype(jnp.float32), axis=0)


def reference(tokens, cotangent, gate_weight, up_weight, down_weight, chosen, counts, gate_prob):
    offsets = (jnp.arange(GROUPS, dtype=jnp.int32) * TOK)[:, None]
    position = jnp.arange(SLOT, dtype=jnp.int32)[None, :]
    mixture = jnp.zeros((TOKENS, D), jnp.float32)
    grad_tokens = jnp.zeros((TOKENS, D), jnp.float32)
    gate_grads = []
    up_grads = []
    down_grads = []
    contract_rows = (((0,), (0,)), ((), ()))
    contract_last = (((1,), (1,)), ((), ()))
    for expert in range(EXPERTS):
        row_ids = (chosen[expert].astype(jnp.int32) + offsets).reshape(-1).astype(jnp.int32)
        live_mask = (position < counts[expert].astype(jnp.int32)[:, None]).reshape(-1)
        weight = jnp.where(live_mask, gate_prob[expert].reshape(-1), 0.0).astype(jnp.float32)
        gathered = tokens[row_ids]
        picked = jnp.where(live_mask[:, None], gathered, jnp.zeros_like(gathered))
        picked_grads = (weight[:, None] * cotangent[row_ids].astype(jnp.float32)).astype(jnp.bfloat16)
        pre_gate = jnp.dot(picked, gate_weight[expert], preferred_element_type=jnp.float32)
        pre_up = jnp.dot(picked, up_weight[expert], preferred_element_type=jnp.float32)
        sigmoid_gate = jax.nn.sigmoid(pre_gate)
        activated = pre_gate * sigmoid_gate
        hidden = (activated * pre_up).astype(jnp.bfloat16)
        down_blocks = down_weight[expert].astype(jnp.float32).reshape(N_FSDP, H // N_FSDP, D)
        partials = jnp.einsum("rkh,khd->krd", split_hidden(hidden), down_blocks, precision=lax.Precision.HIGHEST)
        output = rounded_total(partials).astype(jnp.bfloat16)
        mixture = mixture.at[row_ids].add(weight[:, None] * output.astype(jnp.float32))
        grad_hidden = lax.dot_general(picked_grads, down_weight[expert], contract_last, preferred_element_type=jnp.float32)
        grad_pre_gate = (grad_hidden * pre_up * sigmoid_gate * (1.0 + pre_gate * (1.0 - sigmoid_gate))).astype(jnp.bfloat16)
        grad_pre_up = (grad_hidden * activated).astype(jnp.bfloat16)
        down_grads.append(lax.dot_general(hidden, picked_grads, contract_rows, preferred_element_type=jnp.float32).astype(jnp.bfloat16))
        gate_grads.append(lax.dot_general(picked, grad_pre_gate, contract_rows, preferred_element_type=jnp.float32).astype(jnp.bfloat16))
        up_grads.append(lax.dot_general(picked, grad_pre_up, contract_rows, preferred_element_type=jnp.float32).astype(jnp.bfloat16))
        gate_blocks = gate_weight[expert].astype(jnp.float32).reshape(D, N_FSDP, H // N_FSDP)
        up_blocks = up_weight[expert].astype(jnp.float32).reshape(D, N_FSDP, H // N_FSDP)
        partials = jnp.einsum("rkh,dkh->krd", split_hidden(grad_pre_gate), gate_blocks, precision=lax.Precision.HIGHEST)
        partials = partials + jnp.einsum("rkh,dkh->krd", split_hidden(grad_pre_up), up_blocks, precision=lax.Precision.HIGHEST)
        returned = rounded_total(partials).astype(jnp.bfloat16)
        grad_tokens = grad_tokens.at[row_ids].add(jnp.where(live_mask[:, None], returned.astype(jnp.float32), 0.0))
    return (mixture.astype(jnp.bfloat16), grad_tokens.astype(jnp.bfloat16), jnp.stack(gate_grads), jnp.stack(up_grads), jnp.stack(down_grads))
```

```python
import functools

import jax
import jax.numpy as jnp
from jax import lax
from jax.experimental import pallas as pl
from jax.experimental.pallas import tpu as pltpu
from jax.sharding import PartitionSpec as P

ROWS = (((0,), (0,)), ((), ()))
LAST = (((1,), (1,)), ((), ()))
VMEM_BYTES = 40 * 1024 * 1024


def pick_rows(tokens, cotangent, row_index, live_mask, weight):
    flat_rows = row_index.reshape(-1)
    keep_rows = live_mask.reshape(-1)[:, None]
    taken_tokens = jnp.take(tokens, flat_rows, axis=0)
    picked_tokens = jnp.where(keep_rows, taken_tokens, jnp.zeros_like(taken_tokens))
    taken_grads = jnp.take(cotangent, flat_rows, axis=0).astype(jnp.float32)
    picked_grads = (weight.reshape(-1)[:, None] * taken_grads).astype(jnp.bfloat16)
    shaped = row_index.shape + (tokens.shape[1],)
    return (picked_tokens.reshape(shaped), picked_grads.reshape(shaped))


def to_slots(summed, experts, slot_count):
    return summed.astype(jnp.bfloat16).reshape(experts, slot_count, summed.shape[1])


def send_back(term, experts, slot_count):
    summed = lax.psum_scatter(
        term.astype(jnp.bfloat16), "fsdp", scatter_dimension=1, tiled=True
    ).astype(jnp.float32)
    return lax.all_to_all(
        to_slots(summed, experts, slot_count), "ep", split_axis=0, concat_axis=0, tiled=True
    )


def by_collectives(tokens, cotangent, gate_weight, up_weight, down_weight, chosen, counts, gate_prob):
    experts = chosen.shape[0]
    slot_count = chosen.shape[2]
    features = tokens.shape[1]
    row_index = chosen[:, 0, :]
    position = lax.broadcasted_iota(jnp.int32, (experts, slot_count), 1)
    live_mask = position < counts
    weight = jnp.where(live_mask, gate_prob[:, 0, :], 0.0)
    picked_tokens, picked_grads = pick_rows(tokens, cotangent, row_index, live_mask, weight)
    sliced_tokens, sliced_grads = (
        lax.all_to_all(picked_tokens, "ep", split_axis=0, concat_axis=0, tiled=True),
        lax.all_to_all(picked_grads, "ep", split_axis=0, concat_axis=0, tiled=True),
    )
    rows_tokens, rows_grads = (
        lax.all_gather(sliced_tokens, "fsdp", axis=2, tiled=True),
        lax.all_gather(sliced_grads, "fsdp", axis=2, tiled=True),
    )
    full_width = rows_tokens.shape[2]
    total_rows = rows_tokens.shape[0] * slot_count
    rows_tokens = rows_tokens.reshape(total_rows, full_width)
    rows_grads = rows_grads.reshape(total_rows, full_width)
    gate_local = gate_weight[0]
    up_local = up_weight[0]
    down_local = down_weight[0]
    pre_gate = jnp.dot(rows_tokens, gate_local, preferred_element_type=jnp.float32)
    pre_up = jnp.dot(rows_tokens, up_local, preferred_element_type=jnp.float32)
    sigmoid_gate = jax.nn.sigmoid(pre_gate)
    activated = pre_gate * sigmoid_gate
    hidden = (activated * pre_up).astype(jnp.bfloat16)
    output_term = jnp.dot(hidden, down_local, preferred_element_type=jnp.float32)
    output_back = send_back(output_term, experts, slot_count)
    contract_rows = (((0,), (0,)), ((), ()))
    contract_last = (((1,), (1,)), ((), ()))
    grad_hidden = lax.dot_general(
        rows_grads, down_local, contract_last, preferred_element_type=jnp.float32
    )
    grad_pre_gate = (
        grad_hidden * pre_up * sigmoid_gate * (1.0 + pre_gate * (1.0 - sigmoid_gate))
    ).astype(jnp.bfloat16)
    grad_pre_up = (grad_hidden * activated).astype(jnp.bfloat16)
    grad_down = lax.dot_general(
        hidden, rows_grads, contract_rows, preferred_element_type=jnp.float32
    ).astype(jnp.bfloat16)
    grad_gate = lax.dot_general(
        rows_tokens, grad_pre_gate, contract_rows, preferred_element_type=jnp.float32
    ).astype(jnp.bfloat16)
    grad_up = lax.dot_general(
        rows_tokens, grad_pre_up, contract_rows, preferred_element_type=jnp.float32
    ).astype(jnp.bfloat16)
    grad_term = lax.dot_general(
        grad_pre_gate, gate_local, contract_last, preferred_element_type=jnp.float32
    )
    grad_term = grad_term + lax.dot_general(
        grad_pre_up, up_local, contract_last, preferred_element_type=jnp.float32
    )
    grad_back = send_back(grad_term, experts, slot_count)
    flat_rows = row_index.reshape(-1)
    output_rows = output_back.reshape(-1, features).astype(jnp.float32)
    mixture = (
        jnp.zeros((tokens.shape[0], features), jnp.float32)
        .at[flat_rows]
        .add(weight.reshape(-1)[:, None] * output_rows)
    )
    grad_rows = jnp.where(
        live_mask.reshape(-1)[:, None], grad_back.reshape(-1, features).astype(jnp.float32), 0.0
    )
    grad_tokens = jnp.zeros((tokens.shape[0], features), jnp.float32).at[flat_rows].add(grad_rows)
    return (
        mixture.astype(jnp.bfloat16),
        grad_tokens.astype(jnp.bfloat16),
        grad_gate[None],
        grad_up[None],
        grad_down[None],
    )


def call_kernel(body, name, grid, specs, outs, out_specs, scratch, cost, operands, prefetch=1):
    return pl.pallas_call(
        body,
        name=name,
        out_shape=outs,
        grid_spec=pltpu.PrefetchScalarGridSpec(
            num_scalar_prefetch=prefetch,
            grid=grid,
            in_specs=specs,
            out_specs=out_specs,
            scratch_shapes=scratch,
        ),
        compiler_params=pltpu.CompilerParams(vmem_limit_bytes=VMEM_BYTES),
        cost_estimate=pl.CostEstimate(flops=cost[0], bytes_accessed=cost[1], transcendentals=0),
    )(*operands)


def whole(array):
    zeros = (0,) * array.ndim
    return pl.BlockSpec(array.shape, lambda *_: zeros)


def exchange(array, distance, axis):
    size = lax.axis_size(axis)
    return lax.ppermute(array, axis, [(i, i ^ distance) for i in range(size)])


def slot_columns(me, chosen_ref, counts_ref, prob_ref):
    experts, _, slots = chosen_ref.shape
    diagonal = lax.broadcasted_iota(jnp.int32, (slots, slots), 0) == lax.broadcasted_iota(
        jnp.int32, (slots, slots), 1
    )
    position = lax.broadcasted_iota(jnp.int32, (slots, 1), 0)
    rows, weights = [], []
    for step in range(experts):
        expert = me ^ step
        live = position < counts_ref[expert, 0]
        row = jnp.broadcast_to(chosen_ref[expert].astype(jnp.float32), (slots, slots))
        row = jnp.sum(jnp.where(diagonal, row, 0.0), axis=1, keepdims=True)
        prob = jnp.broadcast_to(prob_ref[expert], (slots, slots))
        prob = jnp.sum(jnp.where(diagonal, prob, 0.0), axis=1, keepdims=True)
        rows.append(jnp.where(live, row, -1.0))
        weights.append(jnp.where(live, prob, 0.0))
    return jnp.concatenate(rows, axis=0), jnp.concatenate(weights, axis=0)


def token_mask(rows, tokens):
    place = lax.broadcasted_iota(jnp.int32, (rows.shape[0], tokens), 1).astype(jnp.float32)
    return place == rows


def pick_body(me_ref, counts_ref, chosen_ref, prob_ref, tokens_ref, cotangent_ref, *outs):
    experts, _, slots = chosen_ref.shape
    rows, weights = slot_columns(me_ref[0], chosen_ref, counts_ref, prob_ref)
    select = token_mask(rows, tokens_ref.shape[0]).astype(jnp.bfloat16)
    picked = jnp.dot(select, tokens_ref[...], preferred_element_type=jnp.float32)
    grads = weights * jnp.dot(select, cotangent_ref[...], preferred_element_type=jnp.float32)
    for value, (even_ref, odd_ref) in zip((picked, grads), (outs[:2], outs[2:])):
        value = value.astype(jnp.bfloat16)
        for step in range(experts):
            target = (even_ref, odd_ref)[step % 2]
            target[pl.ds(step // 2 * slots, slots), :] = value[step * slots : (step + 1) * slots]


def pick_slots(ep_index, chosen, counts, gate_prob, tokens, cotangent):
    experts, _, slots = chosen.shape
    length, width = tokens.shape
    block = width // 2 if width % 256 == 0 else width
    half = experts // 2 * slots
    small = [pl.BlockSpec(memory_space=pltpu.SMEM), whole(chosen), whole(gate_prob)]
    long_spec = pl.BlockSpec((length, block), lambda i, *_: (0, i))
    out = jax.ShapeDtypeStruct((half, width), jnp.bfloat16)
    return call_kernel(
        pick_body,
        "pick_slots",
        (width // block,),
        small + [long_spec] * 2,
        [out] * 4,
        [pl.BlockSpec((half, block), lambda i, *_: (0, i))] * 4,
        [],
        (8 * half * length * width, 6 * length * width),
        (ep_index, counts, chosen, gate_prob, tokens, cotangent),
    )


def spread_body(weighted, layout, me_ref, counts_ref, chosen_ref, prob_ref, *refs):
    pieces, out_ref = refs[:-1], refs[-1]
    slots = chosen_ref.shape[2]
    rows, weights = slot_columns(me_ref[0], chosen_ref, counts_ref, prob_ref)
    blocks = [pieces[p][pl.ds(q * slots, slots), :] for p, q in layout]
    values = jnp.concatenate(blocks, axis=0)
    mask = token_mask(rows, out_ref.shape[0])
    if weighted:
        high = weights.astype(jnp.bfloat16).astype(jnp.float32)
        parts = [jnp.where(mask, high, 0.0), jnp.where(mask, weights - high, 0.0)]
        spread = jnp.concatenate([part.astype(jnp.bfloat16) for part in parts], axis=0)
        values = jnp.concatenate([values, values], axis=0)
    else:
        spread = mask.astype(jnp.bfloat16)
    total = lax.dot_general(spread, values, ROWS, preferred_element_type=jnp.float32)
    out_ref[...] = total.astype(jnp.bfloat16)


def spread_rows(ep_index, chosen, counts, gate_prob, pieces, layout, weighted, length):
    width = pieces[0].shape[1]
    block = width // 2 if width % 256 == 0 else width
    small = [pl.BlockSpec(memory_space=pltpu.SMEM), whole(chosen), whole(gate_prob)]
    piece_specs = [pl.BlockSpec((piece.shape[0], block), lambda i, *_: (0, i)) for piece in pieces]
    return call_kernel(
        functools.partial(spread_body, weighted, layout),
        "spread_rows",
        (width // block,),
        small + piece_specs,
        jax.ShapeDtypeStruct((length, width), jnp.bfloat16),
        pl.BlockSpec((length, block), lambda i, *_: (0, i)),
        [],
        (4 * 128 * length * width, 3 * length * width),
        (ep_index, counts, chosen, gate_prob, *pieces),
    )


def stacked(refs, start, size):
    blocks = [ref[:, start : start + size] for ref in refs]
    return blocks[0] if len(blocks) == 1 else jnp.concatenate(blocks, axis=0)


def per_step(step, count, function):
    for index in range(count):

        @pl.when(step == index)
        def _(index=index):
            function(index)


def pre_body(counts, splits, me_ref, *refs):
    total = sum(counts)
    pieces, (gate_ref, up_ref) = refs[:total], refs[total : total + 2]
    hidden_ref, slope_ref, silu_ref, gate_sum, up_sum = refs[total + 2 :]
    step = pl.program_id(0)
    size = gate_ref.shape[0]

    def add(index):
        slice_index, part = divmod(index, splits)
        first = sum(counts[:slice_index])
        rows = stacked(pieces[first : first + counts[slice_index]], part * size, size)
        gate = jnp.dot(rows, gate_ref[...], preferred_element_type=jnp.float32)
        up = jnp.dot(rows, up_ref[...], preferred_element_type=jnp.float32)
        if index == 0:
            gate_sum[...] = gate
            up_sum[...] = up
        else:
            gate_sum[...] += gate
            up_sum[...] += up

    per_step(step, splits * len(counts), add)

    @pl.when(step == pl.num_programs(0) - 1)
    def _():
        gate = gate_sum[...]
        up = up_sum[...]
        sigmoid = jax.nn.sigmoid(gate)
        silu = gate * sigmoid
        hidden_ref[...] = (silu * up).astype(jnp.bfloat16)
        slope_ref[...] = up * sigmoid * (1.0 + gate * (1.0 - sigmoid))
        silu_ref[...] = silu


def pre_activations(fsdp_index, slices, gate, up, splits=2):
    counts = [len(pieces) for pieces in slices]
    flat = [piece for pieces in slices for piece in pieces]
    rows = sum(piece.shape[0] for piece in slices[0])
    width = slices[0][0].shape[1]
    hidden = gate.shape[1]
    size = width // splits
    weight_spec = pl.BlockSpec(
        (size, hidden), lambda i, me: ((me[0] ^ (i // splits)) * splits + i % splits, 0)
    )
    outs = [jax.ShapeDtypeStruct((rows, hidden), t) for t in (jnp.bfloat16, jnp.float32, jnp.float32)]
    return call_kernel(
        functools.partial(pre_body, counts, splits),
        "pre_activations",
        (splits * len(slices),),
        [whole(piece) for piece in flat] + [weight_spec] * 2,
        outs,
        [whole(out) for out in outs],
        [pltpu.VMEM((rows, hidden), jnp.float32)] * 2,
        (4 * rows * hidden * gate.shape[0], 4 * hidden * gate.shape[0]),
        (fsdp_index, *flat, gate, up),
    )


def hidden_grad_body(counts, me_ref, *refs):
    total = sum(counts)
    pieces, (down_ref, slope_ref, silu_ref) = refs[:total], refs[total : total + 3]
    gate_ref, up_ref, grad_sum = refs[total + 3 :]
    step = pl.program_id(0)

    def add(index):
        first = sum(counts[:index])
        rows = stacked(pieces[first : first + counts[index]], 0, down_ref.shape[1])
        grad = lax.dot_general(rows, down_ref[...], LAST, preferred_element_type=jnp.float32)
        if index == 0:
            grad_sum[...] = grad
        else:
            grad_sum[...] += grad

    per_step(step, len(counts), add)

    @pl.when(step == pl.num_programs(0) - 1)
    def _():
        grad = grad_sum[...]
        gate_ref[...] = (grad * slope_ref[...]).astype(jnp.bfloat16)
        up_ref[...] = (grad * silu_ref[...]).astype(jnp.bfloat16)


def hidden_grads(fsdp_index, slices, down, slope, silu):
    counts = [len(pieces) for pieces in slices]
    flat = [piece for pieces in slices for piece in pieces]
    rows, hidden = slope.shape
    width = slices[0][0].shape[1]
    out = jax.ShapeDtypeStruct((rows, hidden), jnp.bfloat16)
    return call_kernel(
        functools.partial(hidden_grad_body, counts),
        "hidden_grads",
        (len(slices),),
        [whole(piece) for piece in flat]
        + [pl.BlockSpec((hidden, width), lambda i, me: (0, me[0] ^ i)), whole(slope), whole(silu)],
        [out] * 2,
        [whole(out)] * 2,
        [pltpu.VMEM((rows, hidden), jnp.float32)],
        (2 * rows * down.size, 2 * down.size),
        (fsdp_index, *flat, down, slope, silu),
    )


def store_pieces(index, order, pieces, refs, value):
    start = 0
    for piece, size in enumerate(pieces):
        refs[order[index] * len(pieces) + piece][...] = value[start : start + size]
        start += size


def output_body(order, pieces, me_ref, hidden_ref, down_ref, *refs):
    value = jnp.dot(hidden_ref[...], down_ref[...], preferred_element_type=jnp.float32)
    value = value.astype(jnp.bfloat16)
    per_step(
        pl.program_id(0), len(order), lambda index: store_pieces(index, order, pieces, refs, value)
    )


def output_terms(fsdp_index, hidden, down, order, pieces):
    rows, units = hidden.shape
    width = down.shape[1] // len(order)
    outs = [jax.ShapeDtypeStruct((size, width), jnp.bfloat16) for _ in order for size in pieces]
    flip = order[0]
    assert all(order[i] == i ^ flip for i in range(len(order)))
    flat = call_kernel(
        functools.partial(output_body, order, pieces),
        "output_terms",
        (len(order),),
        [whole(hidden), pl.BlockSpec((units, width), lambda i, me: (0, me[0] ^ flip ^ i))],
        outs,
        [whole(out) for out in outs],
        [],
        (2 * rows * down.size, 2 * down.size + 2 * rows * down.shape[1]),
        (fsdp_index, hidden, down),
    )
    return [flat[i * len(pieces) : (i + 1) * len(pieces)] for i in range(len(order))]


def grad_term_body(order, pieces, me_ref, gate_grad_ref, up_grad_ref, gate_ref, up_ref, *refs):
    value = lax.dot_general(
        gate_grad_ref[...], gate_ref[...], LAST, preferred_element_type=jnp.float32
    )
    value = value + lax.dot_general(
        up_grad_ref[...], up_ref[...], LAST, preferred_element_type=jnp.float32
    )
    value = value.astype(jnp.bfloat16)
    per_step(
        pl.program_id(0), len(order), lambda index: store_pieces(index, order, pieces, refs, value)
    )


def grad_terms(fsdp_index, gate_grad, up_grad, gate, up, order, pieces):
    rows, units = gate_grad.shape
    width = gate.shape[0] // len(order)
    outs = [jax.ShapeDtypeStruct((size, width), jnp.bfloat16) for _ in order for size in pieces]
    flip = order[0]
    assert all(order[i] == i ^ flip for i in range(len(order)))
    weight_spec = pl.BlockSpec((width, units), lambda i, me: (me[0] ^ flip ^ i, 0))
    flat = call_kernel(
        functools.partial(grad_term_body, order, pieces),
        "grad_terms",
        (len(order),),
        [whole(gate_grad), whole(up_grad), weight_spec, weight_spec],
        outs,
        [whole(out) for out in outs],
        [],
        (4 * rows * gate.size, 4 * gate.size + 2 * rows * gate.shape[0]),
        (fsdp_index, gate_grad, up_grad, gate, up),
    )
    return [flat[i * len(pieces) : (i + 1) * len(pieces)] for i in range(len(order))]


def down_grad_body(counts, me_ref, hidden_ref, *refs):
    pieces, out_ref = refs[:-1], refs[-1]

    def multiply(index):
        first = sum(counts[:index])
        rows = stacked(pieces[first : first + counts[index]], 0, out_ref.shape[1])
        out_ref[...] = lax.dot_general(
            hidden_ref[...], rows, ROWS, preferred_element_type=jnp.float32
        ).astype(jnp.bfloat16)

    per_step(pl.program_id(0), len(counts), multiply)


def down_grads(fsdp_index, hidden, slices):
    counts = [len(pieces) for pieces in slices]
    flat = [piece for pieces in slices for piece in pieces]
    rows, units = hidden.shape
    width = slices[0][0].shape[1]
    full = width * len(slices)
    return call_kernel(
        functools.partial(down_grad_body, counts),
        "down_grads",
        (len(slices),),
        [whole(hidden)] + [whole(piece) for piece in flat],
        jax.ShapeDtypeStruct((units, full), jnp.bfloat16),
        pl.BlockSpec((units, width), lambda i, me: (0, me[0] ^ i)),
        [],
        (2 * rows * units * full, 2 * (units + rows) * full),
        (fsdp_index, hidden, *flat),
    )


def weight_grad_body(counts, me_ref, gate_grad_ref, up_grad_ref, *refs):
    pieces, (gate_ref, up_ref) = refs[:-2], refs[-2:]

    def multiply(index):
        first = sum(counts[:index])
        rows = stacked(pieces[first : first + counts[index]], 0, gate_ref.shape[0])
        for grad_ref, out_ref in ((gate_grad_ref, gate_ref), (up_grad_ref, up_ref)):
            out_ref[...] = lax.dot_general(
                rows, grad_ref[...], ROWS, preferred_element_type=jnp.float32
            ).astype(jnp.bfloat16)

    per_step(pl.program_id(0), len(counts), multiply)


def weight_grads(fsdp_index, slices, gate_grad, up_grad):
    counts = [len(pieces) for pieces in slices]
    flat = [piece for pieces in slices for piece in pieces]
    rows, units = gate_grad.shape
    width = slices[0][0].shape[1]
    full = width * len(slices)
    out = jax.ShapeDtypeStruct((full, units), jnp.bfloat16)
    return call_kernel(
        functools.partial(weight_grad_body, counts),
        "weight_grads",
        (len(slices),),
        [whole(gate_grad), whole(up_grad)] + [whole(piece) for piece in flat],
        [out] * 2,
        [pl.BlockSpec((width, units), lambda i, me: (me[0] ^ i, 0))] * 2,
        [],
        (4 * rows * units * full, 2 * (2 * units + rows) * full),
        (fsdp_index, gate_grad, up_grad, *flat),
    )


def gather_pair(first, second):
    first_x = exchange(first, 1, "fsdp")
    second_y = exchange(second, 2, "fsdp")
    first_y = exchange(first, 2, "fsdp")
    second_x = exchange(second, 1, "fsdp")
    first_d = exchange(first_x, 2, "fsdp")
    second_d = exchange(second_y, 1, "fsdp")
    return [[first, second], [first_x, second_x], [first_y, second_y], [first_d, second_d]]


def added(*terms):
    return sum(term.astype(jnp.float32) for term in terms).astype(jnp.bfloat16)


def reduce_pair(terms):
    first_d = exchange(terms[3][0], 1, "fsdp")
    second_d = exchange(terms[3][1], 2, "fsdp")
    first_x = exchange(terms[1][0], 1, "fsdp")
    second_y = exchange(terms[2][1], 2, "fsdp")
    first_y = exchange(added(terms[2][0], first_d), 2, "fsdp")
    second_x = exchange(added(terms[1][1], second_d), 1, "fsdp")
    return added(terms[0][0], first_x, first_y), added(terms[0][1], second_y, second_x)


def to_experts(even, odd, slots):
    count = even.shape[0] // slots
    other = exchange(odd, 1, "ep")
    pairs = []
    for step in range(count):
        part = slice(step * slots, (step + 1) * slots)
        pairs.append(jnp.concatenate([even[part], other[part]], axis=0))
    return [pairs[0]] + [exchange(pairs[step], 2 * step, "ep") for step in range(1, count)]


def to_groups(pairs, slots):
    back = [pairs[0]] + [exchange(pair, 2 * step, "ep") for step, pair in enumerate(pairs) if step]
    odd = jnp.concatenate([pair[slots:] for pair in back], axis=0)
    other = exchange(odd, 1, "ep")
    layout = []
    for step in range(len(pairs)):
        layout += [(step, 0), (len(pairs), step)]
    return back + [other], layout


def by_links(tokens, cotangent, gate_weight, up_weight, down_weight, chosen, counts, gate_prob):
    experts, _, slots = chosen.shape
    length = tokens.shape[0]
    ep_index = lax.axis_index("ep").reshape(1)
    fsdp_index = lax.axis_index("fsdp").reshape(1)
    gate, up, down = gate_weight[0], up_weight[0], down_weight[0]
    token_even, token_odd, grad_even, grad_odd = pick_slots(
        ep_index, chosen, counts, gate_prob, tokens, cotangent
    )
    pairs = to_experts(token_even, token_odd, slots)
    near = gather_pair(pairs[0], pairs[1])
    far = gather_pair(pairs[2], pairs[3])
    token_slices = [a + b for a, b in zip(near, far)]
    grad_pairs = to_experts(grad_even, grad_odd, slots)
    grad_slices = gather_pair(
        jnp.concatenate(grad_pairs[:2], axis=0), jnp.concatenate(grad_pairs[2:], axis=0)
    )
    hidden, slope, silu = pre_activations(fsdp_index, token_slices, gate, up)
    half = experts // 2 * slots
    order = (3, 2, 1, 0)
    terms = output_terms(fsdp_index, hidden, down, order, (half, half))
    near_rows, far_rows = reduce_pair(terms)
    two = 2 * slots
    pieces, layout = to_groups(
        [near_rows[:two], near_rows[two:], far_rows[:two], far_rows[two:]], slots
    )
    mixture = spread_rows(ep_index, chosen, counts, gate_prob, pieces, layout, True, length)
    gate_grad, up_grad = hidden_grads(fsdp_index, grad_slices, down, slope, silu)
    terms = grad_terms(fsdp_index, gate_grad, up_grad, gate, up, order, (half, half))
    near_rows, far_rows = reduce_pair(terms)
    pieces, layout = to_groups(
        [near_rows[:two], near_rows[two:], far_rows[:two], far_rows[two:]], slots
    )
    grad_tokens = spread_rows(ep_index, chosen, counts, gate_prob, pieces, layout, False, length)
    grad_down = down_grads(fsdp_index, hidden, grad_slices)
    grad_gate, grad_up = weight_grads(fsdp_index, token_slices, gate_grad, up_grad)
    return mixture, grad_tokens, grad_gate[None], grad_up[None], grad_down[None]


def solution(mesh):
    placed = (
        P("ep", "fsdp"),
        P("ep", "fsdp"),
        P("ep", None, "fsdp"),
        P("ep", None, "fsdp"),
        P("ep", "fsdp", None),
        P(None, "ep", None),
        P(None, "ep"),
        P(None, "ep", None),
    )

    def per_part(*arrays):
        fits = mesh.shape["fsdp"] == 4 and mesh.shape["ep"] == 8 and arrays[0].shape[1] % 128 == 0
        return (by_links if fits else by_collectives)(*arrays)

    return jax.shard_map(
        per_part,
        mesh=mesh,
        in_specs=placed,
        out_specs=(
            P("ep", "fsdp"),
            P("ep", "fsdp"),
            P("ep", None, "fsdp"),
            P("ep", None, "fsdp"),
            P("ep", "fsdp", None),
        ),
        check_vma=False,
    )
```

```python
import functools

import jax
import jax.numpy as jnp
from jax import lax
from jax.experimental import pallas as pl
from jax.experimental.pallas import tpu as pltpu
from jax.sharding import PartitionSpec as P

ROWS = (((0,), (0,)), ((), ()))
LAST = (((1,), (1,)), ((), ()))
IN_VMEM = pl.BlockSpec(memory_space=pltpu.VMEM)
IN_SMEM = pl.BlockSpec(memory_space=pltpu.SMEM)
ANYWHERE = pl.BlockSpec(memory_space=pl.ANY)
MIB = 1024 * 1024


def run_kernel(body, name, operands, specs, outs, out_specs, scratch, mib, later=(), mark=False, cost=1024):
    used = len(operands)
    outs, out_specs = list(outs), list(out_specs)
    results = len(outs)
    if mark:
        outs.append(jax.ShapeDtypeStruct((8, 128), jnp.float32))
        out_specs.append(IN_VMEM)

    def run(*refs):
        refs = [*refs[:used], *refs[used + len(later) :]]
        if mark:
            mark_ref = refs.pop(used + results)
            mark_ref[...] = jnp.zeros_like(mark_ref)
        body(*refs)

    out = pl.pallas_call(
        run,
        name=name,
        in_specs=[*specs, *[ANYWHERE] * len(later)],
        out_shape=outs,
        out_specs=out_specs,
        scratch_shapes=scratch,
        compiler_params=pltpu.CompilerParams(vmem_limit_bytes=mib * MIB),
        cost_estimate=pl.CostEstimate(flops=1024, bytes_accessed=cost, transcendentals=0),
    )(*operands, *later)
    return out if len(out) > 1 else out[0]


def in_hbm(array):
    return pltpu.with_memory_space_constraint(array, pltpu.HBM)


def like(rows, width, kind=jnp.bfloat16):
    return jax.ShapeDtypeStruct((rows, width), kind)


def slot_columns(me, chosen_ref, counts_ref, prob_ref):
    experts, _, slots = chosen_ref.shape
    diagonal = lax.broadcasted_iota(jnp.int32, (slots, slots), 0) == lax.broadcasted_iota(
        jnp.int32, (slots, slots), 1
    )
    position = lax.broadcasted_iota(jnp.int32, (slots, 1), 0)
    rows, weights = [], []
    for step in range(experts):
        expert = me ^ step
        live = position < counts_ref[0, expert]
        row = jnp.broadcast_to(chosen_ref[expert].astype(jnp.float32), (slots, slots))
        row = jnp.sum(jnp.where(diagonal, row, 0.0), axis=1, keepdims=True)
        prob = jnp.broadcast_to(prob_ref[expert], (slots, slots))
        prob = jnp.sum(jnp.where(diagonal, prob, 0.0), axis=1, keepdims=True)
        rows.append(jnp.where(live, row, -1.0))
        weights.append(jnp.where(live, prob, 0.0))
    return jnp.concatenate(rows, axis=0), jnp.concatenate(weights, axis=0)


def pick_body(me_ref, counts_hbm, chosen_hbm, prob_hbm, tokens_hbm, cotangent_hbm, *refs):
    *outs, mask_ref, weights_ref = refs[:-6]
    counts_ref, chosen_ref, prob_ref, tokens_ref, cotangent_ref, sems = refs[-6:]
    experts, _, slots = chosen_ref.shape
    pairs = (
        (counts_hbm, counts_ref),
        (chosen_hbm, chosen_ref),
        (prob_hbm, prob_ref),
        (tokens_hbm, tokens_ref),
        (cotangent_hbm, cotangent_ref),
    )
    copies = [pltpu.make_async_copy(*pair, sems.at[index]) for index, pair in enumerate(pairs)]
    for copy in copies:
        copy.start()
    for copy in copies[:3]:
        copy.wait()
    rows, weights = slot_columns(me_ref[0], chosen_ref, counts_ref, prob_ref)
    length = tokens_ref.shape[0]
    place = lax.broadcasted_iota(jnp.int32, (rows.shape[0], length), 1).astype(jnp.float32)
    mask = (place == rows).astype(jnp.bfloat16)
    mask_ref[...] = mask
    weights_ref[...] = jnp.broadcast_to(weights, weights_ref.shape)
    for which, source_ref in enumerate((tokens_ref, cotangent_ref)):
        copies[3 + which].wait()
        value = jnp.dot(mask, source_ref[...], preferred_element_type=jnp.float32)
        if which:
            value = weights * value
        value = value.astype(jnp.bfloat16)
        step = 0
        for out_ref in outs:
            for start in range(which * slots, out_ref.shape[0], 2 * slots):
                out_ref[pl.ds(start, slots), :] = value[step * slots : (step + 1) * slots]
                step += 1


def pick_slots(me, chosen, counts, gate_prob, tokens, cotangent, split):
    experts, _, slots = chosen.shape
    length, width = tokens.shape
    total = experts * slots
    operands = (counts, chosen, gate_prob, tokens, cotangent)
    return run_kernel(
        pick_body,
        "pick_slots",
        (me, *[in_hbm(array) for array in operands]),
        [IN_SMEM] + [ANYWHERE] * 5,
        [like(2 * slots * part, width) for part in split]
        + [like(total, length), like(total, 128, jnp.float32)],
        [IN_VMEM] * (len(split) + 2),
        [pltpu.SMEM(counts.shape, counts.dtype)]
        + [pltpu.VMEM(array.shape, array.dtype) for array in operands[1:]]
        + [pltpu.SemaphoreType.DMA((5,))],
        16,
    )


def spread_matrix_body(mask_ref, weights_ref, weighted_ref, plain_ref):
    mask = mask_ref[...].astype(jnp.float32)
    weights = weights_ref[...][:, :1]
    high = weights.astype(jnp.bfloat16).astype(jnp.float32)
    count = mask.shape[0]
    plain_ref[...] = mask.T.astype(jnp.bfloat16)
    weighted_ref[:, :count] = (mask * high).T.astype(jnp.bfloat16)
    weighted_ref[:, count:] = (mask * (weights - high)).T.astype(jnp.bfloat16)


def spread_matrices(mask, weights, later=()):
    count, length = mask.shape
    return run_kernel(
        spread_matrix_body,
        "spread_matrices",
        (mask, weights),
        [IN_VMEM] * 2,
        [like(length, 2 * count), like(length, count)],
        [IN_VMEM] * 2,
        [],
        8,
        later,
    )


def spread_body(layout, slots, spread_ref, *refs):
    pieces, (out_hbm, block, sems) = refs[:-3], refs[-3:]
    values = jnp.concatenate([pieces[p][pl.ds(q * slots, slots), :] for p, q in layout], axis=0)
    if spread_ref.shape[1] > values.shape[0]:
        values = jnp.concatenate([values, values], axis=0)
    parts = sems.shape[0]
    size = block.shape[0] // parts
    copies = []
    for part in range(parts):
        rows = pl.ds(part * size, size)
        total = jnp.dot(spread_ref[rows, :], values, preferred_element_type=jnp.float32)
        block[rows, :] = total.astype(jnp.bfloat16)
        copies.append(pltpu.make_async_copy(block.at[rows], out_hbm.at[rows], sems.at[part]))
        copies[-1].start()
    for copy in copies:
        copy.wait()


def spread_rows(spread, pieces, layout, slots, later=(), mark=False, parts=4):
    length, width = spread.shape[0], pieces[0].shape[1]
    return run_kernel(
        functools.partial(spread_body, layout, slots),
        "spread_rows",
        (spread, *pieces),
        [IN_VMEM] * (1 + len(pieces)),
        [like(length, width)],
        [ANYWHERE],
        [pltpu.VMEM((length, width), jnp.bfloat16), pltpu.SemaphoreType.DMA((parts,))],
        16,
        later,
        mark,
    )


def load_body(by_rows, count, me_ref, source_ref, target_ref, sems):
    width = target_ref.shape[1 if by_rows else 2]
    copies = []
    for index in range(count):
        part = pl.ds(pl.multiple_of((me_ref[0] ^ index) * width, width), width)
        source = source_ref.at[part, :] if by_rows else source_ref.at[:, part]
        copies.append(pltpu.make_async_copy(source, target_ref.at[index], sems.at[index]))
        copies[-1].start()
    for copy in copies:
        copy.wait()


def load_weight(me, weight, by_rows, count, later=()):
    first, second = weight.shape
    shape = (count, first // count, second) if by_rows else (count, first, second // count)
    return run_kernel(
        functools.partial(load_body, by_rows, count),
        "load_weight",
        (me, in_hbm(weight)),
        [IN_SMEM, ANYWHERE],
        [jax.ShapeDtypeStruct(shape, weight.dtype)],
        [IN_VMEM],
        [pltpu.SemaphoreType.DMA((count,))],
        4,
        later,
    )


def arrange_body(plan, used, *refs):
    for rows, out_ref in zip(plan, refs[used:]):
        start = 0
        for source, first, size in rows:
            out_ref[pl.ds(start, size), :] = refs[source][pl.ds(first, size), :]
            start += size


def arrange(sources, plan, later=(), cost=1024):
    width = sources[0].shape[1]
    sizes = [sum(size for _, _, size in rows) for rows in plan]
    return run_kernel(
        functools.partial(arrange_body, plan, len(sources)),
        "arrange",
        tuple(sources),
        [IN_VMEM] * len(sources),
        [like(size, width) for size in sizes],
        [IN_VMEM] * len(plan),
        [],
        8,
        later,
        cost=cost,
    )


def add_body(used, *refs):
    total = refs[0][...].astype(jnp.float32)
    for ref in refs[1:used]:
        total += ref[...].astype(jnp.float32)
    start = 0
    for out_ref in refs[used:]:
        out_ref[...] = total[start : start + out_ref.shape[0]].astype(out_ref.dtype)
        start += out_ref.shape[0]


def add_up(terms, parts=1, later=(), cost=1024):
    rows, width = terms[0].shape
    return run_kernel(
        functools.partial(add_body, len(terms)),
        "add_up",
        tuple(terms),
        [IN_VMEM] * len(terms),
        [like(rows // parts, width)] * parts,
        [IN_VMEM] * parts,
        [],
        8,
        later,
        cost=cost,
    )


class Slices:
    def __init__(self, pieces, part, slots):
        self.pieces, self.part, self.slots = pieces, part, slots
        self.flat = [piece for row in pieces for piece in row]
        self.rows = sum(piece.shape[0] for piece in pieces[0]) // 2
        self.width = self.flat[0].shape[1]

    def read(self, refs, index):
        first = sum(len(pieces) for pieces in self.pieces[:index])
        blocks = []
        for ref in refs[first : first + len(self.pieces[index])]:
            for start in range(self.part * self.slots, ref.shape[0], 2 * self.slots):
                blocks.append(ref[pl.ds(start, self.slots), :])
        return jnp.concatenate(blocks, axis=0)


def store_halves(refs, index, term):
    size = term.shape[0] // 2
    refs[2 * index][...] = term[:size].astype(jnp.bfloat16)
    refs[2 * index + 1][...] = term[size:].astype(jnp.bfloat16)


def forward_body(slices, *refs):
    gate_ref, up_ref, down_ref, hidden_ref, slope_ref, silu_ref, *terms = refs[len(slices.flat) :]
    count = gate_ref.shape[0]
    gate = up = None
    for index in range(count):
        rows = slices.read(refs, index)
        more_gate = jnp.dot(rows, gate_ref[index], preferred_element_type=jnp.float32)
        more_up = jnp.dot(rows, up_ref[index], preferred_element_type=jnp.float32)
        gate = more_gate if gate is None else gate + more_gate
        up = more_up if up is None else up + more_up
    sigmoid = jax.nn.sigmoid(gate)
    silu = gate * sigmoid
    hidden = (silu * up).astype(jnp.bfloat16)
    hidden_ref[...] = hidden
    slope_ref[...] = up * sigmoid * (1.0 + gate * (1.0 - sigmoid))
    silu_ref[...] = silu
    for index in reversed(range(count)):
        term = jnp.dot(hidden, down_ref[index], preferred_element_type=jnp.float32)
        store_halves(terms, index, term)


def forward_terms(slices, gate, up, down, later=()):
    count, width, units = gate.shape
    rows = slices.rows
    outs = [like(rows, units), like(rows, units, jnp.float32), like(rows, units, jnp.float32)]
    outs += [like(rows // 2, width)] * (2 * count)
    out = run_kernel(
        functools.partial(forward_body, slices),
        "forward_terms",
        (*slices.flat, gate, up, down),
        [IN_VMEM] * (len(slices.flat) + 3),
        outs,
        [IN_VMEM] * len(outs),
        [],
        8,
        later,
    )
    return out[:3], [out[3 + 2 * i : 5 + 2 * i] for i in range(count)]


def hidden_grad_body(slices, *refs):
    down_ref, slope_ref, silu_ref, gate_grad_ref, up_grad_ref = refs[len(slices.flat) :]
    grad = None
    for index in range(down_ref.shape[0]):
        rows = slices.read(refs, index)
        more = lax.dot_general(rows, down_ref[index], LAST, preferred_element_type=jnp.float32)
        grad = more if grad is None else grad + more
    gate_grad_ref[...] = (grad * slope_ref[...]).astype(jnp.bfloat16)
    up_grad_ref[...] = (grad * silu_ref[...]).astype(jnp.bfloat16)


def hidden_grads(slices, down, slope, silu, later=()):
    return run_kernel(
        functools.partial(hidden_grad_body, slices),
        "hidden_grads",
        (*slices.flat, down, slope, silu),
        [IN_VMEM] * (len(slices.flat) + 3),
        [like(*slope.shape)] * 2,
        [IN_VMEM] * 2,
        [],
        8,
        later,
    )


def grad_term_body(wanted, gate_grad_ref, up_grad_ref, gate_ref, up_ref, *terms):
    for place, index in enumerate(wanted):
        term = lax.dot_general(
            gate_grad_ref[...], gate_ref[index], LAST, preferred_element_type=jnp.float32
        )
        term += lax.dot_general(
            up_grad_ref[...], up_ref[index], LAST, preferred_element_type=jnp.float32
        )
        store_halves(terms, place, term)


def grad_terms(wanted, gate_grad, up_grad, gate, up, later=()):
    _, width, _ = gate.shape
    rows = gate_grad.shape[0]
    terms = run_kernel(
        functools.partial(grad_term_body, wanted),
        "grad_terms",
        (gate_grad, up_grad, gate, up),
        [IN_VMEM] * 4,
        [like(rows // 2, width)] * (2 * len(wanted)),
        [IN_VMEM] * (2 * len(wanted)),
        [],
        8,
        later,
    )
    return [terms[2 * i : 2 * i + 2] for i in range(len(wanted))]


def down_grad_body(slices, me_ref, hidden_ref, *refs):
    out_ref, block, sems = refs[-3:]
    count, _, width = block.shape
    hidden = hidden_ref[...]
    copies = []
    for index in range(count):
        rows = slices.read(refs, index)
        block[index] = lax.dot_general(
            hidden, rows, ROWS, preferred_element_type=jnp.float32
        ).astype(jnp.bfloat16)
        start = pl.multiple_of((me_ref[0] ^ index) * width, width)
        target = out_ref.at[:, pl.ds(start, width)]
        copies.append(pltpu.make_async_copy(block.at[index], target, sems.at[index]))
        copies[-1].start()
    for copy in copies:
        copy.wait()


def down_grads(me, hidden, slices, later=()):
    count = len(slices.pieces)
    units = hidden.shape[1]
    return run_kernel(
        functools.partial(down_grad_body, slices),
        "down_grads",
        (me, hidden, *slices.flat),
        [IN_SMEM] + [IN_VMEM] * (1 + len(slices.flat)),
        [like(units, slices.width * count)],
        [ANYWHERE],
        [
            pltpu.VMEM((count, units, slices.width), jnp.bfloat16),
            pltpu.SemaphoreType.DMA((count,)),
        ],
        16,
        later,
        True,
    )


def weight_grad_body(slices, me_ref, *refs):
    grad_refs, (gate_hbm, up_hbm, block, sems) = refs[:2], refs[-4:]
    _, count, width, _ = block.shape
    copies = []
    for index in range(count):
        rows = slices.read(refs[2:], index)
        start = pl.multiple_of((me_ref[0] ^ index) * width, width)
        for which, out_ref in enumerate((gate_hbm, up_hbm)):
            block[which, index] = lax.dot_general(
                rows, grad_refs[which][...], ROWS, preferred_element_type=jnp.float32
            ).astype(jnp.bfloat16)
            target = out_ref.at[pl.ds(start, width), :]
            sem = sems.at[2 * index + which]
            copies.append(pltpu.make_async_copy(block.at[which, index], target, sem))
            copies[-1].start()
    for copy in copies:
        copy.wait()


def weight_grads(me, slices, gate_grad, up_grad, later=()):
    count = len(slices.pieces)
    units = gate_grad.shape[1]
    return run_kernel(
        functools.partial(weight_grad_body, slices),
        "weight_grads",
        (me, gate_grad, up_grad, *slices.flat),
        [IN_SMEM] + [IN_VMEM] * (2 + len(slices.flat)),
        [like(slices.width * count, units)] * 2,
        [ANYWHERE] * 2,
        [
            pltpu.VMEM((2, count, slices.width, units), jnp.bfloat16),
            pltpu.SemaphoreType.DMA((2 * count,)),
        ],
        20,
        later,
        True,
    )


def pick_rows(tokens, cotangent, row_index, live_mask, weight):
    flat_rows = row_index.reshape(-1)
    keep_rows = live_mask.reshape(-1)[:, None]
    taken_tokens = jnp.take(tokens, flat_rows, axis=0)
    picked_tokens = jnp.where(keep_rows, taken_tokens, jnp.zeros_like(taken_tokens))
    taken_grads = jnp.take(cotangent, flat_rows, axis=0).astype(jnp.float32)
    picked_grads = (weight.reshape(-1)[:, None] * taken_grads).astype(jnp.bfloat16)
    shaped = row_index.shape + (tokens.shape[1],)
    return (picked_tokens.reshape(shaped), picked_grads.reshape(shaped))


def to_slots(summed, experts, slot_count):
    return summed.astype(jnp.bfloat16).reshape(experts, slot_count, summed.shape[1])


def send_back(term, experts, slot_count):
    summed = lax.psum_scatter(
        term.astype(jnp.bfloat16), "fsdp", scatter_dimension=1, tiled=True
    ).astype(jnp.float32)
    return lax.all_to_all(
        to_slots(summed, experts, slot_count), "ep", split_axis=0, concat_axis=0, tiled=True
    )


def by_collectives(tokens, cotangent, gate_weight, up_weight, down_weight, chosen, counts, gate_prob):
    experts = chosen.shape[0]
    slot_count = chosen.shape[2]
    features = tokens.shape[1]
    row_index = chosen[:, 0, :]
    position = lax.broadcasted_iota(jnp.int32, (experts, slot_count), 1)
    live_mask = position < counts
    weight = jnp.where(live_mask, gate_prob[:, 0, :], 0.0)
    picked_tokens, picked_grads = pick_rows(tokens, cotangent, row_index, live_mask, weight)
    sliced_tokens, sliced_grads = (
        lax.all_to_all(picked_tokens, "ep", split_axis=0, concat_axis=0, tiled=True),
        lax.all_to_all(picked_grads, "ep", split_axis=0, concat_axis=0, tiled=True),
    )
    rows_tokens, rows_grads = (
        lax.all_gather(sliced_tokens, "fsdp", axis=2, tiled=True),
        lax.all_gather(sliced_grads, "fsdp", axis=2, tiled=True),
    )
    full_width = rows_tokens.shape[2]
    total_rows = rows_tokens.shape[0] * slot_count
    rows_tokens = rows_tokens.reshape(total_rows, full_width)
    rows_grads = rows_grads.reshape(total_rows, full_width)
    gate_local = gate_weight[0]
    up_local = up_weight[0]
    down_local = down_weight[0]
    pre_gate = jnp.dot(rows_tokens, gate_local, preferred_element_type=jnp.float32)
    pre_up = jnp.dot(rows_tokens, up_local, preferred_element_type=jnp.float32)
    sigmoid_gate = jax.nn.sigmoid(pre_gate)
    activated = pre_gate * sigmoid_gate
    hidden = (activated * pre_up).astype(jnp.bfloat16)
    output_term = jnp.dot(hidden, down_local, preferred_element_type=jnp.float32)
    output_back = send_back(output_term, experts, slot_count)
    contract_rows = (((0,), (0,)), ((), ()))
    contract_last = (((1,), (1,)), ((), ()))
    grad_hidden = lax.dot_general(
        rows_grads, down_local, contract_last, preferred_element_type=jnp.float32
    )
    grad_pre_gate = (
        grad_hidden * pre_up * sigmoid_gate * (1.0 + pre_gate * (1.0 - sigmoid_gate))
    ).astype(jnp.bfloat16)
    grad_pre_up = (grad_hidden * activated).astype(jnp.bfloat16)
    grad_down = lax.dot_general(
        hidden, rows_grads, contract_rows, preferred_element_type=jnp.float32
    ).astype(jnp.bfloat16)
    grad_gate = lax.dot_general(
        rows_tokens, grad_pre_gate, contract_rows, preferred_element_type=jnp.float32
    ).astype(jnp.bfloat16)
    grad_up = lax.dot_general(
        rows_tokens, grad_pre_up, contract_rows, preferred_element_type=jnp.float32
    ).astype(jnp.bfloat16)
    grad_term = lax.dot_general(
        grad_pre_gate, gate_local, contract_last, preferred_element_type=jnp.float32
    )
    grad_term = grad_term + lax.dot_general(
        grad_pre_up, up_local, contract_last, preferred_element_type=jnp.float32
    )
    grad_back = send_back(grad_term, experts, slot_count)
    flat_rows = row_index.reshape(-1)
    output_rows = output_back.reshape(-1, features).astype(jnp.float32)
    mixture = (
        jnp.zeros((tokens.shape[0], features), jnp.float32)
        .at[flat_rows]
        .add(weight.reshape(-1)[:, None] * output_rows)
    )
    grad_rows = jnp.where(
        live_mask.reshape(-1)[:, None], grad_back.reshape(-1, features).astype(jnp.float32), 0.0
    )
    grad_tokens = jnp.zeros((tokens.shape[0], features), jnp.float32).at[flat_rows].add(grad_rows)
    return (
        mixture.astype(jnp.bfloat16),
        grad_tokens.astype(jnp.bfloat16),
        grad_gate[None],
        grad_up[None],
        grad_down[None],
    )


LONG = 64 * MIB


def swap(array, distance, axis):
    size = lax.axis_size(axis)
    return lax.ppermute(array, axis, [(i, i ^ distance) for i in range(size)])


def joined(*arrays):
    return jnp.concatenate(arrays, axis=0)


def by_links(tokens, cotangent, gate_weight, up_weight, down_weight, chosen, counts, gate_prob):
    experts, _, slots = chosen.shape
    count = lax.axis_size("fsdp")
    ep_index = lax.axis_index("ep").reshape(1)
    me = lax.axis_index("fsdp").reshape(1)
    two = 2 * slots
    half = 2 * two
    own, core, even1, odd1, pair2, pair3, mask, weights = pick_slots(
        ep_index,
        chosen,
        counts.reshape(1, experts),
        gate_prob,
        tokens,
        cotangent,
        (1, 1, 1, 1, 2, 2),
    )

    pair2 = swap(pair2, 4, "ep")
    pair3 = swap(pair3, 6, "ep")
    even1 = swap(even1, 2, "ep")
    odd1 = swap(odd1, 3, "ep")
    core = swap(core, 1, "ep")

    gate = load_weight(me, gate_weight[0], True, count, (own,))
    up = load_weight(me, up_weight[0], True, count, (gate,))
    weighted, plain = spread_matrices(mask, weights, (up,))
    near = joined(arrange((own,), [[(0, 0, two)]], (weighted,)), core, even1, odd1)
    near_x = swap(near, 1, "fsdp")
    near_y = swap(near, 2, "fsdp")
    near_d = [swap(near_x[:half], 2, "fsdp"), swap(near_y[half:], 1, "fsdp")]
    odd = swap(joined(pair2[two:], pair3[two:]), 1, "ep")
    far = arrange(
        (pair2, pair3, odd), [[(0, 0, two), (2, 0, two), (1, 0, two), (2, two, two)]], tuple(near_d)
    )
    far_x = swap(far, 1, "fsdp")
    far_y = swap(far, 2, "fsdp")
    down = load_weight(me, down_weight[0], False, count, (far,))
    far_d = [swap(far_x[:half], 2, "fsdp"), swap(far_y[half:], 1, "fsdp")]
    pieces = [[near, far], [near_x, far_x], [near_y, far_y], near_d + far_d]
    tokens, grads = Slices(pieces, 0, slots), Slices(pieces, 1, slots)

    (hidden, slope, silu), terms = forward_terms(tokens, gate, up, down)
    far_sum_d = swap(terms[3][1], 1, "fsdp")
    near_sum_d = swap(terms[3][0], 2, "fsdp")
    far_sum_x = swap(terms[1][1], 1, "fsdp")
    near_sum_y = swap(terms[2][0], 2, "fsdp")
    gate_grad, up_grad = hidden_grads(grads, down, slope, silu, (terms[0][0],))
    back_d = grad_terms((3,), gate_grad, up_grad, gate, up)[0]
    far_back_d = swap(back_d[1], 1, "fsdp")
    near_back_d = swap(back_d[0], 2, "fsdp")
    far_sum_y = add_up([terms[2][1], far_sum_d], 1, (back_d[0],))
    near_sum_x = add_up([terms[1][0], near_sum_d], 1, (back_d[0],))
    back = grad_terms((0, 1, 2), gate_grad, up_grad, gate, up, (far_sum_y, near_sum_x))
    far_sum_y = swap(far_sum_y, 2, "fsdp")
    near_sum_x = swap(near_sum_x, 1, "fsdp")
    far_back_x = swap(back[1][1], 1, "fsdp")
    near_back_y = swap(back[2][0], 2, "fsdp")
    far_back_y = add_up([back[2][1], far_back_d])
    near_back_x = add_up([back[1][0], near_back_d])
    sent = (far_back_y, near_back_x)
    far_back_y = swap(far_back_y, 2, "fsdp")
    near_back_x = swap(near_back_x, 1, "fsdp")
    out2, out3 = add_up([terms[0][1], far_sum_x, far_sum_y], 2, sent)
    near_sum_y = add_up([terms[0][0], near_sum_y], 1, sent, LONG)
    out0, out1 = add_up([near_sum_y, near_sum_x], 2)
    grad_down, down_mark = down_grads(me, hidden, grads, (out0, out2))
    out3 = swap(out3, 6, "ep")
    out2 = swap(out2, 4, "ep")
    out1 = swap(out1, 2, "ep")
    back2, back3 = add_up([back[0][1], far_back_x, far_back_y], 2, (down_mark,))
    near_back_y = add_up([back[0][0], near_back_y], 1, (down_mark,), LONG)
    back0, back1 = add_up([near_back_y, near_back_x], 2)
    back3 = swap(back3, 6, "ep")
    back2 = swap(back2, 4, "ep")
    back1 = swap(back1, 2, "ep")
    layout = []
    for step in range(experts // 2):
        layout += [(step, 0), (experts // 2, step)]
    outs = [out0, out1, out2, out3]
    outs.append(swap(joined(*[piece[slots:] for piece in outs]), 1, "ep"))
    grad_gate, grad_up, mark = weight_grads(me, tokens, gate_grad, up_grad, (back0, back2))
    mixture = spread_rows(weighted, outs, layout, slots)
    backs = [back0, back1, back2, back3]
    odd = arrange(backs, [[(piece, slots, slots) for piece in range(4)]], (mark,))
    backs.append(swap(odd, 1, "ep"))
    grad_tokens = spread_rows(plain, backs, layout, slots)
    return mixture, grad_tokens, grad_gate[None], grad_up[None], grad_down[None]


def solution(mesh):
    placed = (
        P("ep", "fsdp"),
        P("ep", "fsdp"),
        P("ep", None, "fsdp"),
        P("ep", None, "fsdp"),
        P("ep", "fsdp", None),
        P(None, "ep", None),
        P(None, "ep"),
        P(None, "ep", None),
    )

    def per_part(*arrays):
        fits = mesh.shape["fsdp"] == 4 and mesh.shape["ep"] == 8 and arrays[0].shape[1] % 128 == 0
        return (by_links if fits else by_collectives)(*arrays)

    return jax.shard_map(
        per_part,
        mesh=mesh,
        in_specs=placed,
        out_specs=(
            P("ep", "fsdp"),
            P("ep", "fsdp"),
            P("ep", None, "fsdp"),
            P("ep", None, "fsdp"),
            P("ep", "fsdp", None),
        ),
        check_vma=False,
    )
```

```python
import functools

import jax
import jax.numpy as jnp
from jax import lax
from jax.experimental import pallas as pl
from jax.experimental.pallas import tpu as pltpu
from jax.sharding import PartitionSpec as P

ROWS = (((0,), (0,)), ((), ()))
LAST = (((1,), (1,)), ((), ()))
IN_VMEM = pl.BlockSpec(memory_space=pltpu.VMEM)
IN_SMEM = pl.BlockSpec(memory_space=pltpu.SMEM)
ANYWHERE = pl.BlockSpec(memory_space=pl.ANY)
MIB = 1024 * 1024


def run_kernel(body, name, operands, specs, outs, out_specs, scratch, mib, later=(), mark=False, cost=1024):
    used = len(operands)
    outs, out_specs = list(outs), list(out_specs)
    results = len(outs)
    if mark:
        outs.append(jax.ShapeDtypeStruct((8, 128), jnp.float32))
        out_specs.append(IN_VMEM)

    def run(*refs):
        refs = list(refs[len(later) :])
        if mark:
            mark_ref = refs.pop(used + results)
            mark_ref[...] = jnp.zeros_like(mark_ref)
        body(*refs)

    out = pl.pallas_call(
        run,
        name=name,
        in_specs=[*[ANYWHERE] * len(later), *specs],
        out_shape=outs,
        out_specs=out_specs,
        scratch_shapes=scratch,
        compiler_params=pltpu.CompilerParams(vmem_limit_bytes=mib * MIB),
        cost_estimate=pl.CostEstimate(flops=1024, bytes_accessed=cost, transcendentals=0),
    )(*later, *operands)
    return out if len(out) > 1 else out[0]


def in_hbm(array):
    return pltpu.with_memory_space_constraint(array, pltpu.HBM)


def like(rows, width, kind=jnp.bfloat16):
    return jax.ShapeDtypeStruct((rows, width), kind)


def slot_columns(me, chosen_ref, counts_ref, prob_ref):
    experts, _, slots = chosen_ref.shape
    diagonal = lax.broadcasted_iota(jnp.int32, (slots, slots), 0) == lax.broadcasted_iota(
        jnp.int32, (slots, slots), 1
    )
    position = lax.broadcasted_iota(jnp.int32, (slots, 1), 0)
    rows, weights = [], []
    for step in range(experts):
        expert = me ^ step
        live = position < counts_ref[0, expert]
        row = jnp.broadcast_to(chosen_ref[expert].astype(jnp.float32), (slots, slots))
        row = jnp.sum(jnp.where(diagonal, row, 0.0), axis=1, keepdims=True)
        prob = jnp.broadcast_to(prob_ref[expert], (slots, slots))
        prob = jnp.sum(jnp.where(diagonal, prob, 0.0), axis=1, keepdims=True)
        rows.append(jnp.where(live, row, -1.0))
        weights.append(jnp.where(live, prob, 0.0))
    return jnp.concatenate(rows, axis=0), jnp.concatenate(weights, axis=0)


def pick_body(me_ref, counts_hbm, chosen_hbm, prob_hbm, tokens_hbm, cotangent_hbm, *refs):
    *outs, mask_ref, weights_ref = refs[:-6]
    counts_ref, chosen_ref, prob_ref, tokens_ref, cotangent_ref, sems = refs[-6:]
    experts, _, slots = chosen_ref.shape
    pairs = (
        (counts_hbm, counts_ref),
        (chosen_hbm, chosen_ref),
        (prob_hbm, prob_ref),
        (tokens_hbm, tokens_ref),
        (cotangent_hbm, cotangent_ref),
    )
    copies = [pltpu.make_async_copy(*pair, sems.at[index]) for index, pair in enumerate(pairs)]
    for copy in copies:
        copy.start()
    for copy in copies[:3]:
        copy.wait()
    rows, weights = slot_columns(me_ref[0], chosen_ref, counts_ref, prob_ref)
    length = tokens_ref.shape[0]
    place = lax.broadcasted_iota(jnp.int32, (rows.shape[0], length), 1).astype(jnp.float32)
    mask = (place == rows).astype(jnp.bfloat16)
    mask_ref[...] = mask
    weights_ref[...] = jnp.broadcast_to(weights, weights_ref.shape)
    for which, source_ref in enumerate((tokens_ref, cotangent_ref)):
        copies[3 + which].wait()
        value = jnp.dot(mask, source_ref[...], preferred_element_type=jnp.float32)
        if which:
            value = weights * value
        value = value.astype(jnp.bfloat16)
        step = 0
        for out_ref in outs:
            for start in range(which * slots, out_ref.shape[0], 2 * slots):
                out_ref[pl.ds(start, slots), :] = value[step * slots : (step + 1) * slots]
                step += 1


def pick_slots(me, chosen, counts, gate_prob, tokens, cotangent, split):
    experts, _, slots = chosen.shape
    length, width = tokens.shape
    total = experts * slots
    operands = (counts, chosen, gate_prob, tokens, cotangent)
    return run_kernel(
        pick_body,
        "pick_slots",
        (me, *[in_hbm(array) for array in operands]),
        [IN_SMEM] + [ANYWHERE] * 5,
        [like(2 * slots * part, width) for part in split]
        + [like(total, length), like(total, 128, jnp.float32)],
        [IN_VMEM] * (len(split) + 2),
        [pltpu.SMEM(counts.shape, counts.dtype)]
        + [pltpu.VMEM(array.shape, array.dtype) for array in operands[1:]]
        + [pltpu.SemaphoreType.DMA((5,))],
        16,
    )


def spread_matrix_body(mask_ref, weights_ref, weighted_ref, plain_ref):
    mask = mask_ref[...].astype(jnp.float32)
    weights = weights_ref[...][:, :1]
    high = weights.astype(jnp.bfloat16).astype(jnp.float32)
    count = mask.shape[0]
    plain_ref[...] = mask.T.astype(jnp.bfloat16)
    weighted_ref[:, :count] = (mask * high).T.astype(jnp.bfloat16)
    weighted_ref[:, count:] = (mask * (weights - high)).T.astype(jnp.bfloat16)


def spread_matrices(mask, weights, later=()):
    count, length = mask.shape
    return run_kernel(
        spread_matrix_body,
        "spread_matrices",
        (mask, weights),
        [IN_VMEM] * 2,
        [like(length, 2 * count), like(length, count)],
        [IN_VMEM] * 2,
        [],
        8,
        later,
    )


def spread_body(layout, slots, spread_ref, *refs):
    pieces, (out_hbm, block, sems) = refs[:-3], refs[-3:]
    values = jnp.concatenate([pieces[p][pl.ds(q * slots, slots), :] for p, q in layout], axis=0)
    if spread_ref.shape[1] > values.shape[0]:
        values = jnp.concatenate([values, values], axis=0)
    parts = sems.shape[0]
    size = block.shape[0] // parts
    copies = []
    for part in range(parts):
        rows = pl.ds(part * size, size)
        total = jnp.dot(spread_ref[rows, :], values, preferred_element_type=jnp.float32)
        block[rows, :] = total.astype(jnp.bfloat16)
        copies.append(pltpu.make_async_copy(block.at[rows], out_hbm.at[rows], sems.at[part]))
        copies[-1].start()
    for copy in copies:
        copy.wait()


def spread_rows(spread, pieces, layout, slots, later=(), mark=False, parts=4):
    length, width = spread.shape[0], pieces[0].shape[1]
    return run_kernel(
        functools.partial(spread_body, layout, slots),
        "spread_rows",
        (spread, *pieces),
        [IN_VMEM] * (1 + len(pieces)),
        [like(length, width)],
        [ANYWHERE],
        [pltpu.VMEM((length, width), jnp.bfloat16), pltpu.SemaphoreType.DMA((parts,))],
        16,
        later,
        mark,
    )


def load_body(by_rows, count, me_ref, source_ref, target_ref, sems):
    width = target_ref.shape[1 if by_rows else 2]
    copies = []
    for index in range(count):
        part = pl.ds(pl.multiple_of((me_ref[0] ^ index) * width, width), width)
        source = source_ref.at[part, :] if by_rows else source_ref.at[:, part]
        copies.append(pltpu.make_async_copy(source, target_ref.at[index], sems.at[index]))
        copies[-1].start()
    for copy in copies:
        copy.wait()


def load_weight(me, weight, by_rows, count, later=()):
    first, second = weight.shape
    shape = (count, first // count, second) if by_rows else (count, first, second // count)
    return run_kernel(
        functools.partial(load_body, by_rows, count),
        "load_weight",
        (me, in_hbm(weight)),
        [IN_SMEM, ANYWHERE],
        [jax.ShapeDtypeStruct(shape, weight.dtype)],
        [IN_VMEM],
        [pltpu.SemaphoreType.DMA((count,))],
        4,
        later,
    )


def arrange_body(plan, used, *refs):
    for rows, out_ref in zip(plan, refs[used:]):
        start = 0
        for source, first, size in rows:
            out_ref[pl.ds(start, size), :] = refs[source][pl.ds(first, size), :]
            start += size


def arrange(sources, plan, later=(), cost=1024):
    width = sources[0].shape[1]
    sizes = [sum(size for _, _, size in rows) for rows in plan]
    return run_kernel(
        functools.partial(arrange_body, plan, len(sources)),
        "arrange",
        tuple(sources),
        [IN_VMEM] * len(sources),
        [like(size, width) for size in sizes],
        [IN_VMEM] * len(plan),
        [],
        8,
        later,
        cost=cost,
    )


def add_body(used, *refs):
    total = refs[0][...].astype(jnp.float32)
    for ref in refs[1:used]:
        total += ref[...].astype(jnp.float32)
    start = 0
    for out_ref in refs[used:]:
        out_ref[...] = total[start : start + out_ref.shape[0]].astype(out_ref.dtype)
        start += out_ref.shape[0]


def add_up(terms, parts=1, later=(), cost=1024):
    rows, width = terms[0].shape
    return run_kernel(
        functools.partial(add_body, len(terms)),
        "add_up",
        tuple(terms),
        [IN_VMEM] * len(terms),
        [like(rows // parts, width)] * parts,
        [IN_VMEM] * parts,
        [],
        8,
        later,
        cost=cost,
    )


class Slices:
    def __init__(self, pieces, part, slots):
        self.pieces, self.part, self.slots = pieces, part, slots
        self.flat = [piece for row in pieces for piece in row]
        self.rows = sum(piece.shape[0] for piece in pieces[0]) // 2
        self.width = self.flat[0].shape[1]

    def read(self, refs, index):
        first = sum(len(pieces) for pieces in self.pieces[:index])
        blocks = []
        for ref in refs[first : first + len(self.pieces[index])]:
            for start in range(self.part * self.slots, ref.shape[0], 2 * self.slots):
                blocks.append(ref[pl.ds(start, self.slots), :])
        return jnp.concatenate(blocks, axis=0)


def gather_slices(pieces, slots):
    parts = []
    for part in range(2):
        blocks = []
        for ref in pieces:
            for start in range(part * slots, ref.shape[0], 2 * slots):
                blocks.append(ref[pl.ds(start, slots), :])
        parts.append(jnp.concatenate(blocks, axis=0))
    return parts


def products(pieces, slots, index, gate_ref, up_ref, down_ref):
    tokens, grads = gather_slices(pieces, slots)
    return (
        jnp.dot(tokens, gate_ref[index], preferred_element_type=jnp.float32),
        jnp.dot(tokens, up_ref[index], preferred_element_type=jnp.float32),
        lax.dot_general(grads, down_ref[index], LAST, preferred_element_type=jnp.float32),
    )


def partial_body(counts, slots, *refs):
    gate_ref, up_ref, down_ref, *sums = refs[sum(counts) :]
    for index in range(len(counts)):
        first = sum(counts[:index])
        pieces = refs[first : first + counts[index]]
        more = products(pieces, slots, index, gate_ref, up_ref, down_ref)
        for sum_ref, value in zip(sums, more):
            if index == 0:
                sum_ref[...] = value
            else:
                sum_ref[...] += value


def partial_products(slices, slots, gate, up, down, later=()):
    counts = [len(pieces) for pieces in slices]
    flat = [piece for pieces in slices for piece in pieces]
    rows = sum(piece.shape[0] for piece in slices[0]) // 2
    return run_kernel(
        functools.partial(partial_body, counts, slots),
        "partial_products",
        (*flat, gate, up, down),
        [IN_VMEM] * (len(flat) + 3),
        [like(rows, gate.shape[2], jnp.float32)] * 3,
        [IN_VMEM] * 3,
        [],
        8,
        later,
    )


def hidden_body(used, slots, *refs):
    sums, gate_ref, up_ref, down_ref = refs[used : used + 3], *refs[used + 3 : used + 6]
    hidden_ref, gate_grad_ref, up_grad_ref, *terms = refs[used + 6 :]
    last = gate_ref.shape[0] - 1
    more = products(refs[:used], slots, last, gate_ref, up_ref, down_ref)
    gate, up, grad = [sum_ref[...] + value for sum_ref, value in zip(sums, more)]
    sigmoid = jax.nn.sigmoid(gate)
    silu = gate * sigmoid
    hidden = (silu * up).astype(jnp.bfloat16)
    hidden_ref[...] = hidden
    gate_grad_ref[...] = (grad * (up * sigmoid * (1.0 + gate * (1.0 - sigmoid)))).astype(
        jnp.bfloat16
    )
    up_grad_ref[...] = (grad * silu).astype(jnp.bfloat16)
    for index in reversed(range(last + 1)):
        term = jnp.dot(hidden, down_ref[index], preferred_element_type=jnp.float32)
        store_term(terms, index, term)


def store_term(refs, index, term):
    term = term.astype(jnp.bfloat16)
    if index < len(refs) - 2:
        refs[index][...] = term
    else:
        size = term.shape[0] // 2
        refs[index][...] = term[:size]
        refs[index + 1][...] = term[size:]


def hidden_units(pieces, slots, sums, gate, up, down, later=()):
    count, width, units = gate.shape
    rows = sums[0].shape[0]
    out = run_kernel(
        functools.partial(hidden_body, len(pieces), slots),
        "hidden_units",
        (*pieces, *sums, gate, up, down),
        [IN_VMEM] * (len(pieces) + 6),
        [like(rows, units)] * 3
        + [like(rows, width)] * (count - 1)
        + [like(rows // 2, width)] * 2,
        [IN_VMEM] * (4 + count),
        [],
        8,
        later,
    )
    return out[:3], out[3:]


def merge_body(first_ref, second_ref, top_ref, bottom_ref, first_out, second_out):
    size = top_ref.shape[0]
    top, bottom = pl.ds(0, size), pl.ds(size, size)
    for rows, part, source, other, out, other_out in (
        (top, top_ref, first_ref, second_ref, first_out, second_out),
        (bottom, bottom_ref, second_ref, first_ref, second_out, first_out),
    ):
        total = source[rows, :].astype(jnp.float32) + part[...].astype(jnp.float32)
        out[rows, :] = total.astype(out.dtype)
        other_out[rows, :] = other[rows, :]


def merge(first, second, top, bottom, later=()):
    return run_kernel(
        merge_body,
        "merge",
        (first, second, top, bottom),
        [IN_VMEM] * 4,
        [like(*first.shape)] * 2,
        [IN_VMEM] * 2,
        [],
        8,
        later,
    )


def grad_term_body(wanted, gate_grad_ref, up_grad_ref, gate_ref, up_ref, *terms):
    for place, index in enumerate(wanted):
        term = lax.dot_general(
            gate_grad_ref[...], gate_ref[index], LAST, preferred_element_type=jnp.float32
        )
        term += lax.dot_general(
            up_grad_ref[...], up_ref[index], LAST, preferred_element_type=jnp.float32
        )
        size = term.shape[0] // 2
        terms[2 * place][...] = term[:size].astype(jnp.bfloat16)
        terms[2 * place + 1][...] = term[size:].astype(jnp.bfloat16)


def grad_terms(wanted, gate_grad, up_grad, gate, up, later=()):
    _, width, _ = gate.shape
    rows = gate_grad.shape[0]
    terms = run_kernel(
        functools.partial(grad_term_body, wanted),
        "grad_terms",
        (gate_grad, up_grad, gate, up),
        [IN_VMEM] * 4,
        [like(rows // 2, width)] * (2 * len(wanted)),
        [IN_VMEM] * (2 * len(wanted)),
        [],
        8,
        later,
    )
    return [terms[2 * i : 2 * i + 2] for i in range(len(wanted))]


def down_grad_body(slices, me_ref, hidden_ref, *refs):
    out_ref, block, sems = refs[-3:]
    count, _, width = block.shape
    hidden = hidden_ref[...]
    copies = []
    for index in range(count):
        rows = slices.read(refs, index)
        block[index] = lax.dot_general(
            hidden, rows, ROWS, preferred_element_type=jnp.float32
        ).astype(jnp.bfloat16)
        start = pl.multiple_of((me_ref[0] ^ index) * width, width)
        target = out_ref.at[:, pl.ds(start, width)]
        copies.append(pltpu.make_async_copy(block.at[index], target, sems.at[index]))
        copies[-1].start()
    for copy in copies:
        copy.wait()


def down_grads(me, hidden, slices, later=()):
    count = len(slices.pieces)
    units = hidden.shape[1]
    return run_kernel(
        functools.partial(down_grad_body, slices),
        "down_grads",
        (me, hidden, *slices.flat),
        [IN_SMEM] + [IN_VMEM] * (1 + len(slices.flat)),
        [like(units, slices.width * count)],
        [ANYWHERE],
        [
            pltpu.VMEM((count, units, slices.width), jnp.bfloat16),
            pltpu.SemaphoreType.DMA((count,)),
        ],
        16,
        later,
        True,
    )


def weight_grad_body(slices, me_ref, *refs):
    grad_refs, (gate_hbm, up_hbm, block, sems) = refs[:2], refs[-4:]
    _, count, width, _ = block.shape
    copies = []
    for index in range(count):
        rows = slices.read(refs[2:], index)
        start = pl.multiple_of((me_ref[0] ^ index) * width, width)
        for which, out_ref in enumerate((gate_hbm, up_hbm)):
            block[which, index] = lax.dot_general(
                rows, grad_refs[which][...], ROWS, preferred_element_type=jnp.float32
            ).astype(jnp.bfloat16)
            target = out_ref.at[pl.ds(start, width), :]
            sem = sems.at[2 * index + which]
            copies.append(pltpu.make_async_copy(block.at[which, index], target, sem))
            copies[-1].start()
    for copy in copies:
        copy.wait()


def weight_grads(me, slices, gate_grad, up_grad, later=()):
    count = len(slices.pieces)
    units = gate_grad.shape[1]
    return run_kernel(
        functools.partial(weight_grad_body, slices),
        "weight_grads",
        (me, gate_grad, up_grad, *slices.flat),
        [IN_SMEM] + [IN_VMEM] * (2 + len(slices.flat)),
        [like(slices.width * count, units)] * 2,
        [ANYWHERE] * 2,
        [
            pltpu.VMEM((2, count, slices.width, units), jnp.bfloat16),
            pltpu.SemaphoreType.DMA((2 * count,)),
        ],
        20,
        later,
        True,
    )


def pick_rows(tokens, cotangent, row_index, live_mask, weight):
    flat_rows = row_index.reshape(-1)
    keep_rows = live_mask.reshape(-1)[:, None]
    taken_tokens = jnp.take(tokens, flat_rows, axis=0)
    picked_tokens = jnp.where(keep_rows, taken_tokens, jnp.zeros_like(taken_tokens))
    taken_grads = jnp.take(cotangent, flat_rows, axis=0).astype(jnp.float32)
    picked_grads = (weight.reshape(-1)[:, None] * taken_grads).astype(jnp.bfloat16)
    shaped = row_index.shape + (tokens.shape[1],)
    return (picked_tokens.reshape(shaped), picked_grads.reshape(shaped))


def to_slots(summed, experts, slot_count):
    return summed.astype(jnp.bfloat16).reshape(experts, slot_count, summed.shape[1])


def send_back(term, experts, slot_count):
    summed = lax.psum_scatter(
        term.astype(jnp.bfloat16), "fsdp", scatter_dimension=1, tiled=True
    ).astype(jnp.float32)
    return lax.all_to_all(
        to_slots(summed, experts, slot_count), "ep", split_axis=0, concat_axis=0, tiled=True
    )


def by_collectives(tokens, cotangent, gate_weight, up_weight, down_weight, chosen, counts, gate_prob):
    experts = chosen.shape[0]
    slot_count = chosen.shape[2]
    features = tokens.shape[1]
    row_index = chosen[:, 0, :]
    position = lax.broadcasted_iota(jnp.int32, (experts, slot_count), 1)
    live_mask = position < counts
    weight = jnp.where(live_mask, gate_prob[:, 0, :], 0.0)
    picked_tokens, picked_grads = pick_rows(tokens, cotangent, row_index, live_mask, weight)
    sliced_tokens, sliced_grads = (
        lax.all_to_all(picked_tokens, "ep", split_axis=0, concat_axis=0, tiled=True),
        lax.all_to_all(picked_grads, "ep", split_axis=0, concat_axis=0, tiled=True),
    )
    rows_tokens, rows_grads = (
        lax.all_gather(sliced_tokens, "fsdp", axis=2, tiled=True),
        lax.all_gather(sliced_grads, "fsdp", axis=2, tiled=True),
    )
    full_width = rows_tokens.shape[2]
    total_rows = rows_tokens.shape[0] * slot_count
    rows_tokens = rows_tokens.reshape(total_rows, full_width)
    rows_grads = rows_grads.reshape(total_rows, full_width)
    gate_local = gate_weight[0]
    up_local = up_weight[0]
    down_local = down_weight[0]
    pre_gate = jnp.dot(rows_tokens, gate_local, preferred_element_type=jnp.float32)
    pre_up = jnp.dot(rows_tokens, up_local, preferred_element_type=jnp.float32)
    sigmoid_gate = jax.nn.sigmoid(pre_gate)
    activated = pre_gate * sigmoid_gate
    hidden = (activated * pre_up).astype(jnp.bfloat16)
    output_term = jnp.dot(hidden, down_local, preferred_element_type=jnp.float32)
    output_back = send_back(output_term, experts, slot_count)
    contract_rows = (((0,), (0,)), ((), ()))
    contract_last = (((1,), (1,)), ((), ()))
    grad_hidden = lax.dot_general(
        rows_grads, down_local, contract_last, preferred_element_type=jnp.float32
    )
    grad_pre_gate = (
        grad_hidden * pre_up * sigmoid_gate * (1.0 + pre_gate * (1.0 - sigmoid_gate))
    ).astype(jnp.bfloat16)
    grad_pre_up = (grad_hidden * activated).astype(jnp.bfloat16)
    grad_down = lax.dot_general(
        hidden, rows_grads, contract_rows, preferred_element_type=jnp.float32
    ).astype(jnp.bfloat16)
    grad_gate = lax.dot_general(
        rows_tokens, grad_pre_gate, contract_rows, preferred_element_type=jnp.float32
    ).astype(jnp.bfloat16)
    grad_up = lax.dot_general(
        rows_tokens, grad_pre_up, contract_rows, preferred_element_type=jnp.float32
    ).astype(jnp.bfloat16)
    grad_term = lax.dot_general(
        grad_pre_gate, gate_local, contract_last, preferred_element_type=jnp.float32
    )
    grad_term = grad_term + lax.dot_general(
        grad_pre_up, up_local, contract_last, preferred_element_type=jnp.float32
    )
    grad_back = send_back(grad_term, experts, slot_count)
    flat_rows = row_index.reshape(-1)
    output_rows = output_back.reshape(-1, features).astype(jnp.float32)
    mixture = (
        jnp.zeros((tokens.shape[0], features), jnp.float32)
        .at[flat_rows]
        .add(weight.reshape(-1)[:, None] * output_rows)
    )
    grad_rows = jnp.where(
        live_mask.reshape(-1)[:, None], grad_back.reshape(-1, features).astype(jnp.float32), 0.0
    )
    grad_tokens = jnp.zeros((tokens.shape[0], features), jnp.float32).at[flat_rows].add(grad_rows)
    return (
        mixture.astype(jnp.bfloat16),
        grad_tokens.astype(jnp.bfloat16),
        grad_gate[None],
        grad_up[None],
        grad_down[None],
    )


LONG = 64 * MIB


def swap(array, distance, axis):
    size = lax.axis_size(axis)
    return lax.ppermute(array, axis, [(i, i ^ distance) for i in range(size)])


def joined(*arrays):
    return jnp.concatenate(arrays, axis=0)


def by_links(tokens, cotangent, gate_weight, up_weight, down_weight, chosen, counts, gate_prob):
    experts, _, slots = chosen.shape
    count = lax.axis_size("fsdp")
    ep_index = lax.axis_index("ep").reshape(1)
    me = lax.axis_index("fsdp").reshape(1)
    two = 2 * slots
    half = 2 * two
    own, core, even1, odd1, pair2, pair3, mask, weights = pick_slots(
        ep_index,
        chosen,
        counts.reshape(1, experts),
        gate_prob,
        tokens,
        cotangent,
        (1, 1, 1, 1, 2, 2),
    )

    pair2 = swap(pair2, 4, "ep")
    pair3 = swap(pair3, 6, "ep")
    even1 = swap(even1, 2, "ep")
    odd1 = swap(odd1, 3, "ep")
    core = swap(core, 1, "ep")

    gate = load_weight(me, gate_weight[0], True, count, (own,))
    up = load_weight(me, up_weight[0], True, count, (gate,))
    weighted, plain = spread_matrices(mask, weights, (up,))
    near = joined(arrange((own,), [[(0, 0, two)]], (weighted,)), core, even1, odd1)
    near_x = swap(near, 1, "fsdp")
    near_y = swap(near, 2, "fsdp")
    near_d = [swap(near_x[:half], 2, "fsdp"), swap(near_y[half:], 1, "fsdp")]
    odd = swap(joined(pair2[two:], pair3[two:]), 1, "ep")
    far = arrange(
        (pair2, pair3, odd),
        [[(0, 0, two), (2, 0, two), (1, 0, two), (2, two, two)]],
        (near_x, near_y),
    )
    far_x = swap(far, 1, "fsdp")
    far_y = swap(far, 2, "fsdp")
    down = load_weight(me, down_weight[0], False, count, (far,))
    far_d = [swap(far_x[:half], 2, "fsdp"), swap(far_y[half:], 1, "fsdp")]
    pieces = [[near, far], [near_x, far_x], [near_y, far_y], near_d + far_d]
    tokens, grads = Slices(pieces, 0, slots), Slices(pieces, 1, slots)

    sums = partial_products(pieces[:3], slots, gate, up, down)
    (hidden, gate_grad, up_grad), terms = hidden_units(pieces[3], slots, sums, gate, up, down)
    top = swap(terms[3], 2, "fsdp")
    bottom = swap(terms[4], 1, "fsdp")
    back = grad_terms((3, 1, 2, 0), gate_grad, up_grad, gate, up, (terms[0],))
    back_d, back_x, back_y, back_own = back
    far_back_d = swap(back_d[1], 1, "fsdp")
    near_back_d = swap(back_d[0], 2, "fsdp")
    far_back_x = swap(back_x[1], 1, "fsdp")
    sum_x, sum_y = merge(terms[1], terms[2], top, bottom, (back_own[0],))
    sum_x = swap(sum_x, 1, "fsdp")
    sum_y = swap(sum_y, 2, "fsdp")

    far_back_y = add_up([back_y[1], far_back_d])
    near_back_x = add_up([back_x[0], near_back_d])
    sent = (far_back_y, near_back_x)
    far_back_y = swap(far_back_y, 2, "fsdp")
    near_back_x = swap(near_back_x, 1, "fsdp")
    near_back_y = swap(back_y[0], 2, "fsdp")
    grad_down, down_mark = down_grads(me, hidden, grads, sent)
    out0, out1, out2, out3 = add_up([terms[0], sum_x, sum_y], 4, (down_mark,))
    out3 = swap(out3, 6, "ep")
    out2 = swap(out2, 4, "ep")
    out1 = swap(out1, 2, "ep")
    back2, back3 = add_up([back_own[1], far_back_x, far_back_y], 2, (down_mark,))
    back0, back1 = add_up([back_own[0], near_back_x, near_back_y], 2, (down_mark,))
    back3 = swap(back3, 6, "ep")
    back2 = swap(back2, 4, "ep")
    back1 = swap(back1, 2, "ep")
    layout = []
    for step in range(experts // 2):
        layout += [(step, 0), (experts // 2, step)]
    outs = [out0, out1, out2, out3]
    outs.append(swap(joined(*[piece[slots:] for piece in outs]), 1, "ep"))
    grad_gate, grad_up, mark = weight_grads(me, tokens, gate_grad, up_grad, (back0, back2))
    mixture = spread_rows(weighted, outs, layout, slots)
    backs = [back0, back1, back2, back3]
    odd = arrange(backs, [[(piece, slots, slots) for piece in range(4)]], (mark,))
    backs.append(swap(odd, 1, "ep"))
    grad_tokens = spread_rows(plain, backs, layout, slots)
    return mixture, grad_tokens, grad_gate[None], grad_up[None], grad_down[None]


def solution(mesh):
    placed = (
        P("ep", "fsdp"),
        P("ep", "fsdp"),
        P("ep", None, "fsdp"),
        P("ep", None, "fsdp"),
        P("ep", "fsdp", None),
        P(None, "ep", None),
        P(None, "ep"),
        P(None, "ep", None),
    )

    def per_part(*arrays):
        fits = mesh.shape["fsdp"] == 4 and mesh.shape["ep"] == 8 and arrays[0].shape[1] % 128 == 0
        return (by_links if fits else by_collectives)(*arrays)

    return jax.shard_map(
        per_part,
        mesh=mesh,
        in_specs=placed,
        out_specs=(
            P("ep", "fsdp"),
            P("ep", "fsdp"),
            P("ep", None, "fsdp"),
            P("ep", None, "fsdp"),
            P("ep", "fsdp", None),
        ),
        check_vma=False,
    )
```

```python
import functools

import jax
import jax.numpy as jnp
from jax import lax
from jax.experimental import pallas as pl
from jax.experimental.pallas import tpu as pltpu
from jax.sharding import PartitionSpec as P

ROWS = (((0,), (0,)), ((), ()))
PLAIN = (((1,), (0,)), ((), ()))
LAST = (((1,), (1,)), ((), ()))
IN_VMEM = pl.BlockSpec(memory_space=pltpu.VMEM)
IN_SMEM = pl.BlockSpec(memory_space=pltpu.SMEM)
ANYWHERE = pl.BlockSpec(memory_space=pl.ANY)
MIB = 1024 * 1024


def run_kernel(body, name, operands, specs, outs, out_specs, scratch, mib, later=(), mark=False, cost=1024):
    used = len(operands)
    outs, out_specs = list(outs), list(out_specs)
    results = len(outs)
    if mark:
        outs.append(jax.ShapeDtypeStruct((8, 128), jnp.float32))
        out_specs.append(IN_VMEM)

    def run(*refs):
        refs = list(refs[len(later) :])
        if mark:
            mark_ref = refs.pop(used + results)
            mark_ref[...] = jnp.zeros_like(mark_ref)
        body(*refs)

    out = pl.pallas_call(
        run,
        name=name,
        in_specs=[*[ANYWHERE] * len(later), *specs],
        out_shape=outs,
        out_specs=out_specs,
        scratch_shapes=scratch,
        compiler_params=pltpu.CompilerParams(vmem_limit_bytes=mib * MIB),
        cost_estimate=pl.CostEstimate(flops=1024, bytes_accessed=cost, transcendentals=0),
    )(*later, *operands)
    return out if len(out) > 1 else out[0]


def in_hbm(array):
    return pltpu.with_memory_space_constraint(array, pltpu.HBM)


def like(rows, width, kind=jnp.bfloat16):
    return jax.ShapeDtypeStruct((rows, width), kind)


def slot_columns(me, chosen_ref, counts_ref, prob_ref):
    experts, _, slots = chosen_ref.shape
    diagonal = lax.broadcasted_iota(jnp.int32, (slots, slots), 0) == lax.broadcasted_iota(
        jnp.int32, (slots, slots), 1
    )
    position = lax.broadcasted_iota(jnp.int32, (slots, 1), 0)
    rows, weights = [], []
    for step in range(experts):
        expert = me ^ step
        live = position < counts_ref[0, expert]
        row = jnp.broadcast_to(chosen_ref[expert].astype(jnp.float32), (slots, slots))
        row = jnp.sum(jnp.where(diagonal, row, 0.0), axis=1, keepdims=True)
        prob = jnp.broadcast_to(prob_ref[expert], (slots, slots))
        prob = jnp.sum(jnp.where(diagonal, prob, 0.0), axis=1, keepdims=True)
        rows.append(jnp.where(live, row, -1.0))
        weights.append(jnp.where(live, prob, 0.0))
    return jnp.concatenate(rows, axis=0), jnp.concatenate(weights, axis=0)


def pick_body(plan, me_ref, counts_hbm, chosen_hbm, prob_hbm, tokens_hbm, cotangent_hbm, *refs):
    *outs, mask_ref, weights_ref = refs[:-6]
    counts_ref, chosen_ref, prob_ref, tokens_ref, cotangent_ref, sems = refs[-6:]
    experts, _, slots = chosen_ref.shape
    pairs = (
        (counts_hbm, counts_ref),
        (chosen_hbm, chosen_ref),
        (prob_hbm, prob_ref),
        (tokens_hbm, tokens_ref),
        (cotangent_hbm, cotangent_ref),
    )
    copies = [pltpu.make_async_copy(*pair, sems.at[index]) for index, pair in enumerate(pairs)]
    for copy in copies:
        copy.start()
    for copy in copies[:3]:
        copy.wait()
    rows, weights = slot_columns(me_ref[0], chosen_ref, counts_ref, prob_ref)
    length = tokens_ref.shape[0]
    place = lax.broadcasted_iota(jnp.int32, (rows.shape[0], length), 1).astype(jnp.float32)
    mask = (place == rows).astype(jnp.bfloat16)
    mask_ref[...] = mask
    weights_ref[...] = jnp.broadcast_to(weights, weights_ref.shape)
    for which, source_ref in enumerate((tokens_ref, cotangent_ref)):
        copies[3 + which].wait()
        value = jnp.dot(mask, source_ref[...], preferred_element_type=jnp.float32)
        if which:
            value = weights * value
        value = value.astype(jnp.bfloat16)
        for out_ref, blocks in zip(outs, plan):
            for place, (part, step) in enumerate(blocks):
                if part == which:
                    target = pl.ds(place * slots, slots)
                    out_ref[target, :] = value[step * slots : (step + 1) * slots]


def pick_slots(me, chosen, counts, gate_prob, tokens, cotangent, plan):
    experts, _, slots = chosen.shape
    length, width = tokens.shape
    total = experts * slots
    operands = (counts, chosen, gate_prob, tokens, cotangent)
    return run_kernel(
        functools.partial(pick_body, plan),
        "pick_slots",
        (me, *[in_hbm(array) for array in operands]),
        [IN_SMEM] + [ANYWHERE] * 5,
        [like(slots * len(blocks), width) for blocks in plan]
        + [like(total, length), like(total, 128, jnp.float32)],
        [IN_VMEM] * (len(plan) + 2),
        [pltpu.SMEM(counts.shape, counts.dtype)]
        + [pltpu.VMEM(array.shape, array.dtype) for array in operands[1:]]
        + [pltpu.SemaphoreType.DMA((5,))],
        16,
    )


def spread_matrix_body(mask_ref, weights_ref, weighted_ref, plain_ref):
    mask = mask_ref[...].astype(jnp.float32)
    weights = weights_ref[...][:, :1]
    high = weights.astype(jnp.bfloat16).astype(jnp.float32)
    count = mask.shape[0]
    plain_ref[...] = mask.T.astype(jnp.bfloat16)
    weighted_ref[:, :count] = (mask * high).T.astype(jnp.bfloat16)
    weighted_ref[:, count:] = (mask * (weights - high)).T.astype(jnp.bfloat16)


def spread_matrices(mask, weights, later=()):
    count, length = mask.shape
    return run_kernel(
        spread_matrix_body,
        "spread_matrices",
        (mask, weights),
        [IN_VMEM] * 2,
        [like(length, 2 * count), like(length, count)],
        [IN_VMEM] * 2,
        [],
        8,
        later,
    )


def spread_body(layout, slots, spread_ref, *refs):
    pieces, (out_hbm, block, sems) = refs[:-3], refs[-3:]
    values = jnp.concatenate([pieces[p][pl.ds(q * slots, slots), :] for p, q in layout], axis=0)
    if spread_ref.shape[1] > values.shape[0]:
        values = jnp.concatenate([values, values], axis=0)
    parts = sems.shape[0]
    size = block.shape[0] // parts
    copies = []
    for part in range(parts):
        rows = pl.ds(part * size, size)
        total = jnp.dot(spread_ref[rows, :], values, preferred_element_type=jnp.float32)
        block[rows, :] = total.astype(jnp.bfloat16)
        copies.append(pltpu.make_async_copy(block.at[rows], out_hbm.at[rows], sems.at[part]))
        copies[-1].start()
    for copy in copies:
        copy.wait()


def spread_rows(spread, pieces, layout, slots, later=(), mark=False, parts=4):
    length, width = spread.shape[0], pieces[0].shape[1]
    return run_kernel(
        functools.partial(spread_body, layout, slots),
        "spread_rows",
        (spread, *pieces),
        [IN_VMEM] * (1 + len(pieces)),
        [like(length, width)],
        [ANYWHERE],
        [pltpu.VMEM((length, width), jnp.bfloat16), pltpu.SemaphoreType.DMA((parts,))],
        16,
        later,
        mark,
    )


def load_body(by_rows, count, me_ref, source_ref, target_ref, sems):
    width = target_ref.shape[1 if by_rows else 2]
    copies = []
    for index in range(count):
        part = pl.ds(pl.multiple_of((me_ref[0] ^ index) * width, width), width)
        source = source_ref.at[part, :] if by_rows else source_ref.at[:, part]
        copies.append(pltpu.make_async_copy(source, target_ref.at[index], sems.at[index]))
        copies[-1].start()
    for copy in copies:
        copy.wait()


def load_weight(me, weight, by_rows, count, later=()):
    first, second = weight.shape
    shape = (count, first // count, second) if by_rows else (count, first, second // count)
    return run_kernel(
        functools.partial(load_body, by_rows, count),
        "load_weight",
        (me, in_hbm(weight)),
        [IN_SMEM, ANYWHERE],
        [jax.ShapeDtypeStruct(shape, weight.dtype)],
        [IN_VMEM],
        [pltpu.SemaphoreType.DMA((count,))],
        4,
        later,
    )


def arrange_body(plan, used, *refs):
    for rows, out_ref in zip(plan, refs[used:]):
        start = 0
        for source, first, size in rows:
            out_ref[pl.ds(start, size), :] = refs[source][pl.ds(first, size), :]
            start += size


def arrange(sources, plan, later=(), cost=1024):
    width = sources[0].shape[1]
    sizes = [sum(size for _, _, size in rows) for rows in plan]
    return run_kernel(
        functools.partial(arrange_body, plan, len(sources)),
        "arrange",
        tuple(sources),
        [IN_VMEM] * len(sources),
        [like(size, width) for size in sizes],
        [IN_VMEM] * len(plan),
        [],
        8,
        later,
        cost=cost,
    )


def add_body(used, *refs):
    total = refs[0][...].astype(jnp.float32)
    for ref in refs[1:used]:
        total += ref[...].astype(jnp.float32)
    start = 0
    for out_ref in refs[used:]:
        out_ref[...] = total[start : start + out_ref.shape[0]].astype(out_ref.dtype)
        start += out_ref.shape[0]


def add_up(terms, parts=1, later=(), cost=1024):
    rows, width = terms[0].shape
    return run_kernel(
        functools.partial(add_body, len(terms)),
        "add_up",
        tuple(terms),
        [IN_VMEM] * len(terms),
        [like(rows // parts, width)] * parts,
        [IN_VMEM] * parts,
        [],
        8,
        later,
        cost=cost,
    )


def add_pairs_body(*refs):
    for first_ref, second_ref, out_ref in zip(refs[0:4:2], refs[1:4:2], refs[4:]):
        total = first_ref[...].astype(jnp.float32) + second_ref[...].astype(jnp.float32)
        out_ref[...] = total.astype(out_ref.dtype)


def add_pairs(first, second, later=()):
    return run_kernel(
        add_pairs_body,
        "add_pairs",
        (*first, *second),
        [IN_VMEM] * 4,
        [like(*first[0].shape), like(*second[0].shape)],
        [IN_VMEM] * 2,
        [],
        8,
        later,
    )


class Slices:
    def __init__(self, slices, part, slots):
        self.mixed = [[mixed for _, mixed in pieces] for pieces in slices]
        self.flat = [array for pieces in slices for array, _ in pieces]
        self.part, self.slots = part, slots
        self.count, self.width = len(slices), self.flat[0].shape[1]
        self.rows = sum(array.shape[0] // (2 if mixed else 1) for array, mixed in slices[0])

    def read(self, refs, index):
        first = sum(len(mixed) for mixed in self.mixed[:index])
        blocks = []
        for place, mixed in enumerate(self.mixed[index]):
            ref = refs[first + place]
            if mixed:
                for start in range(self.part * self.slots, ref.shape[0], 2 * self.slots):
                    blocks.append(ref[pl.ds(start, self.slots), :])
            else:
                blocks.append(ref[...])
        return blocks[0] if len(blocks) == 1 else jnp.concatenate(blocks, axis=0)


def partial_body(slices, dims, *refs):
    used = len(slices.flat)
    weights, sums = refs[used:][: len(dims)], refs[used + len(dims) :]
    for index in range(slices.count):
        rows = slices.read(refs, index)
        for weight_ref, dim, sum_ref in zip(weights, dims, sums):
            value = lax.dot_general(
                rows, weight_ref[index], dim, preferred_element_type=jnp.float32
            )
            if index == 0:
                sum_ref[...] = value
            else:
                sum_ref[...] += value


def partial_products(slices, weights, dims, units, later=()):
    return run_kernel(
        functools.partial(partial_body, slices, dims),
        "partial_products",
        (*slices.flat, *weights),
        [IN_VMEM] * (len(slices.flat) + len(weights)),
        [like(slices.rows, units, jnp.float32)] * len(weights),
        [IN_VMEM] * len(weights),
        [],
        8,
        later,
    )


def store_term(refs, index, term):
    term = term.astype(jnp.bfloat16)
    size = term.shape[0] // 2
    refs[2 * index][...] = term[:size]
    refs[2 * index + 1][...] = term[size:]


def forward_body(slices, *refs):
    used = len(slices.flat)
    gate_sum, up_sum, gate_ref, up_ref, down_ref = refs[used : used + 5]
    hidden_ref, slope_ref, silu_ref, *terms = refs[used + 5 :]
    last = gate_ref.shape[0] - 1
    rows = slices.read(refs, 0)
    gate = gate_sum[...] + jnp.dot(rows, gate_ref[last], preferred_element_type=jnp.float32)
    up = up_sum[...] + jnp.dot(rows, up_ref[last], preferred_element_type=jnp.float32)
    sigmoid = jax.nn.sigmoid(gate)
    silu = gate * sigmoid
    hidden = (silu * up).astype(jnp.bfloat16)
    hidden_ref[...] = hidden
    slope_ref[...] = up * sigmoid * (1.0 + gate * (1.0 - sigmoid))
    silu_ref[...] = silu
    for index in reversed(range(last + 1)):
        term = jnp.dot(hidden, down_ref[index], preferred_element_type=jnp.float32)
        store_term(terms, index, term)


def forward_terms(slices, sums, gate, up, down, later=()):
    count, width, units = gate.shape
    rows = sums[0].shape[0]
    f32 = jnp.float32
    out = run_kernel(
        functools.partial(forward_body, slices),
        "forward_terms",
        (*slices.flat, *sums, gate, up, down),
        [IN_VMEM] * (len(slices.flat) + 5),
        [like(rows, units), like(rows, units, f32), like(rows, units, f32)]
        + [like(rows // 2, width)] * (2 * count),
        [IN_VMEM] * (3 + 2 * count),
        [],
        8,
        later,
    )
    return out[:3], [out[3 + 2 * i : 5 + 2 * i] for i in range(count)]


def backward_body(slices, *refs):
    used = len(slices.flat)
    grad_sum, slope_ref, silu_ref, gate_ref, up_ref, down_ref = refs[used : used + 6]
    gate_grad_ref, up_grad_ref, *terms = refs[used + 6 :]
    last = gate_ref.shape[0] - 1
    rows = slices.read(refs, 0)
    grad = lax.dot_general(rows, down_ref[last], LAST, preferred_element_type=jnp.float32)
    grad += grad_sum[...]
    gate_grad = (grad * slope_ref[...]).astype(jnp.bfloat16)
    up_grad = (grad * silu_ref[...]).astype(jnp.bfloat16)
    gate_grad_ref[...] = gate_grad
    up_grad_ref[...] = up_grad
    store_term(terms, 0, back_term(gate_grad, up_grad, gate_ref, up_ref, last))


def back_term(gate_grad, up_grad, gate_ref, up_ref, index):
    term = lax.dot_general(gate_grad, gate_ref[index], LAST, preferred_element_type=jnp.float32)
    return term + lax.dot_general(up_grad, up_ref[index], LAST, preferred_element_type=jnp.float32)


def backward_rest_body(gate_grad_ref, up_grad_ref, gate_ref, up_ref, *terms):
    for index in reversed(range(len(terms) // 2)):
        term = back_term(gate_grad_ref[...], up_grad_ref[...], gate_ref, up_ref, index)
        store_term(terms, index, term)


def backward_rest(gate_grad, up_grad, gate, up, later=()):
    count, width, _ = gate.shape
    rows = gate_grad.shape[0]
    out = run_kernel(
        backward_rest_body,
        "backward_rest",
        (gate_grad, up_grad, gate, up),
        [IN_VMEM] * 4,
        [like(rows // 2, width)] * (2 * count - 2),
        [IN_VMEM] * (2 * count - 2),
        [],
        8,
        later,
    )
    return [out[2 * i : 2 * i + 2] for i in range(count - 1)]


def backward_terms(slices, grad_sum, slope, silu, gate, up, down, later=()):
    _, width, units = gate.shape
    rows = slope.shape[0]
    out = run_kernel(
        functools.partial(backward_body, slices),
        "backward_terms",
        (*slices.flat, grad_sum, slope, silu, gate, up, down),
        [IN_VMEM] * (len(slices.flat) + 6),
        [like(rows, units)] * 2 + [like(rows // 2, width)] * 2,
        [IN_VMEM] * 4,
        [],
        8,
        later,
    )
    return out[:2], out[2:]


def merge_body(first_top, first_bottom, second_top, second_bottom, top, bottom, first, second):
    size = top.shape[0]
    upper, lower = pl.ds(0, size), pl.ds(size, size)
    total = first_top[...].astype(jnp.float32) + top[...].astype(jnp.float32)
    first[upper, :] = total.astype(first.dtype)
    first[lower, :] = first_bottom[...]
    total = second_bottom[...].astype(jnp.float32) + bottom[...].astype(jnp.float32)
    second[lower, :] = total.astype(second.dtype)
    second[upper, :] = second_top[...]


def merge(first, second, top, bottom, later=()):
    rows, width = first[0].shape
    return run_kernel(
        merge_body,
        "merge",
        (*first, *second, top, bottom),
        [IN_VMEM] * 6,
        [like(2 * rows, width)] * 2,
        [IN_VMEM] * 2,
        [],
        8,
        later,
    )


def down_grad_body(slices, me_ref, hidden_ref, *refs):
    out_ref, block, sems = refs[-3:]
    count, _, width = block.shape
    hidden = hidden_ref[...]
    copies = []
    for index in range(count):
        rows = slices.read(refs, index)
        block[index] = lax.dot_general(
            hidden, rows, ROWS, preferred_element_type=jnp.float32
        ).astype(jnp.bfloat16)
        start = pl.multiple_of((me_ref[0] ^ index) * width, width)
        target = out_ref.at[:, pl.ds(start, width)]
        copies.append(pltpu.make_async_copy(block.at[index], target, sems.at[index]))
        copies[-1].start()
    for copy in copies:
        copy.wait()


def down_grads(me, hidden, slices, later=()):
    count, width, units = slices.count, slices.width, hidden.shape[1]
    return run_kernel(
        functools.partial(down_grad_body, slices),
        "down_grads",
        (me, hidden, *slices.flat),
        [IN_SMEM] + [IN_VMEM] * (1 + len(slices.flat)),
        [like(units, width * count)],
        [ANYWHERE],
        [
            pltpu.VMEM((count, units, width), jnp.bfloat16),
            pltpu.SemaphoreType.DMA((count,)),
        ],
        16,
        later,
        True,
    )


def weight_grad_body(slices, me_ref, *refs):
    grad_refs, (gate_hbm, up_hbm, block, sems) = refs[:2], refs[-4:]
    _, count, width, _ = block.shape
    copies = []
    for index in range(count):
        rows = slices.read(refs[2:], index)
        start = pl.multiple_of((me_ref[0] ^ index) * width, width)
        for which, out_ref in enumerate((gate_hbm, up_hbm)):
            block[which, index] = lax.dot_general(
                rows, grad_refs[which][...], ROWS, preferred_element_type=jnp.float32
            ).astype(jnp.bfloat16)
            target = out_ref.at[pl.ds(start, width), :]
            sem = sems.at[2 * index + which]
            copies.append(pltpu.make_async_copy(block.at[which, index], target, sem))
            copies[-1].start()
    for copy in copies:
        copy.wait()


def weight_grads(me, slices, gate_grad, up_grad, later=()):
    count, width, units = slices.count, slices.width, gate_grad.shape[1]
    return run_kernel(
        functools.partial(weight_grad_body, slices),
        "weight_grads",
        (me, gate_grad, up_grad, *slices.flat),
        [IN_SMEM] + [IN_VMEM] * (2 + len(slices.flat)),
        [like(width * count, units)] * 2,
        [ANYWHERE] * 2,
        [
            pltpu.VMEM((2, count, width, units), jnp.bfloat16),
            pltpu.SemaphoreType.DMA((2 * count,)),
        ],
        20,
        later,
        True,
    )


def pick_rows(tokens, cotangent, row_index, live_mask, weight):
    flat_rows = row_index.reshape(-1)
    keep_rows = live_mask.reshape(-1)[:, None]
    taken_tokens = jnp.take(tokens, flat_rows, axis=0)
    picked_tokens = jnp.where(keep_rows, taken_tokens, jnp.zeros_like(taken_tokens))
    taken_grads = jnp.take(cotangent, flat_rows, axis=0).astype(jnp.float32)
    picked_grads = (weight.reshape(-1)[:, None] * taken_grads).astype(jnp.bfloat16)
    shaped = row_index.shape + (tokens.shape[1],)
    return (picked_tokens.reshape(shaped), picked_grads.reshape(shaped))


def to_slots(summed, experts, slot_count):
    return summed.astype(jnp.bfloat16).reshape(experts, slot_count, summed.shape[1])


def send_back(term, experts, slot_count):
    summed = lax.psum_scatter(
        term.astype(jnp.bfloat16), "fsdp", scatter_dimension=1, tiled=True
    ).astype(jnp.float32)
    return lax.all_to_all(
        to_slots(summed, experts, slot_count), "ep", split_axis=0, concat_axis=0, tiled=True
    )


def by_collectives(tokens, cotangent, gate_weight, up_weight, down_weight, chosen, counts, gate_prob):
    experts = chosen.shape[0]
    slot_count = chosen.shape[2]
    features = tokens.shape[1]
    row_index = chosen[:, 0, :]
    position = lax.broadcasted_iota(jnp.int32, (experts, slot_count), 1)
    live_mask = position < counts
    weight = jnp.where(live_mask, gate_prob[:, 0, :], 0.0)
    picked_tokens, picked_grads = pick_rows(tokens, cotangent, row_index, live_mask, weight)
    sliced_tokens, sliced_grads = (
        lax.all_to_all(picked_tokens, "ep", split_axis=0, concat_axis=0, tiled=True),
        lax.all_to_all(picked_grads, "ep", split_axis=0, concat_axis=0, tiled=True),
    )
    rows_tokens, rows_grads = (
        lax.all_gather(sliced_tokens, "fsdp", axis=2, tiled=True),
        lax.all_gather(sliced_grads, "fsdp", axis=2, tiled=True),
    )
    full_width = rows_tokens.shape[2]
    total_rows = rows_tokens.shape[0] * slot_count
    rows_tokens = rows_tokens.reshape(total_rows, full_width)
    rows_grads = rows_grads.reshape(total_rows, full_width)
    gate_local = gate_weight[0]
    up_local = up_weight[0]
    down_local = down_weight[0]
    pre_gate = jnp.dot(rows_tokens, gate_local, preferred_element_type=jnp.float32)
    pre_up = jnp.dot(rows_tokens, up_local, preferred_element_type=jnp.float32)
    sigmoid_gate = jax.nn.sigmoid(pre_gate)
    activated = pre_gate * sigmoid_gate
    hidden = (activated * pre_up).astype(jnp.bfloat16)
    output_term = jnp.dot(hidden, down_local, preferred_element_type=jnp.float32)
    output_back = send_back(output_term, experts, slot_count)
    contract_rows = (((0,), (0,)), ((), ()))
    contract_last = (((1,), (1,)), ((), ()))
    grad_hidden = lax.dot_general(
        rows_grads, down_local, contract_last, preferred_element_type=jnp.float32
    )
    grad_pre_gate = (
        grad_hidden * pre_up * sigmoid_gate * (1.0 + pre_gate * (1.0 - sigmoid_gate))
    ).astype(jnp.bfloat16)
    grad_pre_up = (grad_hidden * activated).astype(jnp.bfloat16)
    grad_down = lax.dot_general(
        hidden, rows_grads, contract_rows, preferred_element_type=jnp.float32
    ).astype(jnp.bfloat16)
    grad_gate = lax.dot_general(
        rows_tokens, grad_pre_gate, contract_rows, preferred_element_type=jnp.float32
    ).astype(jnp.bfloat16)
    grad_up = lax.dot_general(
        rows_tokens, grad_pre_up, contract_rows, preferred_element_type=jnp.float32
    ).astype(jnp.bfloat16)
    grad_term = lax.dot_general(
        grad_pre_gate, gate_local, contract_last, preferred_element_type=jnp.float32
    )
    grad_term = grad_term + lax.dot_general(
        grad_pre_up, up_local, contract_last, preferred_element_type=jnp.float32
    )
    grad_back = send_back(grad_term, experts, slot_count)
    flat_rows = row_index.reshape(-1)
    output_rows = output_back.reshape(-1, features).astype(jnp.float32)
    mixture = (
        jnp.zeros((tokens.shape[0], features), jnp.float32)
        .at[flat_rows]
        .add(weight.reshape(-1)[:, None] * output_rows)
    )
    grad_rows = jnp.where(
        live_mask.reshape(-1)[:, None], grad_back.reshape(-1, features).astype(jnp.float32), 0.0
    )
    grad_tokens = jnp.zeros((tokens.shape[0], features), jnp.float32).at[flat_rows].add(grad_rows)
    return (
        mixture.astype(jnp.bfloat16),
        grad_tokens.astype(jnp.bfloat16),
        grad_gate[None],
        grad_up[None],
        grad_down[None],
    )


def swap(array, distance, axis):
    size = lax.axis_size(axis)
    return lax.ppermute(array, axis, [(i, i ^ distance) for i in range(size)])


def joined(*arrays):
    return jnp.concatenate(arrays, axis=0)


def gathered(whole, first, second):
    from_first = swap(whole, first, "fsdp")
    from_second = swap(whole, second, "fsdp")
    passed = arrange((from_first,), [[(0, 0, whole.shape[0])]], (from_second,))
    slices = [[whole], [None], [None], [swap(passed, second, "fsdp")]]
    slices[first], slices[second] = [from_first], [from_second]
    return slices


def pieces_of(mixed, plain):
    return [
        [(piece, True) for piece in some] + [(piece, False) for piece in others]
        for some, others in zip(mixed, plain)
    ]


def by_links(tokens, cotangent, gate_weight, up_weight, down_weight, chosen, counts, gate_prob):
    experts, _, slots = chosen.shape
    count = lax.axis_size("fsdp")
    ep_index = lax.axis_index("ep").reshape(1)
    me = lax.axis_index("fsdp").reshape(1)
    units = gate_weight.shape[2]
    two = 2 * slots
    plan = [[(part, step) for part in range(2)] for step in range(4)]
    plan += [[(part, step), (part, step + 1)] for part in range(2) for step in (4, 6)]
    own, core, even1, odd1, token2, token3, grad2, grad3, mask, weights = pick_slots(
        ep_index, chosen, counts.reshape(1, experts), gate_prob, tokens, cotangent, plan
    )

    token2 = swap(token2, 4, "ep")
    token3 = swap(token3, 6, "ep")
    even1 = swap(even1, 2, "ep")
    odd1 = swap(odd1, 3, "ep")
    core = swap(core, 1, "ep")
    gate = load_weight(me, gate_weight[0], True, count, (own,))
    near = joined(arrange((own,), [[(0, 0, two)]], (gate,)), core, even1, odd1)
    mixed = gathered(near, 1, 2)
    odd = swap(joined(token2[slots:], token3[slots:], token2, token3), 1, "ep")
    ends = [(0, 0, slots), (2, 0, slots), (1, 0, slots), (2, slots, slots)]
    up = load_weight(me, up_weight[0], True, count, (near,))
    far = arrange((token2, token3, odd), [ends], (mixed[1][0], mixed[2][0], up))
    far_tokens = gathered(far, 2, 1)
    grad2 = swap(grad2, 4, "ep")
    grad3 = swap(grad3, 6, "ep")
    down = load_weight(me, down_weight[0], False, count, (up,))
    weighted, plain = spread_matrices(mask, weights, (down,))
    odd = arrange(
        (grad2, grad3),
        [[(0, slots, slots), (1, slots, slots), (0, 0, two), (1, 0, two)]],
    )
    odd = swap(odd, 1, "ep")
    far_grads = gathered(arrange((grad2, grad3, odd), [ends]), 2, 1)
    picked = pieces_of(mixed, far_tokens)
    grads = pieces_of(mixed, far_grads)
    first = Slices(picked[:3], 0, slots)
    last = Slices(picked[3:], 0, slots)

    sums = partial_products(first, (gate, up), (PLAIN, PLAIN), units)
    (hidden, slope, silu), terms = forward_terms(last, sums, gate, up, down)
    bottom = swap(terms[3][1], 1, "fsdp")
    top = swap(terms[3][0], 2, "fsdp")

    first = Slices(grads[:3], 1, slots)
    last = Slices(grads[3:], 1, slots)
    (grad_sum,) = [partial_products(first, (down,), (LAST,), units, (hidden,))]
    sum_x, sum_y = merge(terms[1], terms[2], top, bottom, (grad_sum,))
    (gate_grad, up_grad), back_d = backward_terms(
        last, grad_sum, slope, silu, gate, up, down, (sum_x,)
    )
    sum_x = swap(sum_x, 1, "fsdp")
    sum_y = swap(sum_y, 2, "fsdp")
    bottom = swap(back_d[1], 1, "fsdp")
    top = swap(back_d[0], 2, "fsdp")
    back = backward_rest(gate_grad, up_grad, gate, up)
    out0, out1, out2, out3 = add_up([joined(*terms[0]), sum_x, sum_y], 4, (back[0][0],))
    out3 = swap(out3, 6, "ep")
    out2 = swap(out2, 4, "ep")
    out1 = swap(out1, 2, "ep")

    back_x, back_y = merge(back[1], back[2], top, bottom, (out0,))
    grad_down, mark = down_grads(me, hidden, Slices(grads, 1, slots), (back_x,))
    back_x = swap(back_x, 1, "fsdp")
    back_y = swap(back_y, 2, "fsdp")
    layout = []
    for step in range(experts // 2):
        layout += [(step, 0), (experts // 2, step)]
    outs = [out0, out1, out2, out3]
    outs.append(swap(joined(*[piece[slots:] for piece in outs]), 1, "ep"))
    back0, back1, back2, back3 = add_up([joined(*back[0]), back_x, back_y], 4, (outs[-1], mark))
    back3 = swap(back3, 6, "ep")
    back2 = swap(back2, 4, "ep")
    back1 = swap(back1, 2, "ep")
    grad_gate, grad_up, mark = weight_grads(
        me, Slices(picked, 0, slots), gate_grad, up_grad, (back0,)
    )
    mixture = spread_rows(weighted, outs, layout, slots)
    backs = [back0, back1, back2, back3]
    other = arrange(backs, [[(piece, slots, slots) for piece in range(4)]], (mark,))
    backs.append(swap(other, 1, "ep"))
    grad_tokens = spread_rows(plain, backs, layout, slots)
    return mixture, grad_tokens, grad_gate[None], grad_up[None], grad_down[None]


def solution(mesh):
    placed = (
        P("ep", "fsdp"),
        P("ep", "fsdp"),
        P("ep", None, "fsdp"),
        P("ep", None, "fsdp"),
        P("ep", "fsdp", None),
        P(None, "ep", None),
        P(None, "ep"),
        P(None, "ep", None),
    )

    def per_part(*arrays):
        fits = mesh.shape["fsdp"] == 4 and mesh.shape["ep"] == 8 and arrays[0].shape[1] % 128 == 0
        return (by_links if fits else by_collectives)(*arrays)

    return jax.shard_map(
        per_part,
        mesh=mesh,
        in_specs=placed,
        out_specs=(
            P("ep", "fsdp"),
            P("ep", "fsdp"),
            P("ep", None, "fsdp"),
            P("ep", None, "fsdp"),
            P("ep", "fsdp", None),
        ),
        check_vma=False,
    )
```

```python
import functools

import jax
import jax.numpy as jnp
from jax import lax
from jax.experimental import pallas as pl
from jax.experimental.pallas import tpu as pltpu
from jax.sharding import PartitionSpec as P

ROWS = (((0,), (0,)), ((), ()))
PLAIN = (((1,), (0,)), ((), ()))
LAST = (((1,), (1,)), ((), ()))
IN_VMEM = pl.BlockSpec(memory_space=pltpu.VMEM)
IN_SMEM = pl.BlockSpec(memory_space=pltpu.SMEM)
ANYWHERE = pl.BlockSpec(memory_space=pl.ANY)
MIB = 1024 * 1024


def run_kernel(body, name, operands, specs, outs, out_specs, scratch, mib, later=(), mark=False, aliases=None):
    used = len(operands)
    outs, out_specs = list(outs), list(out_specs)
    results = len(outs)
    if mark:
        outs.append(jax.ShapeDtypeStruct((8, 128), jnp.float32))
        out_specs.append(IN_VMEM)

    def run(*refs):
        refs = list(refs[len(later) :])
        if mark:
            mark_ref = refs.pop(used + results)
            mark_ref[...] = jnp.zeros_like(mark_ref)
        body(*refs)

    out = pl.pallas_call(
        run,
        name=name,
        in_specs=[*[ANYWHERE] * len(later), *specs],
        out_shape=outs,
        out_specs=out_specs,
        scratch_shapes=scratch,
        input_output_aliases={len(later) + i: o for i, o in (aliases or {}).items()},
        compiler_params=pltpu.CompilerParams(vmem_limit_bytes=mib * MIB),
        cost_estimate=pl.CostEstimate(flops=1024, bytes_accessed=1024, transcendentals=0),
    )(*later, *operands)
    return out if len(out) > 1 else out[0]


def in_hbm(array):
    return pltpu.with_memory_space_constraint(array, pltpu.HBM)


def like(rows, width, kind=jnp.bfloat16):
    return jax.ShapeDtypeStruct((rows, width), kind)


def slot_columns(me, chosen_ref, counts_ref, prob_ref):
    experts, _, slots = chosen_ref.shape
    diagonal = lax.broadcasted_iota(jnp.int32, (slots, slots), 0) == lax.broadcasted_iota(
        jnp.int32, (slots, slots), 1
    )
    position = lax.broadcasted_iota(jnp.int32, (slots, 1), 0)
    rows, weights = [], []
    for step in range(experts):
        expert = me ^ step
        live = position < counts_ref[0, expert]
        row = jnp.broadcast_to(chosen_ref[expert].astype(jnp.float32), (slots, slots))
        row = jnp.sum(jnp.where(diagonal, row, 0.0), axis=1, keepdims=True)
        prob = jnp.broadcast_to(prob_ref[expert], (slots, slots))
        prob = jnp.sum(jnp.where(diagonal, prob, 0.0), axis=1, keepdims=True)
        rows.append(jnp.where(live, row, -1.0))
        weights.append(jnp.where(live, prob, 0.0))
    return jnp.concatenate(rows, axis=0), jnp.concatenate(weights, axis=0)


def pick_body(plan, me_ref, counts_hbm, chosen_hbm, prob_hbm, tokens_hbm, cotangent_hbm, *refs):
    *outs, mask_ref, weights_ref = refs[:-6]
    counts_ref, chosen_ref, prob_ref, tokens_ref, cotangent_ref, sems = refs[-6:]
    experts, _, slots = chosen_ref.shape
    pairs = (
        (counts_hbm, counts_ref),
        (chosen_hbm, chosen_ref),
        (prob_hbm, prob_ref),
        (tokens_hbm, tokens_ref),
        (cotangent_hbm, cotangent_ref),
    )
    copies = [pltpu.make_async_copy(*pair, sems.at[index]) for index, pair in enumerate(pairs)]
    for copy in copies:
        copy.start()
    for copy in copies[:3]:
        copy.wait()
    rows, weights = slot_columns(me_ref[0], chosen_ref, counts_ref, prob_ref)
    length = tokens_ref.shape[0]
    place = lax.broadcasted_iota(jnp.int32, (rows.shape[0], length), 1).astype(jnp.float32)
    mask = (place == rows).astype(jnp.bfloat16)
    mask_ref[...] = mask
    weights_ref[...] = jnp.broadcast_to(weights, weights_ref.shape)
    for which, source_ref in enumerate((tokens_ref, cotangent_ref)):
        copies[3 + which].wait()
        value = jnp.dot(mask, source_ref[...], preferred_element_type=jnp.float32)
        if which:
            value = weights * value
        value = value.astype(jnp.bfloat16)
        for out_ref, blocks in zip(outs, plan):
            for place, (part, step) in enumerate(blocks):
                if part == which:
                    target = pl.ds(place * slots, slots)
                    out_ref[target, :] = value[step * slots : (step + 1) * slots]


def pick_slots(me, chosen, counts, gate_prob, tokens, cotangent, plan):
    experts, _, slots = chosen.shape
    length, width = tokens.shape
    total = experts * slots
    operands = (counts, chosen, gate_prob, tokens, cotangent)
    return run_kernel(
        functools.partial(pick_body, plan),
        "pick_slots",
        (me, *[in_hbm(array) for array in operands]),
        [IN_SMEM] + [ANYWHERE] * 5,
        [like(slots * len(blocks), width) for blocks in plan]
        + [like(total, length), like(total, 128, jnp.float32)],
        [IN_VMEM] * (len(plan) + 2),
        [pltpu.SMEM(counts.shape, counts.dtype)]
        + [pltpu.VMEM(array.shape, array.dtype) for array in operands[1:]]
        + [pltpu.SemaphoreType.DMA((5,))],
        16,
    )


def spread_matrix_body(mask_ref, weights_ref, weighted_ref, plain_ref):
    mask = mask_ref[...].astype(jnp.float32)
    weights = weights_ref[...][:, :1]
    high = weights.astype(jnp.bfloat16).astype(jnp.float32)
    count = mask.shape[0]
    plain_ref[...] = mask.T.astype(jnp.bfloat16)
    weighted_ref[:, :count] = (mask * high).T.astype(jnp.bfloat16)
    weighted_ref[:, count:] = (mask * (weights - high)).T.astype(jnp.bfloat16)


def spread_matrices(mask, weights, later=()):
    count, length = mask.shape
    return run_kernel(
        spread_matrix_body,
        "spread_matrices",
        (mask, weights),
        [IN_VMEM] * 2,
        [like(length, 2 * count), like(length, count)],
        [IN_VMEM] * 2,
        [],
        8,
        later,
    )


def spread_body(layout, slots, spread_ref, *refs):
    pieces, (out_hbm, block, sems) = refs[:-3], refs[-3:]
    values = jnp.concatenate([pieces[p][pl.ds(q * slots, slots), :] for p, q in layout], axis=0)
    if spread_ref.shape[1] > values.shape[0]:
        values = jnp.concatenate([values, values], axis=0)
    parts = sems.shape[0]
    size = block.shape[0] // parts
    copies = []
    for part in range(parts):
        rows = pl.ds(part * size, size)
        total = jnp.dot(spread_ref[rows, :], values, preferred_element_type=jnp.float32)
        block[rows, :] = total.astype(jnp.bfloat16)
        copies.append(pltpu.make_async_copy(block.at[rows], out_hbm.at[rows], sems.at[part]))
        copies[-1].start()
    for copy in copies:
        copy.wait()


def spread_rows(spread, pieces, layout, slots, later=(), mark=False, parts=4):
    length, width = spread.shape[0], pieces[0].shape[1]
    return run_kernel(
        functools.partial(spread_body, layout, slots),
        "spread_rows",
        (spread, *pieces),
        [IN_VMEM] * (1 + len(pieces)),
        [like(length, width)],
        [ANYWHERE],
        [pltpu.VMEM((length, width), jnp.bfloat16), pltpu.SemaphoreType.DMA((parts,))],
        16,
        later,
        mark,
    )


def load_body(by_rows, count, me_ref, source_ref, target_ref, sems):
    width = target_ref.shape[1 if by_rows else 2]
    copies = []
    for index in range(count):
        part = pl.ds(pl.multiple_of((me_ref[0] ^ index) * width, width), width)
        source = source_ref.at[part, :] if by_rows else source_ref.at[:, part]
        copies.append(pltpu.make_async_copy(source, target_ref.at[index], sems.at[index]))
        copies[-1].start()
    for copy in copies:
        copy.wait()


def load_weight(me, weight, by_rows, count, later=()):
    first, second = weight.shape
    shape = (count, first // count, second) if by_rows else (count, first, second // count)
    return run_kernel(
        functools.partial(load_body, by_rows, count),
        "load_weight",
        (me, in_hbm(weight)),
        [IN_SMEM, ANYWHERE],
        [jax.ShapeDtypeStruct(shape, weight.dtype)],
        [IN_VMEM],
        [pltpu.SemaphoreType.DMA((count,))],
        4,
        later,
    )


def arrange_body(plan, used, *refs):
    for rows, out_ref in zip(plan, refs[used:]):
        start = 0
        for source, first, size in rows:
            out_ref[pl.ds(start, size), :] = refs[source][pl.ds(first, size), :]
            start += size


def arrange(sources, plan, later=()):
    width = sources[0].shape[1]
    sizes = [sum(size for _, _, size in rows) for rows in plan]
    return run_kernel(
        functools.partial(arrange_body, plan, len(sources)),
        "arrange",
        tuple(sources),
        [IN_VMEM] * len(sources),
        [like(size, width) for size in sizes],
        [IN_VMEM] * len(plan),
        [],
        8,
        later,
    )


def add_body(used, *refs):
    total = refs[0][...].astype(jnp.float32)
    for ref in refs[1:used]:
        total += ref[...].astype(jnp.float32)
    start = 0
    for out_ref in refs[used:]:
        out_ref[...] = total[start : start + out_ref.shape[0]].astype(out_ref.dtype)
        start += out_ref.shape[0]


def add_up(terms, parts=1, later=()):
    rows, width = terms[0].shape
    return run_kernel(
        functools.partial(add_body, len(terms)),
        "add_up",
        tuple(terms),
        [IN_VMEM] * len(terms),
        [like(rows // parts, width)] * parts,
        [IN_VMEM] * parts,
        [],
        8,
        later,
    )


def add_pairs_body(*refs):
    for first_ref, second_ref, out_ref in zip(refs[0:4:2], refs[1:4:2], refs[4:]):
        total = first_ref[...].astype(jnp.float32) + second_ref[...].astype(jnp.float32)
        out_ref[...] = total.astype(out_ref.dtype)


def add_pairs(first, second, later=()):
    return run_kernel(
        add_pairs_body,
        "add_pairs",
        (*first, *second),
        [IN_VMEM] * 4,
        [like(*first[0].shape), like(*second[0].shape)],
        [IN_VMEM] * 2,
        [],
        8,
        later,
    )


class Slices:
    def __init__(self, slices, part, slots):
        self.mixed = [[mixed for _, mixed in pieces] for pieces in slices]
        self.flat = [array for pieces in slices for array, _ in pieces]
        self.part, self.slots = part, slots
        self.count, self.width = len(slices), self.flat[0].shape[1]
        self.rows = sum(array.shape[0] // (2 if mixed else 1) for array, mixed in slices[0])

    def read(self, refs, index):
        first = sum(len(mixed) for mixed in self.mixed[:index])
        blocks = []
        for place, mixed in enumerate(self.mixed[index]):
            ref = refs[first + place]
            if mixed:
                for start in range(self.part * self.slots, ref.shape[0], 2 * self.slots):
                    blocks.append(ref[pl.ds(start, self.slots), :])
            else:
                blocks.append(ref[...])
        return blocks[0] if len(blocks) == 1 else jnp.concatenate(blocks, axis=0)


def partial_body(slices, dims, *refs):
    used = len(slices.flat)
    weights, sums = refs[used:][: len(dims)], refs[used + len(dims) :]
    for index in range(slices.count):
        rows = slices.read(refs, index)
        for weight_ref, dim, sum_ref in zip(weights, dims, sums):
            value = lax.dot_general(
                rows, weight_ref[index], dim, preferred_element_type=jnp.float32
            )
            if index == 0:
                sum_ref[...] = value
            else:
                sum_ref[...] += value


def partial_products(slices, weights, dims, units, later=()):
    return run_kernel(
        functools.partial(partial_body, slices, dims),
        "partial_products",
        (*slices.flat, *weights),
        [IN_VMEM] * (len(slices.flat) + len(weights)),
        [like(slices.rows, units, jnp.float32)] * len(weights),
        [IN_VMEM] * len(weights),
        [],
        8,
        later,
    )


def store_term(refs, index, term):
    term = term.astype(jnp.bfloat16)
    size = term.shape[0] // 2
    refs[2 * index][...] = term[:size]
    refs[2 * index + 1][...] = term[size:]


def forward_body(slices, *refs):
    used = len(slices.flat)
    gate_sum, up_sum, gate_ref, up_ref, down_ref = refs[used : used + 5]
    hidden_ref, slope_ref, silu_ref, *terms = refs[used + 5 :]
    last = gate_ref.shape[0] - 1
    rows = slices.read(refs, 0)
    gate = gate_sum[...] + jnp.dot(rows, gate_ref[last], preferred_element_type=jnp.float32)
    up = up_sum[...] + jnp.dot(rows, up_ref[last], preferred_element_type=jnp.float32)
    sigmoid = jax.nn.sigmoid(gate)
    silu = gate * sigmoid
    hidden = (silu * up).astype(jnp.bfloat16)
    hidden_ref[...] = hidden
    slope_ref[...] = up * sigmoid * (1.0 + gate * (1.0 - sigmoid))
    silu_ref[...] = silu
    for index in reversed(range(last + 1)):
        term = jnp.dot(hidden, down_ref[index], preferred_element_type=jnp.float32)
        store_term(terms, index, term)


def forward_terms(slices, sums, gate, up, down, later=()):
    count, width, units = gate.shape
    rows = sums[0].shape[0]
    f32 = jnp.float32
    out = run_kernel(
        functools.partial(forward_body, slices),
        "forward_terms",
        (*slices.flat, *sums, gate, up, down),
        [IN_VMEM] * (len(slices.flat) + 5),
        [like(rows, units), like(rows, units, f32), like(rows, units, f32)]
        + [like(rows // 2, width)] * (2 * count),
        [IN_VMEM] * (3 + 2 * count),
        [],
        8,
        later,
    )
    return out[:3], [out[3 + 2 * i : 5 + 2 * i] for i in range(count)]


def backward_body(slices, *refs):
    used = len(slices.flat)
    grad_sum, slope_ref, silu_ref, gate_ref, up_ref, down_ref = refs[used : used + 6]
    gate_grad_ref, up_grad_ref, *terms = refs[used + 6 :]
    last = gate_ref.shape[0] - 1
    rows = slices.read(refs, 0)
    grad = lax.dot_general(rows, down_ref[last], LAST, preferred_element_type=jnp.float32)
    grad += grad_sum[...]
    gate_grad = (grad * slope_ref[...]).astype(jnp.bfloat16)
    up_grad = (grad * silu_ref[...]).astype(jnp.bfloat16)
    gate_grad_ref[...] = gate_grad
    up_grad_ref[...] = up_grad
    store_term(terms, 0, back_term(gate_grad, up_grad, gate_ref, up_ref, last))


def back_term(gate_grad, up_grad, gate_ref, up_ref, index):
    term = lax.dot_general(gate_grad, gate_ref[index], LAST, preferred_element_type=jnp.float32)
    return term + lax.dot_general(up_grad, up_ref[index], LAST, preferred_element_type=jnp.float32)


def backward_rest_body(gate_grad_ref, up_grad_ref, gate_ref, up_ref, *terms):
    for index in reversed(range(len(terms) // 2)):
        term = back_term(gate_grad_ref[...], up_grad_ref[...], gate_ref, up_ref, index)
        store_term(terms, index, term)


def backward_rest(gate_grad, up_grad, gate, up, later=()):
    count, width, _ = gate.shape
    rows = gate_grad.shape[0]
    out = run_kernel(
        backward_rest_body,
        "backward_rest",
        (gate_grad, up_grad, gate, up),
        [IN_VMEM] * 4,
        [like(rows // 2, width)] * (2 * count - 2),
        [IN_VMEM] * (2 * count - 2),
        [],
        8,
        later,
    )
    return [out[2 * i : 2 * i + 2] for i in range(count - 1)]


def backward_terms(slices, grad_sum, slope, silu, gate, up, down, later=()):
    _, width, units = gate.shape
    rows = slope.shape[0]
    out = run_kernel(
        functools.partial(backward_body, slices),
        "backward_terms",
        (*slices.flat, grad_sum, slope, silu, gate, up, down),
        [IN_VMEM] * (len(slices.flat) + 6),
        [like(rows, units)] * 2 + [like(rows // 2, width)] * 2,
        [IN_VMEM] * 4,
        [],
        8,
        later,
    )
    return out[:2], out[2:]


def merge_body(first_top, first_bottom, second_top, second_bottom, top, bottom, first, second):
    size = top.shape[0]
    upper, lower = pl.ds(0, size), pl.ds(size, size)
    total = first_top[...].astype(jnp.float32) + top[...].astype(jnp.float32)
    first[upper, :] = total.astype(first.dtype)
    first[lower, :] = first_bottom[...]
    total = second_bottom[...].astype(jnp.float32) + bottom[...].astype(jnp.float32)
    second[lower, :] = total.astype(second.dtype)
    second[upper, :] = second_top[...]


def merge(first, second, top, bottom, later=()):
    rows, width = first[0].shape
    return run_kernel(
        merge_body,
        "merge",
        (*first, *second, top, bottom),
        [IN_VMEM] * 6,
        [like(2 * rows, width)] * 2,
        [IN_VMEM] * 2,
        [],
        8,
        later,
    )


def down_grad_body(slices, start, filled, me_ref, hidden_ref, *refs):
    out_ref, block, sems = refs[-3:]
    _, _, width = block.shape
    hidden = hidden_ref[...]
    copies = []
    for index in range(slices.count):
        block[index] = lax.dot_general(
            hidden, slices.read(refs[filled:], index), ROWS, preferred_element_type=jnp.float32
        ).astype(jnp.bfloat16)
        first = pl.multiple_of((me_ref[0] ^ (start + index)) * width, width)
        target = out_ref.at[:, pl.ds(first, width)]
        copies.append(pltpu.make_async_copy(block.at[index], target, sems.at[index]))
        copies[-1].start()
    for copy in copies:
        copy.wait()


def down_grads(me, hidden, slices, start, total, filled=(), later=()):
    width, units = slices.width, hidden.shape[1]
    return run_kernel(
        functools.partial(down_grad_body, slices, start, len(filled)),
        "down_grads",
        (me, hidden, *filled, *slices.flat),
        [IN_SMEM, IN_VMEM] + [ANYWHERE] * len(filled) + [IN_VMEM] * len(slices.flat),
        [like(units, width * total)],
        [ANYWHERE],
        [
            pltpu.VMEM((slices.count, units, width), jnp.bfloat16),
            pltpu.SemaphoreType.DMA((slices.count,)),
        ],
        16,
        later,
        True,
        {2: 0} if filled else None,
    )


def weight_grad_body(slices, me_ref, *refs):
    grad_refs, (gate_hbm, up_hbm, block, sems) = refs[:2], refs[-4:]
    _, count, width, units = block.shape
    grads = jnp.concatenate([ref[...] for ref in grad_refs], axis=1)
    copies = []
    for index in range(count):
        rows = slices.read(refs[2:], index)
        start = pl.multiple_of((me_ref[0] ^ index) * width, width)
        both = lax.dot_general(rows, grads, ROWS, preferred_element_type=jnp.float32)
        both = both.astype(jnp.bfloat16)
        for which, out_ref in enumerate((gate_hbm, up_hbm)):
            block[which, index] = both[:, which * units : (which + 1) * units]
            target = out_ref.at[pl.ds(start, width), :]
            sem = sems.at[2 * index + which]
            copies.append(pltpu.make_async_copy(block.at[which, index], target, sem))
            copies[-1].start()
    for copy in copies:
        copy.wait()


def weight_grads(me, slices, gate_grad, up_grad, later=()):
    count, width, units = slices.count, slices.width, gate_grad.shape[1]
    return run_kernel(
        functools.partial(weight_grad_body, slices),
        "weight_grads",
        (me, gate_grad, up_grad, *slices.flat),
        [IN_SMEM] + [IN_VMEM] * (2 + len(slices.flat)),
        [like(width * count, units)] * 2,
        [ANYWHERE] * 2,
        [
            pltpu.VMEM((2, count, width, units), jnp.bfloat16),
            pltpu.SemaphoreType.DMA((2 * count,)),
        ],
        20,
        later,
        True,
    )


def pick_rows(tokens, cotangent, row_index, live_mask, weight):
    flat_rows = row_index.reshape(-1)
    keep_rows = live_mask.reshape(-1)[:, None]
    taken_tokens = jnp.take(tokens, flat_rows, axis=0)
    picked_tokens = jnp.where(keep_rows, taken_tokens, jnp.zeros_like(taken_tokens))
    taken_grads = jnp.take(cotangent, flat_rows, axis=0).astype(jnp.float32)
    picked_grads = (weight.reshape(-1)[:, None] * taken_grads).astype(jnp.bfloat16)
    shaped = row_index.shape + (tokens.shape[1],)
    return (picked_tokens.reshape(shaped), picked_grads.reshape(shaped))


def to_slots(summed, experts, slot_count):
    return summed.astype(jnp.bfloat16).reshape(experts, slot_count, summed.shape[1])


def send_back(term, experts, slot_count):
    summed = lax.psum_scatter(
        term.astype(jnp.bfloat16), "fsdp", scatter_dimension=1, tiled=True
    ).astype(jnp.float32)
    return lax.all_to_all(
        to_slots(summed, experts, slot_count), "ep", split_axis=0, concat_axis=0, tiled=True
    )


def by_collectives(tokens, cotangent, gate_weight, up_weight, down_weight, chosen, counts, gate_prob):
    experts = chosen.shape[0]
    slot_count = chosen.shape[2]
    features = tokens.shape[1]
    row_index = chosen[:, 0, :]
    position = lax.broadcasted_iota(jnp.int32, (experts, slot_count), 1)
    live_mask = position < counts
    weight = jnp.where(live_mask, gate_prob[:, 0, :], 0.0)
    picked_tokens, picked_grads = pick_rows(tokens, cotangent, row_index, live_mask, weight)
    sliced_tokens, sliced_grads = (
        lax.all_to_all(picked_tokens, "ep", split_axis=0, concat_axis=0, tiled=True),
        lax.all_to_all(picked_grads, "ep", split_axis=0, concat_axis=0, tiled=True),
    )
    rows_tokens, rows_grads = (
        lax.all_gather(sliced_tokens, "fsdp", axis=2, tiled=True),
        lax.all_gather(sliced_grads, "fsdp", axis=2, tiled=True),
    )
    full_width = rows_tokens.shape[2]
    total_rows = rows_tokens.shape[0] * slot_count
    rows_tokens = rows_tokens.reshape(total_rows, full_width)
    rows_grads = rows_grads.reshape(total_rows, full_width)
    gate_local = gate_weight[0]
    up_local = up_weight[0]
    down_local = down_weight[0]
    pre_gate = jnp.dot(rows_tokens, gate_local, preferred_element_type=jnp.float32)
    pre_up = jnp.dot(rows_tokens, up_local, preferred_element_type=jnp.float32)
    sigmoid_gate = jax.nn.sigmoid(pre_gate)
    activated = pre_gate * sigmoid_gate
    hidden = (activated * pre_up).astype(jnp.bfloat16)
    output_term = jnp.dot(hidden, down_local, preferred_element_type=jnp.float32)
    output_back = send_back(output_term, experts, slot_count)
    contract_rows = (((0,), (0,)), ((), ()))
    contract_last = (((1,), (1,)), ((), ()))
    grad_hidden = lax.dot_general(
        rows_grads, down_local, contract_last, preferred_element_type=jnp.float32
    )
    grad_pre_gate = (
        grad_hidden * pre_up * sigmoid_gate * (1.0 + pre_gate * (1.0 - sigmoid_gate))
    ).astype(jnp.bfloat16)
    grad_pre_up = (grad_hidden * activated).astype(jnp.bfloat16)
    grad_down = lax.dot_general(
        hidden, rows_grads, contract_rows, preferred_element_type=jnp.float32
    ).astype(jnp.bfloat16)
    grad_gate = lax.dot_general(
        rows_tokens, grad_pre_gate, contract_rows, preferred_element_type=jnp.float32
    ).astype(jnp.bfloat16)
    grad_up = lax.dot_general(
        rows_tokens, grad_pre_up, contract_rows, preferred_element_type=jnp.float32
    ).astype(jnp.bfloat16)
    grad_term = lax.dot_general(
        grad_pre_gate, gate_local, contract_last, preferred_element_type=jnp.float32
    )
    grad_term = grad_term + lax.dot_general(
        grad_pre_up, up_local, contract_last, preferred_element_type=jnp.float32
    )
    grad_back = send_back(grad_term, experts, slot_count)
    flat_rows = row_index.reshape(-1)
    output_rows = output_back.reshape(-1, features).astype(jnp.float32)
    mixture = (
        jnp.zeros((tokens.shape[0], features), jnp.float32)
        .at[flat_rows]
        .add(weight.reshape(-1)[:, None] * output_rows)
    )
    grad_rows = jnp.where(
        live_mask.reshape(-1)[:, None], grad_back.reshape(-1, features).astype(jnp.float32), 0.0
    )
    grad_tokens = jnp.zeros((tokens.shape[0], features), jnp.float32).at[flat_rows].add(grad_rows)
    return (
        mixture.astype(jnp.bfloat16),
        grad_tokens.astype(jnp.bfloat16),
        grad_gate[None],
        grad_up[None],
        grad_down[None],
    )


def swap(array, distance, axis):
    size = lax.axis_size(axis)
    return lax.ppermute(array, axis, [(i, i ^ distance) for i in range(size)])


def joined(*arrays):
    return jnp.concatenate(arrays, axis=0)


def gathered(whole, first, second):
    from_first = swap(whole, first, "fsdp")
    from_second = swap(whole, second, "fsdp")
    passed = arrange((from_first,), [[(0, 0, whole.shape[0])]], (from_second,))
    slices = [[whole], [None], [None], [swap(passed, second, "fsdp")]]
    slices[first], slices[second] = [from_first], [from_second]
    return slices


def pieces_of(mixed, plain):
    return [
        [(piece, True) for piece in some] + [(piece, False) for piece in others]
        for some, others in zip(mixed, plain)
    ]


def by_links(tokens, cotangent, gate_weight, up_weight, down_weight, chosen, counts, gate_prob):
    experts, _, slots = chosen.shape
    count = lax.axis_size("fsdp")
    ep_index = lax.axis_index("ep").reshape(1)
    me = lax.axis_index("fsdp").reshape(1)
    units = gate_weight.shape[2]
    two = 2 * slots
    plan = [[(part, step) for part in range(2)] for step in range(4)]
    plan += [[(part, step), (part, step + 1)] for part in range(2) for step in (4, 6)]
    own, core, even1, odd1, token2, token3, grad2, grad3, mask, weights = pick_slots(
        ep_index, chosen, counts.reshape(1, experts), gate_prob, tokens, cotangent, plan
    )

    token2 = swap(token2, 4, "ep")
    token3 = swap(token3, 6, "ep")
    even1 = swap(even1, 2, "ep")
    odd1 = swap(odd1, 3, "ep")
    core = swap(core, 1, "ep")
    gate = load_weight(me, gate_weight[0], True, count, (own,))
    near = joined(arrange((own,), [[(0, 0, two)]], (gate,)), core, even1, odd1)
    near_x = swap(near, 1, "fsdp")
    near_y = swap(near, 2, "fsdp")
    odd = swap(joined(token2[slots:], token3[slots:], token2, token3), 1, "ep")
    ends = [(0, 0, slots), (2, 0, slots), (1, 0, slots), (2, slots, slots)]
    up = load_weight(me, up_weight[0], True, count, (near,))
    far = arrange((token2, token3, odd), [ends], (near_x, near_y, up))
    far_tokens = gathered(far, 2, 1)
    grad2 = swap(grad2, 4, "ep")
    grad3 = swap(grad3, 6, "ep")
    down = load_weight(me, down_weight[0], False, count, (up,))
    weighted, plain = spread_matrices(mask, weights, (down,))
    odd = arrange(
        (grad2, grad3),
        [[(0, slots, slots), (1, slots, slots), (0, 0, two), (1, 0, two)]],
    )
    odd = swap(odd, 1, "ep")
    far_grads = gathered(arrange((grad2, grad3, odd), [ends]), 1, 2)
    halves = [[(0, first, slots) for first in range(part * slots, 4 * two, two)] for part in range(2)]
    near_d = swap(arrange((near_x,), halves[:1]), 2, "fsdp")
    near_grad_d = swap(arrange((near_y,), halves[1:]), 1, "fsdp")
    mixed = [[near], [near_x], [near_y], []]
    picked = pieces_of(mixed, far_tokens)
    grads = pieces_of(mixed, far_grads)
    picked[3].insert(0, (near_d, False))
    grads[3].insert(0, (near_grad_d, False))
    first = Slices(picked[:3], 0, slots)
    last = Slices(picked[3:], 0, slots)

    sums = partial_products(first, (gate, up), (PLAIN, PLAIN), units)
    (hidden, slope, silu), terms = forward_terms(last, sums, gate, up, down)
    bottom = swap(terms[3][1], 1, "fsdp")
    top = swap(terms[3][0], 2, "fsdp")

    first = Slices(grads[:3], 1, slots)
    last = Slices(grads[3:], 1, slots)
    (grad_sum,) = [partial_products(first, (down,), (LAST,), units, (hidden,))]
    grad_down, mark = down_grads(me, hidden, first, 0, count, (), (grad_sum,))
    sum_x, sum_y = merge(terms[1], terms[2], top, bottom, (mark,))
    (gate_grad, up_grad), back_d = backward_terms(
        last, grad_sum, slope, silu, gate, up, down, (sum_x,)
    )
    sum_x = swap(sum_x, 1, "fsdp")
    sum_y = swap(sum_y, 2, "fsdp")
    bottom = swap(back_d[1], 1, "fsdp")
    top = swap(back_d[0], 2, "fsdp")
    back = backward_rest(gate_grad, up_grad, gate, up)
    out0, out1, out2, out3 = add_up([joined(*terms[0]), sum_x, sum_y], 4, (back[0][0],))
    out3 = swap(out3, 6, "ep")
    out2 = swap(out2, 4, "ep")
    out1 = swap(out1, 2, "ep")

    y_far, x_near = add_pairs((back[2][1], bottom), (back[1][0], top), (out0,))
    x_far = swap(back[1][1], 1, "fsdp")
    y_far = swap(y_far, 2, "fsdp")
    x_near = swap(x_near, 1, "fsdp")
    y_near = swap(back[2][0], 2, "fsdp")
    layout = []
    for step in range(experts // 2):
        layout += [(step, 0), (experts // 2, step)]
    outs = [out0, out1, out2, out3]
    outs.append(swap(joined(*[piece[slots:] for piece in outs]), 1, "ep"))
    back2, back3 = add_up([back[0][1], x_far, y_far], 2, (outs[-1],))
    last = Slices(grads[3:], 1, slots)
    grad_down, mark = down_grads(me, hidden, last, count - 1, count, (grad_down,), (back2,))
    back0, back1 = add_up([back[0][0], x_near, y_near], 2, (mark,))
    back3 = swap(back3, 6, "ep")
    back2 = swap(back2, 4, "ep")
    back1 = swap(back1, 2, "ep")
    grad_gate, grad_up, mark = weight_grads(
        me, Slices(picked, 0, slots), gate_grad, up_grad, (back0,)
    )
    mixture = spread_rows(weighted, outs, layout, slots)
    backs = [back0, back1, back2, back3]
    far_odd = [[(0, slots, slots), (1, slots, slots), (0, 0, two)]]
    backs.append(swap(arrange((back2, back3), far_odd, (mark,)), 1, "ep"))
    backs.append(swap(arrange((back0, back1), [far_odd[0][:2]], (mark,)), 1, "ep"))
    layout = [(0, 0), (5, 0), (1, 0), (5, 1), (2, 0), (4, 0), (3, 0), (4, 1)]
    grad_tokens = spread_rows(plain, backs, layout, slots)
    return mixture, grad_tokens, grad_gate[None], grad_up[None], grad_down[None]


def solution(mesh):
    placed = (
        P("ep", "fsdp"),
        P("ep", "fsdp"),
        P("ep", None, "fsdp"),
        P("ep", None, "fsdp"),
        P("ep", "fsdp", None),
        P(None, "ep", None),
        P(None, "ep"),
        P(None, "ep", None),
    )

    def per_part(*arrays):
        fits = mesh.shape["fsdp"] == 4 and mesh.shape["ep"] == 8 and arrays[0].shape[1] % 128 == 0
        return (by_links if fits else by_collectives)(*arrays)

    return jax.shard_map(
        per_part,
        mesh=mesh,
        in_specs=placed,
        out_specs=(
            P("ep", "fsdp"),
            P("ep", "fsdp"),
            P("ep", None, "fsdp"),
            P("ep", None, "fsdp"),
            P("ep", "fsdp", None),
        ),
        check_vma=False,
    )
```

```python
import functools

import jax
import jax.numpy as jnp
from jax import lax
from jax.experimental import pallas as pl
from jax.experimental.pallas import tpu as pltpu
from jax.sharding import PartitionSpec as P

ROWS = (((0,), (0,)), ((), ()))
PLAIN = (((1,), (0,)), ((), ()))
LAST = (((1,), (1,)), ((), ()))
IN_VMEM = pl.BlockSpec(memory_space=pltpu.VMEM)
IN_SMEM = pl.BlockSpec(memory_space=pltpu.SMEM)
ANYWHERE = pl.BlockSpec(memory_space=pl.ANY)
MIB = 1024 * 1024


def run_kernel(body, name, operands, specs, outs, out_specs, scratch, mib, later=(), mark=False, aliases=None):
    used = len(operands)
    outs, out_specs = list(outs), list(out_specs)
    results = len(outs)
    if mark:
        outs.append(jax.ShapeDtypeStruct((8, 128), jnp.float32))
        out_specs.append(IN_VMEM)

    def run(*refs):
        refs = list(refs[len(later) :])
        if mark:
            mark_ref = refs.pop(used + results)
            mark_ref[...] = jnp.zeros_like(mark_ref)
        body(*refs)

    out = pl.pallas_call(
        run,
        name=name,
        in_specs=[*[ANYWHERE] * len(later), *specs],
        out_shape=outs,
        out_specs=out_specs,
        scratch_shapes=scratch,
        input_output_aliases={len(later) + i: o for i, o in (aliases or {}).items()},
        compiler_params=pltpu.CompilerParams(vmem_limit_bytes=mib * MIB),
        cost_estimate=pl.CostEstimate(flops=1024, bytes_accessed=1024, transcendentals=0),
    )(*later, *operands)
    return out if len(out) > 1 else out[0]


def in_hbm(array):
    return pltpu.with_memory_space_constraint(array, pltpu.HBM)


def like(rows, width, kind=jnp.bfloat16):
    return jax.ShapeDtypeStruct((rows, width), kind)


def slot_columns(me, chosen_ref, counts_ref, prob_ref):
    experts, _, slots = chosen_ref.shape
    diagonal = lax.broadcasted_iota(jnp.int32, (slots, slots), 0) == lax.broadcasted_iota(
        jnp.int32, (slots, slots), 1
    )
    position = lax.broadcasted_iota(jnp.int32, (slots, 1), 0)
    rows, weights = [], []
    for step in range(experts):
        expert = me ^ step
        live = position < counts_ref[0, expert]
        row = jnp.broadcast_to(chosen_ref[expert].astype(jnp.float32), (slots, slots))
        row = jnp.sum(jnp.where(diagonal, row, 0.0), axis=1, keepdims=True)
        prob = jnp.broadcast_to(prob_ref[expert], (slots, slots))
        prob = jnp.sum(jnp.where(diagonal, prob, 0.0), axis=1, keepdims=True)
        rows.append(jnp.where(live, row, -1.0))
        weights.append(jnp.where(live, prob, 0.0))
    return jnp.concatenate(rows, axis=0), jnp.concatenate(weights, axis=0)


def pick_body(plan, me_ref, counts_hbm, chosen_hbm, prob_hbm, tokens_hbm, cotangent_hbm, *refs):
    *outs, mask_ref, weights_ref = refs[:-6]
    counts_ref, chosen_ref, prob_ref, tokens_ref, cotangent_ref, sems = refs[-6:]
    experts, _, slots = chosen_ref.shape
    pairs = (
        (counts_hbm, counts_ref),
        (chosen_hbm, chosen_ref),
        (prob_hbm, prob_ref),
        (tokens_hbm, tokens_ref),
        (cotangent_hbm, cotangent_ref),
    )
    copies = [pltpu.make_async_copy(*pair, sems.at[index]) for index, pair in enumerate(pairs)]
    for copy in copies:
        copy.start()
    for copy in copies[:3]:
        copy.wait()
    rows, weights = slot_columns(me_ref[0], chosen_ref, counts_ref, prob_ref)
    length = tokens_ref.shape[0]
    place = lax.broadcasted_iota(jnp.int32, (rows.shape[0], length), 1).astype(jnp.float32)
    mask = (place == rows).astype(jnp.bfloat16)
    mask_ref[...] = mask
    weights_ref[...] = jnp.broadcast_to(weights, weights_ref.shape)
    for which, source_ref in enumerate((tokens_ref, cotangent_ref)):
        copies[3 + which].wait()
        value = jnp.dot(mask, source_ref[...], preferred_element_type=jnp.float32)
        if which:
            value = weights * value
        value = value.astype(jnp.bfloat16)
        for out_ref, blocks in zip(outs, plan):
            for place, (part, step) in enumerate(blocks):
                if part == which:
                    target = pl.ds(place * slots, slots)
                    out_ref[target, :] = value[step * slots : (step + 1) * slots]


def pick_slots(me, chosen, counts, gate_prob, tokens, cotangent, plan):
    experts, _, slots = chosen.shape
    length, width = tokens.shape
    total = experts * slots
    operands = (counts, chosen, gate_prob, tokens, cotangent)
    return run_kernel(
        functools.partial(pick_body, plan),
        "pick_slots",
        (me, *[in_hbm(array) for array in operands]),
        [IN_SMEM] + [ANYWHERE] * 5,
        [like(slots * len(blocks), width) for blocks in plan]
        + [like(total, length), like(total, 128, jnp.float32)],
        [IN_VMEM] * (len(plan) + 2),
        [pltpu.SMEM(counts.shape, counts.dtype)]
        + [pltpu.VMEM(array.shape, array.dtype) for array in operands[1:]]
        + [pltpu.SemaphoreType.DMA((5,))],
        16,
    )


def spread_matrix_body(mask_ref, weights_ref, weighted_ref, plain_ref):
    mask = mask_ref[...].astype(jnp.float32)
    weights = weights_ref[...][:, :1]
    high = weights.astype(jnp.bfloat16).astype(jnp.float32)
    count = mask.shape[0]
    plain_ref[...] = mask.T.astype(jnp.bfloat16)
    weighted_ref[:, :count] = (mask * high).T.astype(jnp.bfloat16)
    weighted_ref[:, count:] = (mask * (weights - high)).T.astype(jnp.bfloat16)


def spread_matrices(mask, weights, later=()):
    count, length = mask.shape
    return run_kernel(
        spread_matrix_body,
        "spread_matrices",
        (mask, weights),
        [IN_VMEM] * 2,
        [like(length, 2 * count), like(length, count)],
        [IN_VMEM] * 2,
        [],
        8,
        later,
    )


def spread_body(layout, slots, spread_ref, *refs):
    pieces, (out_hbm, block, sems) = refs[:-3], refs[-3:]
    values = jnp.concatenate([pieces[p][pl.ds(q * slots, slots), :] for p, q in layout], axis=0)
    if spread_ref.shape[1] > values.shape[0]:
        values = jnp.concatenate([values, values], axis=0)
    parts = sems.shape[0]
    size = block.shape[0] // parts
    copies = []
    for part in range(parts):
        rows = pl.ds(part * size, size)
        total = jnp.dot(spread_ref[rows, :], values, preferred_element_type=jnp.float32)
        block[rows, :] = total.astype(jnp.bfloat16)
        copies.append(pltpu.make_async_copy(block.at[rows], out_hbm.at[rows], sems.at[part]))
        copies[-1].start()
    for copy in copies:
        copy.wait()


def spread_rows(spread, pieces, layout, slots, later=(), mark=False, parts=4):
    length, width = spread.shape[0], pieces[0].shape[1]
    return run_kernel(
        functools.partial(spread_body, layout, slots),
        "spread_rows",
        (spread, *pieces),
        [IN_VMEM] * (1 + len(pieces)),
        [like(length, width)],
        [ANYWHERE],
        [pltpu.VMEM((length, width), jnp.bfloat16), pltpu.SemaphoreType.DMA((parts,))],
        16,
        later,
        mark,
    )


def load_body(by_rows, count, me_ref, source_ref, target_ref, sems):
    width = target_ref.shape[1 if by_rows else 2]
    copies = []
    for index in range(count):
        part = pl.ds(pl.multiple_of((me_ref[0] ^ index) * width, width), width)
        source = source_ref.at[part, :] if by_rows else source_ref.at[:, part]
        copies.append(pltpu.make_async_copy(source, target_ref.at[index], sems.at[index]))
        copies[-1].start()
    for copy in copies:
        copy.wait()


def load_weight(me, weight, by_rows, count, later=()):
    first, second = weight.shape
    shape = (count, first // count, second) if by_rows else (count, first, second // count)
    return run_kernel(
        functools.partial(load_body, by_rows, count),
        "load_weight",
        (me, in_hbm(weight)),
        [IN_SMEM, ANYWHERE],
        [jax.ShapeDtypeStruct(shape, weight.dtype)],
        [IN_VMEM],
        [pltpu.SemaphoreType.DMA((count,))],
        4,
        later,
    )


def arrange_body(plan, used, *refs):
    for rows, out_ref in zip(plan, refs[used:]):
        start = 0
        for source, first, size in rows:
            out_ref[pl.ds(start, size), :] = refs[source][pl.ds(first, size), :]
            start += size


def arrange(sources, plan, later=()):
    width = sources[0].shape[1]
    sizes = [sum(size for _, _, size in rows) for rows in plan]
    return run_kernel(
        functools.partial(arrange_body, plan, len(sources)),
        "arrange",
        tuple(sources),
        [IN_VMEM] * len(sources),
        [like(size, width) for size in sizes],
        [IN_VMEM] * len(plan),
        [],
        8,
        later,
    )


def add_body(used, *refs):
    total = refs[0][...].astype(jnp.float32)
    for ref in refs[1:used]:
        total += ref[...].astype(jnp.float32)
    start = 0
    for out_ref in refs[used:]:
        out_ref[...] = total[start : start + out_ref.shape[0]].astype(out_ref.dtype)
        start += out_ref.shape[0]


def add_up(terms, parts=1, later=()):
    rows, width = terms[0].shape
    return run_kernel(
        functools.partial(add_body, len(terms)),
        "add_up",
        tuple(terms),
        [IN_VMEM] * len(terms),
        [like(rows // parts, width)] * parts,
        [IN_VMEM] * parts,
        [],
        8,
        later,
    )


def near_body(first_ref, top_ref, second_ref, first_out, second_out):
    total = first_ref[...].astype(jnp.float32) + top_ref[...].astype(jnp.float32)
    first_out[...] = total.astype(first_out.dtype)
    second_out[...] = second_ref[...]


def near_pair(first, top, second, later=()):
    return run_kernel(
        near_body,
        "near_pair",
        (first, top, second),
        [IN_VMEM] * 3,
        [like(*first.shape)] * 2,
        [IN_VMEM] * 2,
        [],
        8,
        later,
    )


class Slices:
    def __init__(self, slices, part, slots):
        self.mixed = [[mixed for _, mixed in pieces] for pieces in slices]
        self.flat = [array for pieces in slices for array, _ in pieces]
        self.part, self.slots = part, slots
        self.count, self.width = len(slices), self.flat[0].shape[1]
        self.rows = sum(array.shape[0] // (2 if mixed else 1) for array, mixed in slices[0])

    def read(self, refs, index):
        first = sum(len(mixed) for mixed in self.mixed[:index])
        blocks = []
        for place, mixed in enumerate(self.mixed[index]):
            ref = refs[first + place]
            if mixed:
                for start in range(self.part * self.slots, ref.shape[0], 2 * self.slots):
                    blocks.append(ref[pl.ds(start, self.slots), :])
            else:
                blocks.append(ref[...])
        return blocks[0] if len(blocks) == 1 else jnp.concatenate(blocks, axis=0)


def partial_body(slices, dims, *refs):
    used = len(slices.flat)
    weights, sums = refs[used:][: len(dims)], refs[used + len(dims) :]
    for index in range(slices.count):
        rows = slices.read(refs, index)
        for weight_ref, dim, sum_ref in zip(weights, dims, sums):
            value = lax.dot_general(
                rows, weight_ref[index], dim, preferred_element_type=jnp.float32
            )
            if index == 0:
                sum_ref[...] = value
            else:
                sum_ref[...] += value


def partial_products(slices, weights, dims, units, later=()):
    return run_kernel(
        functools.partial(partial_body, slices, dims),
        "partial_products",
        (*slices.flat, *weights),
        [IN_VMEM] * (len(slices.flat) + len(weights)),
        [like(slices.rows, units, jnp.float32)] * len(weights),
        [IN_VMEM] * len(weights),
        [],
        8,
        later,
    )


def store_term(refs, index, term):
    term = term.astype(jnp.bfloat16)
    size = term.shape[0] // 2
    refs[2 * index][...] = term[:size]
    refs[2 * index + 1][...] = term[size:]


def forward_body(slices, *refs):
    used = len(slices.flat)
    gate_sum, up_sum, gate_ref, up_ref, down_ref = refs[used : used + 5]
    hidden_ref, slope_ref, silu_ref, *terms = refs[used + 5 :]
    last = gate_ref.shape[0] - 1
    rows = slices.read(refs, 0)
    gate = gate_sum[...] + jnp.dot(rows, gate_ref[last], preferred_element_type=jnp.float32)
    up = up_sum[...] + jnp.dot(rows, up_ref[last], preferred_element_type=jnp.float32)
    sigmoid = jax.nn.sigmoid(gate)
    silu = gate * sigmoid
    hidden = (silu * up).astype(jnp.bfloat16)
    hidden_ref[...] = hidden
    slope_ref[...] = up * sigmoid * (1.0 + gate * (1.0 - sigmoid))
    silu_ref[...] = silu
    for index in reversed(range(last + 1)):
        term = jnp.dot(hidden, down_ref[index], preferred_element_type=jnp.float32)
        store_term(terms, index, term)


def forward_terms(slices, sums, gate, up, down, later=()):
    count, width, units = gate.shape
    rows = sums[0].shape[0]
    f32 = jnp.float32
    out = run_kernel(
        functools.partial(forward_body, slices),
        "forward_terms",
        (*slices.flat, *sums, gate, up, down),
        [IN_VMEM] * (len(slices.flat) + 5),
        [like(rows, units), like(rows, units, f32), like(rows, units, f32)]
        + [like(rows // 2, width)] * (2 * count),
        [IN_VMEM] * (3 + 2 * count),
        [],
        8,
        later,
    )
    return out[:3], [out[3 + 2 * i : 5 + 2 * i] for i in range(count)]


def backward_body(slices, *refs):
    used = len(slices.flat)
    grad_sum, slope_ref, silu_ref, gate_ref, up_ref, down_ref = refs[used : used + 6]
    gate_grad_ref, up_grad_ref, *terms = refs[used + 6 :]
    last = gate_ref.shape[0] - 1
    rows = slices.read(refs, 0)
    grad = lax.dot_general(rows, down_ref[last], LAST, preferred_element_type=jnp.float32)
    grad += grad_sum[...]
    gate_grad = (grad * slope_ref[...]).astype(jnp.bfloat16)
    up_grad = (grad * silu_ref[...]).astype(jnp.bfloat16)
    gate_grad_ref[...] = gate_grad
    up_grad_ref[...] = up_grad
    store_term(terms, 0, back_term(gate_grad, up_grad, gate_ref, up_ref, last))


def back_term(gate_grad, up_grad, gate_ref, up_ref, index):
    term = lax.dot_general(gate_grad, gate_ref[index], LAST, preferred_element_type=jnp.float32)
    return term + lax.dot_general(up_grad, up_ref[index], LAST, preferred_element_type=jnp.float32)


def backward_rest_body(gate_grad_ref, up_grad_ref, gate_ref, up_ref, *terms):
    for index in reversed(range(len(terms) // 2)):
        term = back_term(gate_grad_ref[...], up_grad_ref[...], gate_ref, up_ref, index)
        store_term(terms, index, term)


def backward_rest(gate_grad, up_grad, gate, up, later=()):
    count, width, _ = gate.shape
    rows = gate_grad.shape[0]
    out = run_kernel(
        backward_rest_body,
        "backward_rest",
        (gate_grad, up_grad, gate, up),
        [IN_VMEM] * 4,
        [like(rows // 2, width)] * (2 * count - 2),
        [IN_VMEM] * (2 * count - 2),
        [],
        8,
        later,
    )
    return [out[2 * i : 2 * i + 2] for i in range(count - 1)]


def backward_terms(slices, grad_sum, slope, silu, gate, up, down, later=()):
    _, width, units = gate.shape
    rows = slope.shape[0]
    out = run_kernel(
        functools.partial(backward_body, slices),
        "backward_terms",
        (*slices.flat, grad_sum, slope, silu, gate, up, down),
        [IN_VMEM] * (len(slices.flat) + 6),
        [like(rows, units)] * 2 + [like(rows // 2, width)] * 2,
        [IN_VMEM] * 4,
        [],
        8,
        later,
    )
    return out[:2], out[2:]


def merge_body(first_top, first_bottom, second_top, second_bottom, top, bottom, first, second):
    size = top.shape[0]
    upper, lower = pl.ds(0, size), pl.ds(size, size)
    total = first_top[...].astype(jnp.float32) + top[...].astype(jnp.float32)
    first[upper, :] = total.astype(first.dtype)
    first[lower, :] = first_bottom[...]
    total = second_bottom[...].astype(jnp.float32) + bottom[...].astype(jnp.float32)
    second[lower, :] = total.astype(second.dtype)
    second[upper, :] = second_top[...]


def merge(first, second, top, bottom, later=()):
    rows, width = first[0].shape
    return run_kernel(
        merge_body,
        "merge",
        (*first, *second, top, bottom),
        [IN_VMEM] * 6,
        [like(2 * rows, width)] * 2,
        [IN_VMEM] * 2,
        [],
        8,
        later,
    )


def down_grad_body(slices, start, filled, me_ref, hidden_ref, *refs):
    out_ref, block, sems = refs[-3:]
    _, _, width = block.shape
    hidden = hidden_ref[...]
    copies = []
    for index in range(slices.count):
        block[index] = lax.dot_general(
            hidden, slices.read(refs[filled:], index), ROWS, preferred_element_type=jnp.float32
        ).astype(jnp.bfloat16)
        first = pl.multiple_of((me_ref[0] ^ (start + index)) * width, width)
        target = out_ref.at[:, pl.ds(first, width)]
        copies.append(pltpu.make_async_copy(block.at[index], target, sems.at[index]))
        copies[-1].start()
    for copy in copies:
        copy.wait()


def down_grads(me, hidden, slices, start, total, filled=(), later=()):
    width, units = slices.width, hidden.shape[1]
    return run_kernel(
        functools.partial(down_grad_body, slices, start, len(filled)),
        "down_grads",
        (me, hidden, *filled, *slices.flat),
        [IN_SMEM, IN_VMEM] + [ANYWHERE] * len(filled) + [IN_VMEM] * len(slices.flat),
        [like(units, width * total)],
        [ANYWHERE],
        [
            pltpu.VMEM((slices.count, units, width), jnp.bfloat16),
            pltpu.SemaphoreType.DMA((slices.count,)),
        ],
        16,
        later,
        True,
        {2: 0} if filled else None,
    )


def weight_grad_body(slices, me_ref, *refs):
    grad_refs, (gate_hbm, up_hbm, block, sems) = refs[:2], refs[-4:]
    _, count, width, units = block.shape
    grads = jnp.concatenate([ref[...] for ref in grad_refs], axis=1)
    copies = []
    for index in range(count):
        rows = slices.read(refs[2:], index)
        start = pl.multiple_of((me_ref[0] ^ index) * width, width)
        both = lax.dot_general(rows, grads, ROWS, preferred_element_type=jnp.float32)
        both = both.astype(jnp.bfloat16)
        for which, out_ref in enumerate((gate_hbm, up_hbm)):
            block[which, index] = both[:, which * units : (which + 1) * units]
            target = out_ref.at[pl.ds(start, width), :]
            sem = sems.at[2 * index + which]
            copies.append(pltpu.make_async_copy(block.at[which, index], target, sem))
            copies[-1].start()
    for copy in copies:
        copy.wait()


def weight_grads(me, slices, gate_grad, up_grad, later=()):
    count, width, units = slices.count, slices.width, gate_grad.shape[1]
    return run_kernel(
        functools.partial(weight_grad_body, slices),
        "weight_grads",
        (me, gate_grad, up_grad, *slices.flat),
        [IN_SMEM] + [IN_VMEM] * (2 + len(slices.flat)),
        [like(width * count, units)] * 2,
        [ANYWHERE] * 2,
        [
            pltpu.VMEM((2, count, width, units), jnp.bfloat16),
            pltpu.SemaphoreType.DMA((2 * count,)),
        ],
        20,
        later,
        True,
    )


def pick_rows(tokens, cotangent, row_index, live_mask, weight):
    flat_rows = row_index.reshape(-1)
    keep_rows = live_mask.reshape(-1)[:, None]
    taken_tokens = jnp.take(tokens, flat_rows, axis=0)
    picked_tokens = jnp.where(keep_rows, taken_tokens, jnp.zeros_like(taken_tokens))
    taken_grads = jnp.take(cotangent, flat_rows, axis=0).astype(jnp.float32)
    picked_grads = (weight.reshape(-1)[:, None] * taken_grads).astype(jnp.bfloat16)
    shaped = row_index.shape + (tokens.shape[1],)
    return (picked_tokens.reshape(shaped), picked_grads.reshape(shaped))


def to_slots(summed, experts, slot_count):
    return summed.astype(jnp.bfloat16).reshape(experts, slot_count, summed.shape[1])


def send_back(term, experts, slot_count):
    summed = lax.psum_scatter(
        term.astype(jnp.bfloat16), "fsdp", scatter_dimension=1, tiled=True
    ).astype(jnp.float32)
    return lax.all_to_all(
        to_slots(summed, experts, slot_count), "ep", split_axis=0, concat_axis=0, tiled=True
    )


def by_collectives(tokens, cotangent, gate_weight, up_weight, down_weight, chosen, counts, gate_prob):
    experts = chosen.shape[0]
    slot_count = chosen.shape[2]
    features = tokens.shape[1]
    row_index = chosen[:, 0, :]
    position = lax.broadcasted_iota(jnp.int32, (experts, slot_count), 1)
    live_mask = position < counts
    weight = jnp.where(live_mask, gate_prob[:, 0, :], 0.0)
    picked_tokens, picked_grads = pick_rows(tokens, cotangent, row_index, live_mask, weight)
    sliced_tokens, sliced_grads = (
        lax.all_to_all(picked_tokens, "ep", split_axis=0, concat_axis=0, tiled=True),
        lax.all_to_all(picked_grads, "ep", split_axis=0, concat_axis=0, tiled=True),
    )
    rows_tokens, rows_grads = (
        lax.all_gather(sliced_tokens, "fsdp", axis=2, tiled=True),
        lax.all_gather(sliced_grads, "fsdp", axis=2, tiled=True),
    )
    full_width = rows_tokens.shape[2]
    total_rows = rows_tokens.shape[0] * slot_count
    rows_tokens = rows_tokens.reshape(total_rows, full_width)
    rows_grads = rows_grads.reshape(total_rows, full_width)
    gate_local = gate_weight[0]
    up_local = up_weight[0]
    down_local = down_weight[0]
    pre_gate = jnp.dot(rows_tokens, gate_local, preferred_element_type=jnp.float32)
    pre_up = jnp.dot(rows_tokens, up_local, preferred_element_type=jnp.float32)
    sigmoid_gate = jax.nn.sigmoid(pre_gate)
    activated = pre_gate * sigmoid_gate
    hidden = (activated * pre_up).astype(jnp.bfloat16)
    output_term = jnp.dot(hidden, down_local, preferred_element_type=jnp.float32)
    output_back = send_back(output_term, experts, slot_count)
    contract_rows = (((0,), (0,)), ((), ()))
    contract_last = (((1,), (1,)), ((), ()))
    grad_hidden = lax.dot_general(
        rows_grads, down_local, contract_last, preferred_element_type=jnp.float32
    )
    grad_pre_gate = (
        grad_hidden * pre_up * sigmoid_gate * (1.0 + pre_gate * (1.0 - sigmoid_gate))
    ).astype(jnp.bfloat16)
    grad_pre_up = (grad_hidden * activated).astype(jnp.bfloat16)
    grad_down = lax.dot_general(
        hidden, rows_grads, contract_rows, preferred_element_type=jnp.float32
    ).astype(jnp.bfloat16)
    grad_gate = lax.dot_general(
        rows_tokens, grad_pre_gate, contract_rows, preferred_element_type=jnp.float32
    ).astype(jnp.bfloat16)
    grad_up = lax.dot_general(
        rows_tokens, grad_pre_up, contract_rows, preferred_element_type=jnp.float32
    ).astype(jnp.bfloat16)
    grad_term = lax.dot_general(
        grad_pre_gate, gate_local, contract_last, preferred_element_type=jnp.float32
    )
    grad_term = grad_term + lax.dot_general(
        grad_pre_up, up_local, contract_last, preferred_element_type=jnp.float32
    )
    grad_back = send_back(grad_term, experts, slot_count)
    flat_rows = row_index.reshape(-1)
    output_rows = output_back.reshape(-1, features).astype(jnp.float32)
    mixture = (
        jnp.zeros((tokens.shape[0], features), jnp.float32)
        .at[flat_rows]
        .add(weight.reshape(-1)[:, None] * output_rows)
    )
    grad_rows = jnp.where(
        live_mask.reshape(-1)[:, None], grad_back.reshape(-1, features).astype(jnp.float32), 0.0
    )
    grad_tokens = jnp.zeros((tokens.shape[0], features), jnp.float32).at[flat_rows].add(grad_rows)
    return (
        mixture.astype(jnp.bfloat16),
        grad_tokens.astype(jnp.bfloat16),
        grad_gate[None],
        grad_up[None],
        grad_down[None],
    )


def swap(array, distance, axis):
    size = lax.axis_size(axis)
    return lax.ppermute(array, axis, [(i, i ^ distance) for i in range(size)])


def joined(*arrays):
    return jnp.concatenate(arrays, axis=0)


def gathered(whole, first, second):
    from_first = swap(whole, first, "fsdp")
    from_second = swap(whole, second, "fsdp")
    passed = arrange((from_first,), [[(0, 0, whole.shape[0])]], (from_second,))
    slices = [[whole], [None], [None], [swap(passed, second, "fsdp")]]
    slices[first], slices[second] = [from_first], [from_second]
    return slices


def pieces_of(mixed, plain):
    return [
        [(piece, True) for piece in some] + [(piece, False) for piece in others]
        for some, others in zip(mixed, plain)
    ]


def by_links(tokens, cotangent, gate_weight, up_weight, down_weight, chosen, counts, gate_prob):
    experts, _, slots = chosen.shape
    count = lax.axis_size("fsdp")
    ep_index = lax.axis_index("ep").reshape(1)
    me = lax.axis_index("fsdp").reshape(1)
    units = gate_weight.shape[2]
    two = 2 * slots
    plan = [[(part, step) for part in range(2)] for step in range(4)]
    plan += [[(part, step), (part, step + 1)] for part in range(2) for step in (4, 6)]
    own, core, even1, odd1, token2, token3, grad2, grad3, mask, weights = pick_slots(
        ep_index, chosen, counts.reshape(1, experts), gate_prob, tokens, cotangent, plan
    )

    token2 = swap(token2, 4, "ep")
    token3 = swap(token3, 6, "ep")
    even1 = swap(even1, 2, "ep")
    odd1 = swap(odd1, 3, "ep")
    core = swap(core, 1, "ep")
    gate = load_weight(me, gate_weight[0], True, count, (own,))
    near = joined(arrange((own,), [[(0, 0, two)]], (gate,)), core, even1, odd1)
    near_x = swap(near, 1, "fsdp")
    near_y = swap(near, 2, "fsdp")
    odd = swap(joined(token2[slots:], token3[slots:], token2, token3), 1, "ep")
    ends = [(0, 0, slots), (2, 0, slots), (1, 0, slots), (2, slots, slots)]
    up = load_weight(me, up_weight[0], True, count, (near,))
    far = arrange((token2, token3, odd), [ends], (near_x, near_y, up))
    far_tokens = gathered(far, 2, 1)
    grad2 = swap(grad2, 4, "ep")
    grad3 = swap(grad3, 6, "ep")
    down = load_weight(me, down_weight[0], False, count, (up,))
    weighted, plain = spread_matrices(mask, weights, (down,))
    odd = arrange(
        (grad2, grad3),
        [[(0, slots, slots), (1, slots, slots), (0, 0, two), (1, 0, two)]],
    )
    odd = swap(odd, 1, "ep")
    far_grads = gathered(arrange((grad2, grad3, odd), [ends]), 1, 2)
    halves = [[(0, first, slots) for first in range(part * slots, 4 * two, two)] for part in range(2)]
    near_d = swap(arrange((near_x,), halves[:1]), 2, "fsdp")
    near_grad_d = swap(arrange((near_y,), halves[1:]), 1, "fsdp")
    mixed = [[near], [near_x], [near_y], []]
    picked = pieces_of(mixed, far_tokens)
    grads = pieces_of(mixed, far_grads)
    picked[3].insert(0, (near_d, False))
    grads[3].insert(0, (near_grad_d, False))
    first = Slices(picked[:3], 0, slots)
    last = Slices(picked[3:], 0, slots)

    sums = partial_products(first, (gate, up), (PLAIN, PLAIN), units)
    (hidden, slope, silu), terms = forward_terms(last, sums, gate, up, down)
    bottom = swap(terms[3][1], 1, "fsdp")
    top = swap(terms[3][0], 2, "fsdp")

    first = Slices(grads[:3], 1, slots)
    last = Slices(grads[3:], 1, slots)
    (grad_sum,) = [partial_products(first, (down,), (LAST,), units, (hidden,))]
    grad_down, mark = down_grads(me, hidden, first, 0, count, (), (grad_sum,))
    sum_x, sum_y = merge(terms[1], terms[2], top, bottom, (mark,))
    (gate_grad, up_grad), back_d = backward_terms(
        last, grad_sum, slope, silu, gate, up, down, (sum_x,)
    )
    sum_x = swap(sum_x, 1, "fsdp")
    sum_y = swap(sum_y, 2, "fsdp")
    bottom = swap(back_d[1], 1, "fsdp")
    top = swap(back_d[0], 2, "fsdp")
    back = backward_rest(gate_grad, up_grad, gate, up)
    out0, out1, out2, out3 = add_up([joined(*terms[0]), sum_x, sum_y], 4, (back[0][0],))
    out3 = swap(out3, 6, "ep")
    out2 = swap(out2, 4, "ep")
    out1 = swap(out1, 2, "ep")

    y_far = add_up([back[2][1], bottom], 1, (out0,))
    x_near, y_near = near_pair(back[1][0], top, back[2][0], (y_far,))
    x_far = swap(back[1][1], 1, "fsdp")
    y_far = swap(y_far, 2, "fsdp")
    x_near = swap(x_near, 1, "fsdp")
    y_near = swap(y_near, 2, "fsdp")
    layout = []
    for step in range(experts // 2):
        layout += [(step, 0), (experts // 2, step)]
    outs = [out0, out1, out2, out3]
    outs.append(swap(joined(*[piece[slots:] for piece in outs]), 1, "ep"))
    back2, back3 = add_up([back[0][1], x_far, y_far], 2)
    last = Slices(grads[3:], 1, slots)
    grad_down, mark = down_grads(me, hidden, last, count - 1, count, (grad_down,), (back2,))
    back0, back1 = add_up([back[0][0], x_near, y_near], 2, (mark, outs[-1]))
    back3 = swap(back3, 6, "ep")
    back2 = swap(back2, 4, "ep")
    back1 = swap(back1, 2, "ep")
    grad_gate, grad_up, mark = weight_grads(
        me, Slices(picked, 0, slots), gate_grad, up_grad, (back0,)
    )
    mixture = spread_rows(weighted, outs, layout, slots)
    backs = [back0, back1, back2, back3]
    far_odd = [[(0, slots, slots), (1, slots, slots), (0, 0, two)]]
    backs.append(swap(arrange((back2, back3), far_odd, (mark,)), 1, "ep"))
    backs.append(swap(arrange((back0, back1), [far_odd[0][:2]], (mark,)), 1, "ep"))
    layout = [(0, 0), (5, 0), (1, 0), (5, 1), (2, 0), (4, 0), (3, 0), (4, 1)]
    grad_tokens = spread_rows(plain, backs, layout, slots)
    return mixture, grad_tokens, grad_gate[None], grad_up[None], grad_down[None]


def solution(mesh):
    placed = (
        P("ep", "fsdp"),
        P("ep", "fsdp"),
        P("ep", None, "fsdp"),
        P("ep", None, "fsdp"),
        P("ep", "fsdp", None),
        P(None, "ep", None),
        P(None, "ep"),
        P(None, "ep", None),
    )

    def per_part(*arrays):
        fits = mesh.shape["fsdp"] == 4 and mesh.shape["ep"] == 8 and arrays[0].shape[1] % 128 == 0
        return (by_links if fits else by_collectives)(*arrays)

    return jax.shard_map(
        per_part,
        mesh=mesh,
        in_specs=placed,
        out_specs=(
            P("ep", "fsdp"),
            P("ep", "fsdp"),
            P("ep", None, "fsdp"),
            P("ep", None, "fsdp"),
            P("ep", "fsdp", None),
        ),
        check_vma=False,
    )
```

```python
import functools

import jax
import jax.numpy as jnp
from jax import lax
from jax.experimental import pallas as pl
from jax.experimental.pallas import tpu as pltpu
from jax.sharding import PartitionSpec as P

ROWS = (((0,), (0,)), ((), ()))
PLAIN = (((1,), (0,)), ((), ()))
LAST = (((1,), (1,)), ((), ()))
IN_VMEM = pl.BlockSpec(memory_space=pltpu.VMEM)
IN_SMEM = pl.BlockSpec(memory_space=pltpu.SMEM)
ANYWHERE = pl.BlockSpec(memory_space=pl.ANY)
MIB = 1024 * 1024


def run_kernel(body, name, operands, specs, outs, out_specs, scratch, mib, later=(), mark=False, aliases=None):
    used = len(operands)
    outs, out_specs = list(outs), list(out_specs)
    results = len(outs)
    if mark:
        outs.append(jax.ShapeDtypeStruct((8, 128), jnp.float32))
        out_specs.append(IN_VMEM)

    def run(*refs):
        refs = list(refs[len(later) :])
        if mark:
            mark_ref = refs.pop(used + results)
            mark_ref[...] = jnp.zeros_like(mark_ref)
        body(*refs)

    out = pl.pallas_call(
        run,
        name=name,
        in_specs=[*[ANYWHERE] * len(later), *specs],
        out_shape=outs,
        out_specs=out_specs,
        scratch_shapes=scratch,
        input_output_aliases={len(later) + i: o for i, o in (aliases or {}).items()},
        compiler_params=pltpu.CompilerParams(vmem_limit_bytes=mib * MIB),
        cost_estimate=pl.CostEstimate(flops=1024, bytes_accessed=1024, transcendentals=0),
    )(*later, *operands)
    return out if len(out) > 1 else out[0]


def in_hbm(array):
    return pltpu.with_memory_space_constraint(array, pltpu.HBM)


def like(rows, width, kind=jnp.bfloat16):
    return jax.ShapeDtypeStruct((rows, width), kind)


def slot_columns(me, chosen_ref, counts_ref, prob_ref):
    experts, _, slots = chosen_ref.shape
    diagonal = lax.broadcasted_iota(jnp.int32, (slots, slots), 0) == lax.broadcasted_iota(
        jnp.int32, (slots, slots), 1
    )
    position = lax.broadcasted_iota(jnp.int32, (slots, 1), 0)
    rows, weights = [], []
    for step in range(experts):
        expert = me ^ step
        live = position < counts_ref[0, expert]
        row = jnp.broadcast_to(chosen_ref[expert].astype(jnp.float32), (slots, slots))
        row = jnp.sum(jnp.where(diagonal, row, 0.0), axis=1, keepdims=True)
        prob = jnp.broadcast_to(prob_ref[expert], (slots, slots))
        prob = jnp.sum(jnp.where(diagonal, prob, 0.0), axis=1, keepdims=True)
        rows.append(jnp.where(live, row, -1.0))
        weights.append(jnp.where(live, prob, 0.0))
    return jnp.concatenate(rows, axis=0), jnp.concatenate(weights, axis=0)


def pick_body(plan, me_ref, counts_hbm, chosen_hbm, prob_hbm, tokens_hbm, cotangent_hbm, *refs):
    *outs, mask_ref, weights_ref = refs[:-6]
    counts_ref, chosen_ref, prob_ref, tokens_ref, cotangent_ref, sems = refs[-6:]
    experts, _, slots = chosen_ref.shape
    length = tokens_ref.shape[0]
    halves = [pl.ds(first, length // 2) for first in (0, length // 2)]
    pairs = [(counts_hbm, counts_ref), (chosen_hbm, chosen_ref), (prob_hbm, prob_ref)]
    for source, target in ((tokens_hbm, tokens_ref), (cotangent_hbm, cotangent_ref)):
        pairs += [(source.at[half], target.at[half]) for half in halves]
    copies = [pltpu.make_async_copy(*pair, sems.at[index]) for index, pair in enumerate(pairs)]
    for copy in copies:
        copy.start()
    for copy in copies[:3]:
        copy.wait()
    rows, weights = slot_columns(me_ref[0], chosen_ref, counts_ref, prob_ref)
    place = lax.broadcasted_iota(jnp.int32, (rows.shape[0], length), 1).astype(jnp.float32)
    mask = (place == rows).astype(jnp.bfloat16)
    mask_ref[...] = mask
    weights_ref[...] = jnp.broadcast_to(weights, weights_ref.shape)
    for which, source_ref in enumerate((tokens_ref, cotangent_ref)):
        value = 0.0
        for part, half in enumerate(halves):
            copies[3 + 2 * which + part].wait()
            columns = mask[:, part * (length // 2) : (part + 1) * (length // 2)]
            value += jnp.dot(columns, source_ref[half, :], preferred_element_type=jnp.float32)
        if which:
            value = weights * value
        value = value.astype(jnp.bfloat16)
        for out_ref, blocks in zip(outs, plan):
            for place, (part, step) in enumerate(blocks):
                if part == which:
                    target = pl.ds(place * slots, slots)
                    out_ref[target, :] = value[step * slots : (step + 1) * slots]


def pick_slots(me, chosen, counts, gate_prob, tokens, cotangent, plan):
    experts, _, slots = chosen.shape
    length, width = tokens.shape
    total = experts * slots
    operands = (counts, chosen, gate_prob, tokens, cotangent)
    return run_kernel(
        functools.partial(pick_body, plan),
        "pick_slots",
        (me, *[in_hbm(array) for array in operands]),
        [IN_SMEM] + [ANYWHERE] * 5,
        [like(slots * len(blocks), width) for blocks in plan]
        + [like(total, length), like(total, 128, jnp.float32)],
        [IN_VMEM] * (len(plan) + 2),
        [pltpu.SMEM(counts.shape, counts.dtype)]
        + [pltpu.VMEM(array.shape, array.dtype) for array in operands[1:]]
        + [pltpu.SemaphoreType.DMA((7,))],
        16,
    )


def spread_matrix_body(mask_ref, weights_ref, weighted_ref, plain_ref):
    mask = mask_ref[...].astype(jnp.float32)
    weights = weights_ref[...][:, :1]
    high = weights.astype(jnp.bfloat16).astype(jnp.float32)
    count = mask.shape[0]
    plain_ref[...] = mask.T.astype(jnp.bfloat16)
    weighted_ref[:, :count] = (mask * high).T.astype(jnp.bfloat16)
    weighted_ref[:, count:] = (mask * (weights - high)).T.astype(jnp.bfloat16)


def spread_matrices(mask, weights, later=()):
    count, length = mask.shape
    return run_kernel(
        spread_matrix_body,
        "spread_matrices",
        (mask, weights),
        [IN_VMEM] * 2,
        [like(length, 2 * count), like(length, count)],
        [IN_VMEM] * 2,
        [],
        8,
        later,
    )


def spread_body(layout, slots, spread_ref, *refs):
    pieces, (out_hbm, block, sems) = refs[:-3], refs[-3:]
    values = jnp.concatenate([pieces[p][pl.ds(q * slots, slots), :] for p, q in layout], axis=0)
    if spread_ref.shape[1] > values.shape[0]:
        values = jnp.concatenate([values, values], axis=0)
    parts = sems.shape[0]
    size = block.shape[1] // parts
    copies = []
    for part in range(parts):
        columns = pl.ds(part * size, size)
        total = jnp.dot(
            spread_ref[...],
            values[:, part * size : (part + 1) * size],
            preferred_element_type=jnp.float32,
        )
        block[:, columns] = total.astype(jnp.bfloat16)
        target = out_hbm.at[:, columns]
        copies.append(pltpu.make_async_copy(block.at[:, columns], target, sems.at[part]))
        copies[-1].start()
    for copy in copies:
        copy.wait()


def spread_rows(spread, pieces, layout, slots, later=(), mark=False):
    length, width = spread.shape[0], pieces[0].shape[1]
    parts = width // 256 if width % 256 == 0 else 1
    return run_kernel(
        functools.partial(spread_body, layout, slots),
        "spread_rows",
        (spread, *pieces),
        [IN_VMEM] * (1 + len(pieces)),
        [like(length, width)],
        [ANYWHERE],
        [pltpu.VMEM((length, width), jnp.bfloat16), pltpu.SemaphoreType.DMA((parts,))],
        16,
        later,
        mark,
    )


def load_body(by_rows, count, me_ref, source_ref, target_ref, sems):
    width = target_ref.shape[1 if by_rows else 2]
    copies = []
    for index in range(count):
        part = pl.ds(pl.multiple_of((me_ref[0] ^ index) * width, width), width)
        source = source_ref.at[part, :] if by_rows else source_ref.at[:, part]
        copies.append(pltpu.make_async_copy(source, target_ref.at[index], sems.at[index]))
        copies[-1].start()
    for copy in copies:
        copy.wait()


def load_weight(me, weight, by_rows, count, later=()):
    first, second = weight.shape
    shape = (count, first // count, second) if by_rows else (count, first, second // count)
    return run_kernel(
        functools.partial(load_body, by_rows, count),
        "load_weight",
        (me, in_hbm(weight)),
        [IN_SMEM, ANYWHERE],
        [jax.ShapeDtypeStruct(shape, weight.dtype)],
        [IN_VMEM],
        [pltpu.SemaphoreType.DMA((count,))],
        4,
        later,
    )


def arrange_body(plan, used, *refs):
    for rows, out_ref in zip(plan, refs[used:]):
        start = 0
        for source, first, size in rows:
            out_ref[pl.ds(start, size), :] = refs[source][pl.ds(first, size), :]
            start += size


def arrange(sources, plan, later=()):
    width = sources[0].shape[1]
    sizes = [sum(size for _, _, size in rows) for rows in plan]
    return run_kernel(
        functools.partial(arrange_body, plan, len(sources)),
        "arrange",
        tuple(sources),
        [IN_VMEM] * len(sources),
        [like(size, width) for size in sizes],
        [IN_VMEM] * len(plan),
        [],
        8,
        later,
    )


def add_body(used, *refs):
    total = refs[0][...].astype(jnp.float32)
    for ref in refs[1:used]:
        total += ref[...].astype(jnp.float32)
    start = 0
    for out_ref in refs[used:]:
        out_ref[...] = total[start : start + out_ref.shape[0]].astype(out_ref.dtype)
        start += out_ref.shape[0]


def add_up(terms, parts=1, later=()):
    rows, width = terms[0].shape
    return run_kernel(
        functools.partial(add_body, len(terms)),
        "add_up",
        tuple(terms),
        [IN_VMEM] * len(terms),
        [like(rows // parts, width)] * parts,
        [IN_VMEM] * parts,
        [],
        8,
        later,
    )


def near_body(first_ref, top_ref, second_ref, first_out, second_out):
    total = first_ref[...].astype(jnp.float32) + top_ref[...].astype(jnp.float32)
    first_out[...] = total.astype(first_out.dtype)
    second_out[...] = second_ref[...]


def near_pair(first, top, second, later=()):
    return run_kernel(
        near_body,
        "near_pair",
        (first, top, second),
        [IN_VMEM] * 3,
        [like(*first.shape)] * 2,
        [IN_VMEM] * 2,
        [],
        8,
        later,
    )


class Slices:
    def __init__(self, slices, part, slots):
        self.mixed = [[mixed for _, mixed in pieces] for pieces in slices]
        self.flat = [array for pieces in slices for array, _ in pieces]
        self.part, self.slots = part, slots
        self.count, self.width = len(slices), self.flat[0].shape[1]
        self.rows = sum(array.shape[0] // (2 if mixed else 1) for array, mixed in slices[0])

    def read(self, refs, index):
        first = sum(len(mixed) for mixed in self.mixed[:index])
        blocks = []
        for place, mixed in enumerate(self.mixed[index]):
            ref = refs[first + place]
            if mixed:
                for start in range(self.part * self.slots, ref.shape[0], 2 * self.slots):
                    blocks.append(ref[pl.ds(start, self.slots), :])
            else:
                blocks.append(ref[...])
        return blocks[0] if len(blocks) == 1 else jnp.concatenate(blocks, axis=0)


def partial_body(slices, dims, *refs):
    used = len(slices.flat)
    weights, sums = refs[used:][: len(dims)], refs[used + len(dims) :]
    for index in range(slices.count):
        rows = slices.read(refs, index)
        for weight_ref, dim, sum_ref in zip(weights, dims, sums):
            value = lax.dot_general(
                rows, weight_ref[index], dim, preferred_element_type=jnp.float32
            )
            if index == 0:
                sum_ref[...] = value
            else:
                sum_ref[...] += value


def partial_products(slices, weights, dims, units, later=()):
    return run_kernel(
        functools.partial(partial_body, slices, dims),
        "partial_products",
        (*slices.flat, *weights),
        [IN_VMEM] * (len(slices.flat) + len(weights)),
        [like(slices.rows, units, jnp.float32)] * len(weights),
        [IN_VMEM] * len(weights),
        [],
        8,
        later,
    )


def store_term(refs, index, term):
    term = term.astype(jnp.bfloat16)
    size = term.shape[0] // 2
    refs[2 * index][...] = term[:size]
    refs[2 * index + 1][...] = term[size:]


def forward_body(slices, *refs):
    used = len(slices.flat)
    gate_sum, up_sum, gate_ref, up_ref, down_ref = refs[used : used + 5]
    hidden_ref, slope_ref, silu_ref, *terms = refs[used + 5 :]
    last = gate_ref.shape[0] - 1
    rows = slices.read(refs, 0)
    gate = gate_sum[...] + jnp.dot(rows, gate_ref[last], preferred_element_type=jnp.float32)
    up = up_sum[...] + jnp.dot(rows, up_ref[last], preferred_element_type=jnp.float32)
    sigmoid = jax.nn.sigmoid(gate)
    silu = gate * sigmoid
    hidden = (silu * up).astype(jnp.bfloat16)
    hidden_ref[...] = hidden
    slope_ref[...] = up * sigmoid * (1.0 + gate * (1.0 - sigmoid))
    silu_ref[...] = silu
    for index in reversed(range(last + 1)):
        term = jnp.dot(hidden, down_ref[index], preferred_element_type=jnp.float32)
        store_term(terms, index, term)


def forward_terms(slices, sums, gate, up, down, later=()):
    count, width, units = gate.shape
    rows = sums[0].shape[0]
    f32 = jnp.float32
    out = run_kernel(
        functools.partial(forward_body, slices),
        "forward_terms",
        (*slices.flat, *sums, gate, up, down),
        [IN_VMEM] * (len(slices.flat) + 5),
        [like(rows, units), like(rows, units, f32), like(rows, units, f32)]
        + [like(rows // 2, width)] * (2 * count),
        [IN_VMEM] * (3 + 2 * count),
        [],
        8,
        later,
    )
    return out[:3], [out[3 + 2 * i : 5 + 2 * i] for i in range(count)]


def backward_body(slices, *refs):
    used = len(slices.flat)
    grad_sum, slope_ref, silu_ref, gate_ref, up_ref, down_ref = refs[used : used + 6]
    gate_grad_ref, up_grad_ref, *terms = refs[used + 6 :]
    last = gate_ref.shape[0] - 1
    rows = slices.read(refs, 0)
    grad = lax.dot_general(rows, down_ref[last], LAST, preferred_element_type=jnp.float32)
    grad += grad_sum[...]
    gate_grad = (grad * slope_ref[...]).astype(jnp.bfloat16)
    up_grad = (grad * silu_ref[...]).astype(jnp.bfloat16)
    gate_grad_ref[...] = gate_grad
    up_grad_ref[...] = up_grad
    store_term(terms, 0, back_term(gate_grad, up_grad, gate_ref, up_ref, last))


def back_term(gate_grad, up_grad, gate_ref, up_ref, index):
    term = lax.dot_general(gate_grad, gate_ref[index], LAST, preferred_element_type=jnp.float32)
    return term + lax.dot_general(up_grad, up_ref[index], LAST, preferred_element_type=jnp.float32)


def backward_rest_body(gate_grad_ref, up_grad_ref, gate_ref, up_ref, *terms):
    for index in reversed(range(len(terms) // 2)):
        term = back_term(gate_grad_ref[...], up_grad_ref[...], gate_ref, up_ref, index)
        store_term(terms, index, term)


def backward_rest(gate_grad, up_grad, gate, up, later=()):
    count, width, _ = gate.shape
    rows = gate_grad.shape[0]
    out = run_kernel(
        backward_rest_body,
        "backward_rest",
        (gate_grad, up_grad, gate, up),
        [IN_VMEM] * 4,
        [like(rows // 2, width)] * (2 * count - 2),
        [IN_VMEM] * (2 * count - 2),
        [],
        8,
        later,
    )
    return [out[2 * i : 2 * i + 2] for i in range(count - 1)]


def backward_terms(slices, grad_sum, slope, silu, gate, up, down, later=()):
    _, width, units = gate.shape
    rows = slope.shape[0]
    out = run_kernel(
        functools.partial(backward_body, slices),
        "backward_terms",
        (*slices.flat, grad_sum, slope, silu, gate, up, down),
        [IN_VMEM] * (len(slices.flat) + 6),
        [like(rows, units)] * 2 + [like(rows // 2, width)] * 2,
        [IN_VMEM] * 4,
        [],
        8,
        later,
    )
    return out[:2], out[2:]


def merge_body(first_top, first_bottom, second_top, second_bottom, top, bottom, first, second):
    size = top.shape[0]
    upper, lower = pl.ds(0, size), pl.ds(size, size)
    total = first_top[...].astype(jnp.float32) + top[...].astype(jnp.float32)
    first[upper, :] = total.astype(first.dtype)
    first[lower, :] = first_bottom[...]
    total = second_bottom[...].astype(jnp.float32) + bottom[...].astype(jnp.float32)
    second[lower, :] = total.astype(second.dtype)
    second[upper, :] = second_top[...]


def merge(first, second, top, bottom, later=()):
    rows, width = first[0].shape
    return run_kernel(
        merge_body,
        "merge",
        (*first, *second, top, bottom),
        [IN_VMEM] * 6,
        [like(2 * rows, width)] * 2,
        [IN_VMEM] * 2,
        [],
        8,
        later,
    )


def down_grad_body(slices, start, filled, me_ref, hidden_ref, *refs):
    out_ref, block, sems = refs[-3:]
    _, _, width = block.shape
    hidden = hidden_ref[...]
    copies = []
    for index in range(slices.count):
        block[index] = lax.dot_general(
            hidden, slices.read(refs[filled:], index), ROWS, preferred_element_type=jnp.float32
        ).astype(jnp.bfloat16)
        first = pl.multiple_of((me_ref[0] ^ (start + index)) * width, width)
        target = out_ref.at[:, pl.ds(first, width)]
        copies.append(pltpu.make_async_copy(block.at[index], target, sems.at[index]))
        copies[-1].start()
    for copy in copies:
        copy.wait()


def down_grads(me, hidden, slices, start, total, filled=(), later=()):
    width, units = slices.width, hidden.shape[1]
    return run_kernel(
        functools.partial(down_grad_body, slices, start, len(filled)),
        "down_grads",
        (me, hidden, *filled, *slices.flat),
        [IN_SMEM, IN_VMEM] + [ANYWHERE] * len(filled) + [IN_VMEM] * len(slices.flat),
        [like(units, width * total)],
        [ANYWHERE],
        [
            pltpu.VMEM((slices.count, units, width), jnp.bfloat16),
            pltpu.SemaphoreType.DMA((slices.count,)),
        ],
        16,
        later,
        True,
        {2: 0} if filled else None,
    )


def weight_grad_body(slices, parts, me_ref, *refs):
    grad_refs, (gate_hbm, up_hbm, block, sems) = refs[:2], refs[-4:]
    _, count, width, units = block.shape
    grads = jnp.concatenate([ref[...] for ref in grad_refs], axis=1)
    size = width // parts
    copies = []
    for index in range(count):
        rows = slices.read(refs[2:], index)
        start = pl.multiple_of((me_ref[0] ^ index) * width, width)
        for part in range(parts):
            columns = rows[:, part * size : (part + 1) * size]
            both = lax.dot_general(columns, grads, ROWS, preferred_element_type=jnp.float32)
            both = both.astype(jnp.bfloat16)
            for which, out_ref in enumerate((gate_hbm, up_hbm)):
                source = block.at[which, index, pl.ds(part * size, size), :]
                source[...] = both[:, which * units : (which + 1) * units]
                target = out_ref.at[pl.ds(start + part * size, size), :]
                sem = sems.at[(index * parts + part) * 2 + which]
                copies.append(pltpu.make_async_copy(source, target, sem))
                copies[-1].start()
    for copy in copies:
        copy.wait()


def weight_grads(me, slices, gate_grad, up_grad, later=()):
    count, width, units = slices.count, slices.width, gate_grad.shape[1]
    parts = 2 if width % 256 == 0 else 1
    return run_kernel(
        functools.partial(weight_grad_body, slices, parts),
        "weight_grads",
        (me, gate_grad, up_grad, *slices.flat),
        [IN_SMEM] + [IN_VMEM] * (2 + len(slices.flat)),
        [like(width * count, units)] * 2,
        [ANYWHERE] * 2,
        [
            pltpu.VMEM((2, count, width, units), jnp.bfloat16),
            pltpu.SemaphoreType.DMA((2 * count * parts,)),
        ],
        20,
        later,
        True,
    )


def pick_rows(tokens, cotangent, row_index, live_mask, weight):
    flat_rows = row_index.reshape(-1)
    keep_rows = live_mask.reshape(-1)[:, None]
    taken_tokens = jnp.take(tokens, flat_rows, axis=0)
    picked_tokens = jnp.where(keep_rows, taken_tokens, jnp.zeros_like(taken_tokens))
    taken_grads = jnp.take(cotangent, flat_rows, axis=0).astype(jnp.float32)
    picked_grads = (weight.reshape(-1)[:, None] * taken_grads).astype(jnp.bfloat16)
    shaped = row_index.shape + (tokens.shape[1],)
    return (picked_tokens.reshape(shaped), picked_grads.reshape(shaped))


def to_slots(summed, experts, slot_count):
    return summed.astype(jnp.bfloat16).reshape(experts, slot_count, summed.shape[1])


def send_back(term, experts, slot_count):
    summed = lax.psum_scatter(
        term.astype(jnp.bfloat16), "fsdp", scatter_dimension=1, tiled=True
    ).astype(jnp.float32)
    return lax.all_to_all(
        to_slots(summed, experts, slot_count), "ep", split_axis=0, concat_axis=0, tiled=True
    )


def by_collectives(tokens, cotangent, gate_weight, up_weight, down_weight, chosen, counts, gate_prob):
    experts = chosen.shape[0]
    slot_count = chosen.shape[2]
    features = tokens.shape[1]
    row_index = chosen[:, 0, :]
    position = lax.broadcasted_iota(jnp.int32, (experts, slot_count), 1)
    live_mask = position < counts
    weight = jnp.where(live_mask, gate_prob[:, 0, :], 0.0)
    picked_tokens, picked_grads = pick_rows(tokens, cotangent, row_index, live_mask, weight)
    sliced_tokens, sliced_grads = (
        lax.all_to_all(picked_tokens, "ep", split_axis=0, concat_axis=0, tiled=True),
        lax.all_to_all(picked_grads, "ep", split_axis=0, concat_axis=0, tiled=True),
    )
    rows_tokens, rows_grads = (
        lax.all_gather(sliced_tokens, "fsdp", axis=2, tiled=True),
        lax.all_gather(sliced_grads, "fsdp", axis=2, tiled=True),
    )
    full_width = rows_tokens.shape[2]
    total_rows = rows_tokens.shape[0] * slot_count
    rows_tokens = rows_tokens.reshape(total_rows, full_width)
    rows_grads = rows_grads.reshape(total_rows, full_width)
    gate_local = gate_weight[0]
    up_local = up_weight[0]
    down_local = down_weight[0]
    pre_gate = jnp.dot(rows_tokens, gate_local, preferred_element_type=jnp.float32)
    pre_up = jnp.dot(rows_tokens, up_local, preferred_element_type=jnp.float32)
    sigmoid_gate = jax.nn.sigmoid(pre_gate)
    activated = pre_gate * sigmoid_gate
    hidden = (activated * pre_up).astype(jnp.bfloat16)
    output_term = jnp.dot(hidden, down_local, preferred_element_type=jnp.float32)
    output_back = send_back(output_term, experts, slot_count)
    contract_rows = (((0,), (0,)), ((), ()))
    contract_last = (((1,), (1,)), ((), ()))
    grad_hidden = lax.dot_general(
        rows_grads, down_local, contract_last, preferred_element_type=jnp.float32
    )
    grad_pre_gate = (
        grad_hidden * pre_up * sigmoid_gate * (1.0 + pre_gate * (1.0 - sigmoid_gate))
    ).astype(jnp.bfloat16)
    grad_pre_up = (grad_hidden * activated).astype(jnp.bfloat16)
    grad_down = lax.dot_general(
        hidden, rows_grads, contract_rows, preferred_element_type=jnp.float32
    ).astype(jnp.bfloat16)
    grad_gate = lax.dot_general(
        rows_tokens, grad_pre_gate, contract_rows, preferred_element_type=jnp.float32
    ).astype(jnp.bfloat16)
    grad_up = lax.dot_general(
        rows_tokens, grad_pre_up, contract_rows, preferred_element_type=jnp.float32
    ).astype(jnp.bfloat16)
    grad_term = lax.dot_general(
        grad_pre_gate, gate_local, contract_last, preferred_element_type=jnp.float32
    )
    grad_term = grad_term + lax.dot_general(
        grad_pre_up, up_local, contract_last, preferred_element_type=jnp.float32
    )
    grad_back = send_back(grad_term, experts, slot_count)
    flat_rows = row_index.reshape(-1)
    output_rows = output_back.reshape(-1, features).astype(jnp.float32)
    mixture = (
        jnp.zeros((tokens.shape[0], features), jnp.float32)
        .at[flat_rows]
        .add(weight.reshape(-1)[:, None] * output_rows)
    )
    grad_rows = jnp.where(
        live_mask.reshape(-1)[:, None], grad_back.reshape(-1, features).astype(jnp.float32), 0.0
    )
    grad_tokens = jnp.zeros((tokens.shape[0], features), jnp.float32).at[flat_rows].add(grad_rows)
    return (
        mixture.astype(jnp.bfloat16),
        grad_tokens.astype(jnp.bfloat16),
        grad_gate[None],
        grad_up[None],
        grad_down[None],
    )


def swap(array, distance, axis):
    size = lax.axis_size(axis)
    return lax.ppermute(array, axis, [(i, i ^ distance) for i in range(size)])


def joined(*arrays):
    return jnp.concatenate(arrays, axis=0)


def gathered(whole, first, second):
    from_first = swap(whole, first, "fsdp")
    from_second = swap(whole, second, "fsdp")
    passed = arrange((from_first,), [[(0, 0, whole.shape[0])]], (from_second,))
    slices = [[whole], [None], [None], [swap(passed, second, "fsdp")]]
    slices[first], slices[second] = [from_first], [from_second]
    return slices


def pieces_of(mixed, plain):
    return [
        [(piece, True) for piece in some] + [(piece, False) for piece in others]
        for some, others in zip(mixed, plain)
    ]


def by_links(tokens, cotangent, gate_weight, up_weight, down_weight, chosen, counts, gate_prob):
    experts, _, slots = chosen.shape
    count = lax.axis_size("fsdp")
    ep_index = lax.axis_index("ep").reshape(1)
    me = lax.axis_index("fsdp").reshape(1)
    units = gate_weight.shape[2]
    two = 2 * slots
    plan = [[(part, step) for part in range(2)] for step in range(4)]
    plan += [[(part, step), (part, step + 1)] for part in range(2) for step in (4, 6)]
    own, core, even1, odd1, token2, token3, grad2, grad3, mask, weights = pick_slots(
        ep_index, chosen, counts.reshape(1, experts), gate_prob, tokens, cotangent, plan
    )

    token2 = swap(token2, 4, "ep")
    token3 = swap(token3, 6, "ep")
    even1 = swap(even1, 2, "ep")
    odd1 = swap(odd1, 3, "ep")
    core = swap(core, 1, "ep")
    gate = load_weight(me, gate_weight[0], True, count, (own,))
    near = joined(arrange((own,), [[(0, 0, two)]], (gate,)), core, even1, odd1)
    near_x = swap(near, 1, "fsdp")
    near_y = swap(near, 2, "fsdp")
    odd = swap(joined(token2[slots:], token3[slots:], token2), 1, "ep")
    ends = [(0, 0, slots), (2, 0, slots), (1, 0, slots), (2, slots, slots)]
    up = load_weight(me, up_weight[0], True, count, (near,))
    far = arrange((token2, token3, odd), [ends], (near_x, near_y, up))
    far_tokens = gathered(far, 2, 1)
    grad2 = swap(grad2, 4, "ep")
    grad3 = swap(grad3, 6, "ep")
    down = load_weight(me, down_weight[0], False, count, (up,))
    weighted, plain = spread_matrices(mask, weights, (down,))
    odd = arrange(
        (grad2, grad3),
        [[(0, slots, slots), (1, slots, slots), (0, 0, two), (1, 0, two)]],
    )
    odd = swap(odd, 1, "ep")
    far_grads = gathered(arrange((grad2, grad3, odd), [ends]), 1, 2)
    halves = [[(0, first, slots) for first in range(part * slots, 4 * two, two)] for part in range(2)]
    near_d = swap(arrange((near_x,), halves[:1]), 2, "fsdp")
    near_grad_d = swap(arrange((near_y,), halves[1:]), 1, "fsdp")
    mixed = [[near], [near_x], [near_y], []]
    picked = pieces_of(mixed, far_tokens)
    grads = pieces_of(mixed, far_grads)
    picked[3].insert(0, (near_d, False))
    grads[3].insert(0, (near_grad_d, False))
    first = Slices(picked[:3], 0, slots)
    last = Slices(picked[3:], 0, slots)

    sums = partial_products(first, (gate, up), (PLAIN, PLAIN), units)
    (hidden, slope, silu), terms = forward_terms(last, sums, gate, up, down)
    bottom = swap(terms[3][1], 1, "fsdp")
    top = swap(terms[3][0], 2, "fsdp")

    first = Slices(grads[:3], 1, slots)
    last = Slices(grads[3:], 1, slots)
    (grad_sum,) = [partial_products(first, (down,), (LAST,), units, (hidden,))]
    grad_down, mark = down_grads(me, hidden, first, 0, count, (), (grad_sum,))
    sum_x, sum_y = merge(terms[1], terms[2], top, bottom, (mark,))
    (gate_grad, up_grad), back_d = backward_terms(
        last, grad_sum, slope, silu, gate, up, down, (sum_x,)
    )
    sum_x = swap(sum_x, 1, "fsdp")
    sum_y = swap(sum_y, 2, "fsdp")
    bottom = swap(back_d[1], 1, "fsdp")
    top = swap(back_d[0], 2, "fsdp")
    back = backward_rest(gate_grad, up_grad, gate, up)
    out0, out1, out2, out3 = add_up([joined(*terms[0]), sum_x, sum_y], 4, (back[0][0],))
    out3 = swap(out3, 6, "ep")
    out2 = swap(out2, 4, "ep")
    out1 = swap(out1, 2, "ep")

    y_far = add_up([back[2][1], bottom], 1, (out0,))
    x_near, y_near = near_pair(back[1][0], top, back[2][0], (y_far,))
    x_far = swap(back[1][1], 1, "fsdp")
    y_far = swap(y_far, 2, "fsdp")
    x_near = swap(x_near, 1, "fsdp")
    y_near = swap(y_near, 2, "fsdp")
    layout = []
    for step in range(experts // 2):
        layout += [(step, 0), (experts // 2, step)]
    outs = [out0, out1, out2, out3]
    outs.append(swap(joined(*[piece[slots:] for piece in outs]), 1, "ep"))
    back2, back3 = add_up([back[0][1], x_far, y_far], 2)
    last = Slices(grads[3:], 1, slots)
    grad_down, mark = down_grads(me, hidden, last, count - 1, count, (grad_down,), (back2,))
    back0, back1 = add_up([back[0][0], x_near, y_near], 2, (mark, outs[-1]))
    back3 = swap(back3, 6, "ep")
    back2 = swap(back2, 4, "ep")
    back1 = swap(back1, 2, "ep")
    grad_gate, grad_up, mark = weight_grads(
        me, Slices(picked, 0, slots), gate_grad, up_grad, (back0,)
    )
    mixture = spread_rows(weighted, outs, layout, slots)
    backs = [back0, back1, back2, back3]
    far_odd = [[(0, slots, slots), (1, slots, slots), (0, 0, two)]]
    backs.append(swap(arrange((back2, back3), far_odd, (mark,)), 1, "ep"))
    backs.append(swap(arrange((back0, back1), [far_odd[0][:2]], (mark,)), 1, "ep"))
    layout = [(0, 0), (5, 0), (1, 0), (5, 1), (2, 0), (4, 0), (3, 0), (4, 1)]
    grad_tokens = spread_rows(plain, backs, layout, slots)
    return mixture, grad_tokens, grad_gate[None], grad_up[None], grad_down[None]


def solution(mesh):
    placed = (
        P("ep", "fsdp"),
        P("ep", "fsdp"),
        P("ep", None, "fsdp"),
        P("ep", None, "fsdp"),
        P("ep", "fsdp", None),
        P(None, "ep", None),
        P(None, "ep"),
        P(None, "ep", None),
    )

    def per_part(*arrays):
        fits = mesh.shape["fsdp"] == 4 and mesh.shape["ep"] == 8 and arrays[0].shape[1] % 128 == 0
        return (by_links if fits else by_collectives)(*arrays)

    return jax.shard_map(
        per_part,
        mesh=mesh,
        in_specs=placed,
        out_specs=(
            P("ep", "fsdp"),
            P("ep", "fsdp"),
            P("ep", None, "fsdp"),
            P("ep", None, "fsdp"),
            P("ep", "fsdp", None),
        ),
        check_vma=False,
    )
```

```python
import functools

import jax
import jax.numpy as jnp
from jax import lax
from jax.experimental import pallas as pl
from jax.experimental.pallas import tpu as pltpu
from jax.sharding import PartitionSpec as P

ROWS = (((0,), (0,)), ((), ()))
PLAIN = (((1,), (0,)), ((), ()))
LAST = (((1,), (1,)), ((), ()))
IN_VMEM = pl.BlockSpec(memory_space=pltpu.VMEM)
IN_SMEM = pl.BlockSpec(memory_space=pltpu.SMEM)
ANYWHERE = pl.BlockSpec(memory_space=pl.ANY)
MIB = 1024 * 1024


def run_kernel(body, name, operands, specs, outs, out_specs, scratch, mib, later=(), mark=False, aliases=None):
    used = len(operands)
    outs, out_specs = list(outs), list(out_specs)
    results = len(outs)
    if mark:
        outs.append(jax.ShapeDtypeStruct((8, 128), jnp.float32))
        out_specs.append(IN_VMEM)

    def run(*refs):
        refs = list(refs[len(later) :])
        if mark:
            mark_ref = refs.pop(used + results)
            mark_ref[...] = jnp.zeros_like(mark_ref)
        body(*refs)

    out = pl.pallas_call(
        run,
        name=name,
        in_specs=[*[ANYWHERE] * len(later), *specs],
        out_shape=outs,
        out_specs=out_specs,
        scratch_shapes=scratch,
        input_output_aliases={len(later) + i: o for i, o in (aliases or {}).items()},
        compiler_params=pltpu.CompilerParams(vmem_limit_bytes=mib * MIB),
        cost_estimate=pl.CostEstimate(flops=1024, bytes_accessed=1024, transcendentals=0),
    )(*later, *operands)
    return out if len(out) > 1 else out[0]


def in_hbm(array):
    return pltpu.with_memory_space_constraint(array, pltpu.HBM)


def like(rows, width, kind=jnp.bfloat16):
    return jax.ShapeDtypeStruct((rows, width), kind)


def slot_columns(me, chosen_ref, counts_ref, prob_ref):
    experts, _, slots = chosen_ref.shape
    diagonal = lax.broadcasted_iota(jnp.int32, (slots, slots), 0) == lax.broadcasted_iota(
        jnp.int32, (slots, slots), 1
    )
    position = lax.broadcasted_iota(jnp.int32, (slots, 1), 0)
    rows, weights = [], []
    for step in range(experts):
        expert = me ^ step
        live = position < counts_ref[0, expert]
        row = jnp.broadcast_to(chosen_ref[expert].astype(jnp.float32), (slots, slots))
        row = jnp.sum(jnp.where(diagonal, row, 0.0), axis=1, keepdims=True)
        prob = jnp.broadcast_to(prob_ref[expert], (slots, slots))
        prob = jnp.sum(jnp.where(diagonal, prob, 0.0), axis=1, keepdims=True)
        rows.append(jnp.where(live, row, -1.0))
        weights.append(jnp.where(live, prob, 0.0))
    return jnp.concatenate(rows, axis=0), jnp.concatenate(weights, axis=0)


def pick_body(plan, me_ref, counts_hbm, chosen_hbm, prob_hbm, tokens_hbm, cotangent_hbm, *refs):
    *outs, mask_ref, weights_ref = refs[:-6]
    counts_ref, chosen_ref, prob_ref, tokens_ref, cotangent_ref, sems = refs[-6:]
    experts, _, slots = chosen_ref.shape
    length = tokens_ref.shape[0]
    halves = [pl.ds(first, length // 2) for first in (0, length // 2)]
    pairs = [(counts_hbm, counts_ref), (chosen_hbm, chosen_ref), (prob_hbm, prob_ref)]
    for source, target in ((tokens_hbm, tokens_ref), (cotangent_hbm, cotangent_ref)):
        pairs += [(source.at[half], target.at[half]) for half in halves]
    copies = [pltpu.make_async_copy(*pair, sems.at[index]) for index, pair in enumerate(pairs)]
    for copy in copies:
        copy.start()
    for copy in copies[:3]:
        copy.wait()
    rows, weights = slot_columns(me_ref[0], chosen_ref, counts_ref, prob_ref)
    place = lax.broadcasted_iota(jnp.int32, (rows.shape[0], length), 1).astype(jnp.float32)
    mask = (place == rows).astype(jnp.bfloat16)
    mask_ref[...] = mask
    weights_ref[...] = jnp.broadcast_to(weights, weights_ref.shape)
    for which, source_ref in enumerate((tokens_ref, cotangent_ref)):
        value = 0.0
        for part, half in enumerate(halves):
            copies[3 + 2 * which + part].wait()
            columns = mask[:, part * (length // 2) : (part + 1) * (length // 2)]
            value += jnp.dot(columns, source_ref[half, :], preferred_element_type=jnp.float32)
        if which:
            value = weights * value
        value = value.astype(jnp.bfloat16)
        for out_ref, blocks in zip(outs, plan):
            for place, (part, step) in enumerate(blocks):
                if part == which:
                    target = pl.ds(place * slots, slots)
                    out_ref[target, :] = value[step * slots : (step + 1) * slots]


def pick_slots(me, chosen, counts, gate_prob, tokens, cotangent, plan):
    experts, _, slots = chosen.shape
    length, width = tokens.shape
    total = experts * slots
    operands = (counts, chosen, gate_prob, tokens, cotangent)
    return run_kernel(
        functools.partial(pick_body, plan),
        "pick_slots",
        (me, *[in_hbm(array) for array in operands]),
        [IN_SMEM] + [ANYWHERE] * 5,
        [like(slots * len(blocks), width) for blocks in plan]
        + [like(total, length), like(total, 128, jnp.float32)],
        [IN_VMEM] * (len(plan) + 2),
        [pltpu.SMEM(counts.shape, counts.dtype)]
        + [pltpu.VMEM(array.shape, array.dtype) for array in operands[1:]]
        + [pltpu.SemaphoreType.DMA((7,))],
        16,
    )


def spread_matrix_body(mask_ref, weights_ref, weighted_ref, plain_ref):
    mask = mask_ref[...].astype(jnp.float32)
    weights = weights_ref[...][:, :1]
    high = weights.astype(jnp.bfloat16).astype(jnp.float32)
    count = mask.shape[0]
    plain_ref[...] = mask.T.astype(jnp.bfloat16)
    weighted_ref[:, :count] = (mask * high).T.astype(jnp.bfloat16)
    weighted_ref[:, count:] = (mask * (weights - high)).T.astype(jnp.bfloat16)


def spread_matrices(mask, weights, later=()):
    count, length = mask.shape
    return run_kernel(
        spread_matrix_body,
        "spread_matrices",
        (mask, weights),
        [IN_VMEM] * 2,
        [like(length, 2 * count), like(length, count)],
        [IN_VMEM] * 2,
        [],
        8,
        later,
    )


def spread_body(layout, slots, spread_ref, *refs):
    pieces, (out_hbm, block, sems) = refs[:-3], refs[-3:]
    values = jnp.concatenate([pieces[p][pl.ds(q * slots, slots), :] for p, q in layout], axis=0)
    if spread_ref.shape[1] > values.shape[0]:
        values = jnp.concatenate([values, values], axis=0)
    parts = sems.shape[0]
    size = block.shape[1] // parts
    copies = []
    for part in range(parts):
        columns = pl.ds(part * size, size)
        total = jnp.dot(
            spread_ref[...],
            values[:, part * size : (part + 1) * size],
            preferred_element_type=jnp.float32,
        )
        block[:, columns] = total.astype(jnp.bfloat16)
        target = out_hbm.at[:, columns]
        copies.append(pltpu.make_async_copy(block.at[:, columns], target, sems.at[part]))
        copies[-1].start(priority=len(copies) % 2)
    for copy in copies:
        copy.wait()


def spread_rows(spread, pieces, layout, slots, later=(), mark=False):
    length, width = spread.shape[0], pieces[0].shape[1]
    parts = width // 256 if width % 256 == 0 else 1
    return run_kernel(
        functools.partial(spread_body, layout, slots),
        "spread_rows",
        (spread, *pieces),
        [IN_VMEM] * (1 + len(pieces)),
        [like(length, width)],
        [ANYWHERE],
        [pltpu.VMEM((length, width), jnp.bfloat16), pltpu.SemaphoreType.DMA((parts,))],
        16,
        later,
        mark,
    )


def load_body(by_rows, count, me_ref, source_ref, target_ref, sems):
    width = target_ref.shape[1 if by_rows else 2]
    copies = []
    for index in range(count):
        part = pl.ds(pl.multiple_of((me_ref[0] ^ index) * width, width), width)
        source = source_ref.at[part, :] if by_rows else source_ref.at[:, part]
        copies.append(pltpu.make_async_copy(source, target_ref.at[index], sems.at[index]))
        copies[-1].start(priority=len(copies) % 2)
    for copy in copies:
        copy.wait()


def load_weight(me, weight, by_rows, count, later=()):
    first, second = weight.shape
    shape = (count, first // count, second) if by_rows else (count, first, second // count)
    return run_kernel(
        functools.partial(load_body, by_rows, count),
        "load_weight",
        (me, in_hbm(weight)),
        [IN_SMEM, ANYWHERE],
        [jax.ShapeDtypeStruct(shape, weight.dtype)],
        [IN_VMEM],
        [pltpu.SemaphoreType.DMA((count,))],
        4,
        later,
    )


def arrange_body(plan, used, *refs):
    for rows, out_ref in zip(plan, refs[used:]):
        start = 0
        for source, first, size in rows:
            out_ref[pl.ds(start, size), :] = refs[source][pl.ds(first, size), :]
            start += size


def arrange(sources, plan, later=()):
    width = sources[0].shape[1]
    sizes = [sum(size for _, _, size in rows) for rows in plan]
    return run_kernel(
        functools.partial(arrange_body, plan, len(sources)),
        "arrange",
        tuple(sources),
        [IN_VMEM] * len(sources),
        [like(size, width) for size in sizes],
        [IN_VMEM] * len(plan),
        [],
        8,
        later,
    )


def add_body(used, *refs):
    total = refs[0][...].astype(jnp.float32)
    for ref in refs[1:used]:
        total += ref[...].astype(jnp.float32)
    start = 0
    for out_ref in refs[used:]:
        out_ref[...] = total[start : start + out_ref.shape[0]].astype(out_ref.dtype)
        start += out_ref.shape[0]


def add_up(terms, parts=1, later=()):
    rows, width = terms[0].shape
    return run_kernel(
        functools.partial(add_body, len(terms)),
        "add_up",
        tuple(terms),
        [IN_VMEM] * len(terms),
        [like(rows // parts, width)] * parts,
        [IN_VMEM] * parts,
        [],
        8,
        later,
    )


def near_body(first_ref, top_ref, second_ref, first_out, second_out):
    total = first_ref[...].astype(jnp.float32) + top_ref[...].astype(jnp.float32)
    first_out[...] = total.astype(first_out.dtype)
    second_out[...] = second_ref[...]


def near_pair(first, top, second, later=()):
    return run_kernel(
        near_body,
        "near_pair",
        (first, top, second),
        [IN_VMEM] * 3,
        [like(*first.shape)] * 2,
        [IN_VMEM] * 2,
        [],
        8,
        later,
    )


class Slices:
    def __init__(self, slices, part, slots):
        self.mixed = [[mixed for _, mixed in pieces] for pieces in slices]
        self.flat = [array for pieces in slices for array, _ in pieces]
        self.part, self.slots = part, slots
        self.count, self.width = len(slices), self.flat[0].shape[1]
        self.rows = sum(array.shape[0] // (2 if mixed else 1) for array, mixed in slices[0])

    def read(self, refs, index):
        first = sum(len(mixed) for mixed in self.mixed[:index])
        blocks = []
        for place, mixed in enumerate(self.mixed[index]):
            ref = refs[first + place]
            if mixed:
                for start in range(self.part * self.slots, ref.shape[0], 2 * self.slots):
                    blocks.append(ref[pl.ds(start, self.slots), :])
            else:
                blocks.append(ref[...])
        return blocks[0] if len(blocks) == 1 else jnp.concatenate(blocks, axis=0)


def partial_body(slices, dims, *refs):
    used = len(slices.flat)
    weights, sums = refs[used:][: len(dims)], refs[used + len(dims) :]
    for index in range(slices.count):
        rows = slices.read(refs, index)
        for weight_ref, dim, sum_ref in zip(weights, dims, sums):
            value = lax.dot_general(
                rows, weight_ref[index], dim, preferred_element_type=jnp.float32
            )
            if index == 0:
                sum_ref[...] = value
            else:
                sum_ref[...] += value


def partial_products(slices, weights, dims, units, later=()):
    return run_kernel(
        functools.partial(partial_body, slices, dims),
        "partial_products",
        (*slices.flat, *weights),
        [IN_VMEM] * (len(slices.flat) + len(weights)),
        [like(slices.rows, units, jnp.float32)] * len(weights),
        [IN_VMEM] * len(weights),
        [],
        8,
        later,
    )


def store_term(refs, index, term):
    term = term.astype(jnp.bfloat16)
    size = term.shape[0] // 2
    refs[2 * index][...] = term[:size]
    refs[2 * index + 1][...] = term[size:]


def forward_body(slices, *refs):
    used = len(slices.flat)
    gate_sum, up_sum, gate_ref, up_ref, down_ref = refs[used : used + 5]
    hidden_ref, slope_ref, silu_ref, *terms = refs[used + 5 :]
    last = gate_ref.shape[0] - 1
    rows = slices.read(refs, 0)
    gate = gate_sum[...] + jnp.dot(rows, gate_ref[last], preferred_element_type=jnp.float32)
    up = up_sum[...] + jnp.dot(rows, up_ref[last], preferred_element_type=jnp.float32)
    sigmoid = jax.nn.sigmoid(gate)
    silu = gate * sigmoid
    hidden = (silu * up).astype(jnp.bfloat16)
    hidden_ref[...] = hidden
    slope_ref[...] = up * sigmoid * (1.0 + gate * (1.0 - sigmoid))
    silu_ref[...] = silu
    for index in reversed(range(last + 1)):
        term = jnp.dot(hidden, down_ref[index], preferred_element_type=jnp.float32)
        store_term(terms, index, term)


def forward_terms(slices, sums, gate, up, down, later=()):
    count, width, units = gate.shape
    rows = sums[0].shape[0]
    f32 = jnp.float32
    out = run_kernel(
        functools.partial(forward_body, slices),
        "forward_terms",
        (*slices.flat, *sums, gate, up, down),
        [IN_VMEM] * (len(slices.flat) + 5),
        [like(rows, units), like(rows, units, f32), like(rows, units, f32)]
        + [like(rows // 2, width)] * (2 * count),
        [IN_VMEM] * (3 + 2 * count),
        [],
        8,
        later,
    )
    return out[:3], [out[3 + 2 * i : 5 + 2 * i] for i in range(count)]


def backward_body(slices, *refs):
    used = len(slices.flat)
    grad_sum, slope_ref, silu_ref, gate_ref, up_ref, down_ref = refs[used : used + 6]
    gate_grad_ref, up_grad_ref, *terms = refs[used + 6 :]
    last = gate_ref.shape[0] - 1
    rows = slices.read(refs, 0)
    grad = lax.dot_general(rows, down_ref[last], LAST, preferred_element_type=jnp.float32)
    grad += grad_sum[...]
    gate_grad = (grad * slope_ref[...]).astype(jnp.bfloat16)
    up_grad = (grad * silu_ref[...]).astype(jnp.bfloat16)
    gate_grad_ref[...] = gate_grad
    up_grad_ref[...] = up_grad
    store_term(terms, 0, back_term(gate_grad, up_grad, gate_ref, up_ref, last))


def back_term(gate_grad, up_grad, gate_ref, up_ref, index):
    term = lax.dot_general(gate_grad, gate_ref[index], LAST, preferred_element_type=jnp.float32)
    return term + lax.dot_general(up_grad, up_ref[index], LAST, preferred_element_type=jnp.float32)


def backward_rest_body(gate_grad_ref, up_grad_ref, gate_ref, up_ref, *terms):
    for index in reversed(range(len(terms) // 2)):
        term = back_term(gate_grad_ref[...], up_grad_ref[...], gate_ref, up_ref, index)
        store_term(terms, index, term)


def backward_rest(gate_grad, up_grad, gate, up, later=()):
    count, width, _ = gate.shape
    rows = gate_grad.shape[0]
    out = run_kernel(
        backward_rest_body,
        "backward_rest",
        (gate_grad, up_grad, gate, up),
        [IN_VMEM] * 4,
        [like(rows // 2, width)] * (2 * count - 2),
        [IN_VMEM] * (2 * count - 2),
        [],
        8,
        later,
    )
    return [out[2 * i : 2 * i + 2] for i in range(count - 1)]


def backward_terms(slices, grad_sum, slope, silu, gate, up, down, later=()):
    _, width, units = gate.shape
    rows = slope.shape[0]
    out = run_kernel(
        functools.partial(backward_body, slices),
        "backward_terms",
        (*slices.flat, grad_sum, slope, silu, gate, up, down),
        [IN_VMEM] * (len(slices.flat) + 6),
        [like(rows, units)] * 2 + [like(rows // 2, width)] * 2,
        [IN_VMEM] * 4,
        [],
        8,
        later,
    )
    return out[:2], out[2:]


def merge_body(first_top, first_bottom, second_top, second_bottom, top, bottom, first, second):
    size = top.shape[0]
    upper, lower = pl.ds(0, size), pl.ds(size, size)
    total = first_top[...].astype(jnp.float32) + top[...].astype(jnp.float32)
    first[upper, :] = total.astype(first.dtype)
    first[lower, :] = first_bottom[...]
    total = second_bottom[...].astype(jnp.float32) + bottom[...].astype(jnp.float32)
    second[lower, :] = total.astype(second.dtype)
    second[upper, :] = second_top[...]


def merge(first, second, top, bottom, later=()):
    rows, width = first[0].shape
    return run_kernel(
        merge_body,
        "merge",
        (*first, *second, top, bottom),
        [IN_VMEM] * 6,
        [like(2 * rows, width)] * 2,
        [IN_VMEM] * 2,
        [],
        8,
        later,
    )


def down_grad_body(slices, start, filled, me_ref, hidden_ref, *refs):
    out_ref, block, sems = refs[-3:]
    _, _, width = block.shape
    hidden = hidden_ref[...]
    copies = []
    for index in range(slices.count):
        block[index] = lax.dot_general(
            hidden, slices.read(refs[filled:], index), ROWS, preferred_element_type=jnp.float32
        ).astype(jnp.bfloat16)
        first = pl.multiple_of((me_ref[0] ^ (start + index)) * width, width)
        target = out_ref.at[:, pl.ds(first, width)]
        copies.append(pltpu.make_async_copy(block.at[index], target, sems.at[index]))
        copies[-1].start(priority=len(copies) % 2)
    for copy in copies:
        copy.wait()


def down_grads(me, hidden, slices, start, total, filled=(), later=()):
    width, units = slices.width, hidden.shape[1]
    return run_kernel(
        functools.partial(down_grad_body, slices, start, len(filled)),
        "down_grads",
        (me, hidden, *filled, *slices.flat),
        [IN_SMEM, IN_VMEM] + [ANYWHERE] * len(filled) + [IN_VMEM] * len(slices.flat),
        [like(units, width * total)],
        [ANYWHERE],
        [
            pltpu.VMEM((slices.count, units, width), jnp.bfloat16),
            pltpu.SemaphoreType.DMA((slices.count,)),
        ],
        16,
        later,
        True,
        {2: 0} if filled else None,
    )


def weight_grad_body(slices, parts, me_ref, *refs):
    grad_refs, (gate_hbm, up_hbm, block, sems) = refs[:2], refs[-4:]
    _, count, width, units = block.shape
    grads = jnp.concatenate([ref[...] for ref in grad_refs], axis=1)
    size = width // parts
    copies = []
    for index in range(count):
        rows = slices.read(refs[2:], index)
        start = pl.multiple_of((me_ref[0] ^ index) * width, width)
        for part in range(parts):
            columns = rows[:, part * size : (part + 1) * size]
            both = lax.dot_general(columns, grads, ROWS, preferred_element_type=jnp.float32)
            both = both.astype(jnp.bfloat16)
            for which, out_ref in enumerate((gate_hbm, up_hbm)):
                source = block.at[which, index, pl.ds(part * size, size), :]
                source[...] = both[:, which * units : (which + 1) * units]
                target = out_ref.at[pl.ds(start + part * size, size), :]
                sem = sems.at[(index * parts + part) * 2 + which]
                copies.append(pltpu.make_async_copy(source, target, sem))
                copies[-1].start(priority=len(copies) % 2)
    for copy in copies:
        copy.wait()


def weight_grads(me, slices, gate_grad, up_grad, later=()):
    count, width, units = slices.count, slices.width, gate_grad.shape[1]
    parts = 2 if width % 256 == 0 else 1
    return run_kernel(
        functools.partial(weight_grad_body, slices, parts),
        "weight_grads",
        (me, gate_grad, up_grad, *slices.flat),
        [IN_SMEM] + [IN_VMEM] * (2 + len(slices.flat)),
        [like(width * count, units)] * 2,
        [ANYWHERE] * 2,
        [
            pltpu.VMEM((2, count, width, units), jnp.bfloat16),
            pltpu.SemaphoreType.DMA((2 * count * parts,)),
        ],
        20,
        later,
        True,
    )


def pick_rows(tokens, cotangent, row_index, live_mask, weight):
    flat_rows = row_index.reshape(-1)
    keep_rows = live_mask.reshape(-1)[:, None]
    taken_tokens = jnp.take(tokens, flat_rows, axis=0)
    picked_tokens = jnp.where(keep_rows, taken_tokens, jnp.zeros_like(taken_tokens))
    taken_grads = jnp.take(cotangent, flat_rows, axis=0).astype(jnp.float32)
    picked_grads = (weight.reshape(-1)[:, None] * taken_grads).astype(jnp.bfloat16)
    shaped = row_index.shape + (tokens.shape[1],)
    return (picked_tokens.reshape(shaped), picked_grads.reshape(shaped))


def to_slots(summed, experts, slot_count):
    return summed.astype(jnp.bfloat16).reshape(experts, slot_count, summed.shape[1])


def send_back(term, experts, slot_count):
    summed = lax.psum_scatter(
        term.astype(jnp.bfloat16), "fsdp", scatter_dimension=1, tiled=True
    ).astype(jnp.float32)
    return lax.all_to_all(
        to_slots(summed, experts, slot_count), "ep", split_axis=0, concat_axis=0, tiled=True
    )


def by_collectives(tokens, cotangent, gate_weight, up_weight, down_weight, chosen, counts, gate_prob):
    experts = chosen.shape[0]
    slot_count = chosen.shape[2]
    features = tokens.shape[1]
    row_index = chosen[:, 0, :]
    position = lax.broadcasted_iota(jnp.int32, (experts, slot_count), 1)
    live_mask = position < counts
    weight = jnp.where(live_mask, gate_prob[:, 0, :], 0.0)
    picked_tokens, picked_grads = pick_rows(tokens, cotangent, row_index, live_mask, weight)
    sliced_tokens, sliced_grads = (
        lax.all_to_all(picked_tokens, "ep", split_axis=0, concat_axis=0, tiled=True),
        lax.all_to_all(picked_grads, "ep", split_axis=0, concat_axis=0, tiled=True),
    )
    rows_tokens, rows_grads = (
        lax.all_gather(sliced_tokens, "fsdp", axis=2, tiled=True),
        lax.all_gather(sliced_grads, "fsdp", axis=2, tiled=True),
    )
    full_width = rows_tokens.shape[2]
    total_rows = rows_tokens.shape[0] * slot_count
    rows_tokens = rows_tokens.reshape(total_rows, full_width)
    rows_grads = rows_grads.reshape(total_rows, full_width)
    gate_local = gate_weight[0]
    up_local = up_weight[0]
    down_local = down_weight[0]
    pre_gate = jnp.dot(rows_tokens, gate_local, preferred_element_type=jnp.float32)
    pre_up = jnp.dot(rows_tokens, up_local, preferred_element_type=jnp.float32)
    sigmoid_gate = jax.nn.sigmoid(pre_gate)
    activated = pre_gate * sigmoid_gate
    hidden = (activated * pre_up).astype(jnp.bfloat16)
    output_term = jnp.dot(hidden, down_local, preferred_element_type=jnp.float32)
    output_back = send_back(output_term, experts, slot_count)
    contract_rows = (((0,), (0,)), ((), ()))
    contract_last = (((1,), (1,)), ((), ()))
    grad_hidden = lax.dot_general(
        rows_grads, down_local, contract_last, preferred_element_type=jnp.float32
    )
    grad_pre_gate = (
        grad_hidden * pre_up * sigmoid_gate * (1.0 + pre_gate * (1.0 - sigmoid_gate))
    ).astype(jnp.bfloat16)
    grad_pre_up = (grad_hidden * activated).astype(jnp.bfloat16)
    grad_down = lax.dot_general(
        hidden, rows_grads, contract_rows, preferred_element_type=jnp.float32
    ).astype(jnp.bfloat16)
    grad_gate = lax.dot_general(
        rows_tokens, grad_pre_gate, contract_rows, preferred_element_type=jnp.float32
    ).astype(jnp.bfloat16)
    grad_up = lax.dot_general(
        rows_tokens, grad_pre_up, contract_rows, preferred_element_type=jnp.float32
    ).astype(jnp.bfloat16)
    grad_term = lax.dot_general(
        grad_pre_gate, gate_local, contract_last, preferred_element_type=jnp.float32
    )
    grad_term = grad_term + lax.dot_general(
        grad_pre_up, up_local, contract_last, preferred_element_type=jnp.float32
    )
    grad_back = send_back(grad_term, experts, slot_count)
    flat_rows = row_index.reshape(-1)
    output_rows = output_back.reshape(-1, features).astype(jnp.float32)
    mixture = (
        jnp.zeros((tokens.shape[0], features), jnp.float32)
        .at[flat_rows]
        .add(weight.reshape(-1)[:, None] * output_rows)
    )
    grad_rows = jnp.where(
        live_mask.reshape(-1)[:, None], grad_back.reshape(-1, features).astype(jnp.float32), 0.0
    )
    grad_tokens = jnp.zeros((tokens.shape[0], features), jnp.float32).at[flat_rows].add(grad_rows)
    return (
        mixture.astype(jnp.bfloat16),
        grad_tokens.astype(jnp.bfloat16),
        grad_gate[None],
        grad_up[None],
        grad_down[None],
    )


def swap(array, distance, axis):
    size = lax.axis_size(axis)
    return lax.ppermute(array, axis, [(i, i ^ distance) for i in range(size)])


def joined(*arrays):
    return jnp.concatenate(arrays, axis=0)


def gathered(whole, first, second):
    from_first = swap(whole, first, "fsdp")
    from_second = swap(whole, second, "fsdp")
    passed = arrange((from_first,), [[(0, 0, whole.shape[0])]], (from_second,))
    slices = [[whole], [None], [None], [swap(passed, second, "fsdp")]]
    slices[first], slices[second] = [from_first], [from_second]
    return slices


def pieces_of(mixed, plain):
    return [
        [(piece, True) for piece in some] + [(piece, False) for piece in others]
        for some, others in zip(mixed, plain)
    ]


def by_links(tokens, cotangent, gate_weight, up_weight, down_weight, chosen, counts, gate_prob):
    experts, _, slots = chosen.shape
    count = lax.axis_size("fsdp")
    ep_index = lax.axis_index("ep").reshape(1)
    me = lax.axis_index("fsdp").reshape(1)
    units = gate_weight.shape[2]
    two = 2 * slots
    plan = [[(part, step) for part in range(2)] for step in range(4)]
    plan += [[(part, step), (part, step + 1)] for part in range(2) for step in (4, 6)]
    own, core, even1, odd1, token2, token3, grad2, grad3, mask, weights = pick_slots(
        ep_index, chosen, counts.reshape(1, experts), gate_prob, tokens, cotangent, plan
    )

    token2 = swap(token2, 4, "ep")
    token3 = swap(token3, 6, "ep")
    even1 = swap(even1, 2, "ep")
    odd1 = swap(odd1, 3, "ep")
    core = swap(core, 1, "ep")
    gate = load_weight(me, gate_weight[0], True, count, (own,))
    near = joined(arrange((own,), [[(0, 0, two)]], (gate,)), core, even1, odd1)
    near_x = swap(near, 1, "fsdp")
    near_y = swap(near, 2, "fsdp")
    odd = swap(joined(token2[slots:], token3[slots:], token2), 1, "ep")
    ends = [(0, 0, slots), (2, 0, slots), (1, 0, slots), (2, slots, slots)]
    up = load_weight(me, up_weight[0], True, count, (near,))
    far = arrange((token2, token3, odd), [ends], (near_x, near_y, up))
    far_tokens = gathered(far, 2, 1)
    grad2 = swap(grad2, 4, "ep")
    grad3 = swap(grad3, 6, "ep")
    down = load_weight(me, down_weight[0], False, count, (up,))
    weighted, plain = spread_matrices(mask, weights, (down,))
    odd = arrange(
        (grad2, grad3),
        [[(0, slots, slots), (1, slots, slots), (0, 0, two), (1, 0, two)]],
    )
    odd = swap(odd, 1, "ep")
    far_grads = gathered(arrange((grad2, grad3, odd), [ends]), 1, 2)
    halves = [[(0, first, slots) for first in range(part * slots, 4 * two, two)] for part in range(2)]
    near_d = swap(arrange((near_x,), halves[:1]), 2, "fsdp")
    near_grad_d = swap(arrange((near_y,), halves[1:]), 1, "fsdp")
    mixed = [[near], [near_x], [near_y], []]
    picked = pieces_of(mixed, far_tokens)
    grads = pieces_of(mixed, far_grads)
    picked[3].insert(0, (near_d, False))
    grads[3].insert(0, (near_grad_d, False))
    first = Slices(picked[:3], 0, slots)
    last = Slices(picked[3:], 0, slots)

    sums = partial_products(first, (gate, up), (PLAIN, PLAIN), units)
    (hidden, slope, silu), terms = forward_terms(last, sums, gate, up, down)
    bottom = swap(terms[3][1], 1, "fsdp")
    top = swap(terms[3][0], 2, "fsdp")

    first = Slices(grads[:3], 1, slots)
    last = Slices(grads[3:], 1, slots)
    (grad_sum,) = [partial_products(first, (down,), (LAST,), units, (hidden,))]
    grad_down, mark = down_grads(me, hidden, first, 0, count, (), (grad_sum,))
    sum_x, sum_y = merge(terms[1], terms[2], top, bottom, (mark,))
    (gate_grad, up_grad), back_d = backward_terms(
        last, grad_sum, slope, silu, gate, up, down, (sum_x,)
    )
    sum_x = swap(sum_x, 1, "fsdp")
    sum_y = swap(sum_y, 2, "fsdp")
    bottom = swap(back_d[1], 1, "fsdp")
    top = swap(back_d[0], 2, "fsdp")
    back = backward_rest(gate_grad, up_grad, gate, up)
    out0, out1, out2, out3 = add_up([joined(*terms[0]), sum_x, sum_y], 4, (back[0][0],))
    out3 = swap(out3, 6, "ep")
    out2 = swap(out2, 4, "ep")
    out1 = swap(out1, 2, "ep")

    y_far = add_up([back[2][1], bottom], 1, (out0,))
    x_near, y_near = near_pair(back[1][0], top, back[2][0], (y_far,))
    x_far = swap(back[1][1], 1, "fsdp")
    y_far = swap(y_far, 2, "fsdp")
    x_near = swap(x_near, 1, "fsdp")
    y_near = swap(y_near, 2, "fsdp")
    layout = []
    for step in range(experts // 2):
        layout += [(step, 0), (experts // 2, step)]
    outs = [out0, out1, out2, out3]
    outs.append(swap(joined(*[piece[slots:] for piece in outs]), 1, "ep"))
    back2, back3 = add_up([back[0][1], x_far, y_far], 2)
    last = Slices(grads[3:], 1, slots)
    grad_down, mark = down_grads(me, hidden, last, count - 1, count, (grad_down,), (back2,))
    back0, back1 = add_up([back[0][0], x_near, y_near], 2, (mark, outs[-1]))
    back3 = swap(back3, 6, "ep")
    back2 = swap(back2, 4, "ep")
    back1 = swap(back1, 2, "ep")
    grad_gate, grad_up, mark = weight_grads(
        me, Slices(picked, 0, slots), gate_grad, up_grad, (back0,)
    )
    mixture = spread_rows(weighted, outs, layout, slots)
    backs = [back0, back1, back2, back3]
    far_odd = [[(0, slots, slots), (1, slots, slots), (0, 0, two)]]
    backs.append(swap(arrange((back2, back3), far_odd, (mark,)), 1, "ep"))
    backs.append(swap(arrange((back0, back1), [far_odd[0][:2]], (mark,)), 1, "ep"))
    layout = [(0, 0), (5, 0), (1, 0), (5, 1), (2, 0), (4, 0), (3, 0), (4, 1)]
    grad_tokens = spread_rows(plain, backs, layout, slots)
    return mixture, grad_tokens, grad_gate[None], grad_up[None], grad_down[None]


def solution(mesh):
    placed = (
        P("ep", "fsdp"),
        P("ep", "fsdp"),
        P("ep", None, "fsdp"),
        P("ep", None, "fsdp"),
        P("ep", "fsdp", None),
        P(None, "ep", None),
        P(None, "ep"),
        P(None, "ep", None),
    )

    def per_part(*arrays):
        fits = mesh.shape["fsdp"] == 4 and mesh.shape["ep"] == 8 and arrays[0].shape[1] % 128 == 0
        return (by_links if fits else by_collectives)(*arrays)

    return jax.shard_map(
        per_part,
        mesh=mesh,
        in_specs=placed,
        out_specs=(
            P("ep", "fsdp"),
            P("ep", "fsdp"),
            P("ep", None, "fsdp"),
            P("ep", None, "fsdp"),
            P("ep", "fsdp", None),
        ),
        check_vma=False,
    )
```
